128 devices in a mesh: ctx: 8 (over y, core), exp: 16 (over z, x).
Axes of the slice: x: 4, y: 4, z: 4, core: 2. Of those that a mesh axis runs over, the one named last changes fastest.
Arguments:
- tokens: bfloat16 [16, 2048, 1024], P('exp', 'ctx'), may hold values from -6 to 6
- norm_attn: bfloat16 [1024], P(('ctx', 'exp')), may hold values from 0.5 to 1.5
- w_query: bfloat16 [1024, 1024], P(('ctx', 'exp')), may hold values from -0.1875 to 0.1875
- w_key: bfloat16 [1024, 512], P(('ctx', 'exp')), may hold values from -0.1875 to 0.1875
- w_value: bfloat16 [1024, 512], P(('ctx', 'exp')), may hold values from -0.1875 to 0.1875
- w_out: bfloat16 [1024, 1024], P(('ctx', 'exp')), may hold values from -4 to 4
- norm_moe: bfloat16 [1024], P(('ctx', 'exp')), may hold values from 0.5 to 1.5
- w_router: bfloat16 [1024, 32], P(('ctx', 'exp')), may hold values from -0.09375 to 0.09375
- w_gate: bfloat16 [32, 1024, 512], P('exp', 'ctx'), may hold values from -0.1875 to 0.1875
- w_up: bfloat16 [32, 1024, 512], P('exp', 'ctx'), may hold values from -0.1875 to 0.1875
- w_down: bfloat16 [32, 512, 1024], P('exp', None, 'ctx'), may hold values from -1 to 1
- routes: int32 [16, 2048, 8], P('exp', 'ctx'), may hold values from 0 to 31, all different within a row; in each aligned block of 256 rows (0 to 255, 256 to 511, ..., all dimensions but the last counted through in order) at most 96 rows name the same one
- cotangent: bfloat16 [16, 2048, 1024], P('exp', 'ctx'), may hold values from -6 to 6
Outputs:
- output: bfloat16 [16, 2048, 1024], P('exp', 'ctx')
- grad_tokens: bfloat16 [16, 2048, 1024], P('exp', 'ctx')
- grad_norm_attn: float32 [1024], P(('ctx', 'exp'))
- grad_query: float32 [1024, 1024], P(('ctx', 'exp'))
- grad_key: float32 [1024, 512], P(('ctx', 'exp'))
- grad_value: float32 [1024, 512], P(('ctx', 'exp'))
- grad_out_proj: float32 [1024, 1024], P(('ctx', 'exp'))
- grad_norm_moe: float32 [1024], P(('ctx', 'exp'))
- grad_router: float32 [1024, 32], P(('ctx', 'exp'))
- grad_gate: float32 [32, 1024, 512], P('exp', 'ctx')
- grad_up: float32 [32, 1024, 512], P('exp', 'ctx')
- grad_down: float32 [32, 512, 1024], P('exp', None, 'ctx')
The draws below stay inside these ranges and needn't reach their ends.
Inputs may be any that keep to these rules, and one draw needn't show every extreme that they name: `routes`: each row names 8 different experts. In the rows of one device (each aligned block of 256 rows in order of sequence and position) no expert is named more than 96 times; in some blocks one is named exactly 96 times.
All inputs are finite; a program needn't handle non-finite values.
Results may differ from the reference program's by a relative error of at most 0.038.
Values may be sent and summed in bfloat16 or wider, within the bound.
A program may use at most 192 MiB of HBM per device.

```python
import math
import jax
import jax.numpy as jnp
import numpy as np
from jax import lax

D = 1024
HEADS = 16
HEAD = 64
KV_HEADS = 8
FF = 512
EXPERTS = 32
TOP = 8
TOK_DEV = 256
QW = 1024
KVW = 512
CAP = 96
SEQ = 2048
SEQS = 16


def block_levels(stream_key, extent, shards, smallest, high):
    def one(dim, parts):
        steps = jax.random.uniform(jax.random.fold_in(jax.random.fold_in(stream_key, 6), dim), (parts,), jnp.float32, smallest / len(shards), high / len(shards))
        return jnp.repeat(jnp.exp(steps), extent[dim] // parts).reshape((-1,) + (1,) * (len(extent) - dim - 1))

    level = one(*shards[0])
    for cut in shards[1:]:
        level = level * one(*cut)
    return level


def shared_out(own_key, own, number, rows, amount, top, most, lean):
    order = jax.random.permutation(own_key, amount)
    packed, ordinary = portions_of(amount, rows * top, most, lean, True), portions_of(amount, rows * top, most, lean, False)
    places = jnp.arange(amount)

    def named(lengths, rotation):
        used = int((lengths > 0).sum())
        fixed = max(1, used // 4)
        passed = fixed + (places - fixed + rotation * (used - fixed)) % max(1, amount - fixed)
        return jnp.zeros((amount,), jnp.int32).at[order[jnp.where(places < fixed, places, passed)]].set(jnp.asarray(lengths, jnp.int32))

    lengths = jnp.where(number % 4 == 0, named(packed, number // 4), named(ordinary, number - number // 4 - 1))
    mixed = jax.random.permutation(jax.random.fold_in(own, 3), amount)
    source_of, receiver = mixed[0:amount // 2 * 2:2], mixed[1:amount // 2 * 2:2]
    slack = jnp.minimum(lengths[source_of] - 1, most - lengths[receiver]) // 2
    slack = jnp.where((source_of == order[0]) | (receiver == order[0]) | (lengths[receiver] == 0), 0, jnp.maximum(slack, 0))
    passed = jax.random.randint(jax.random.fold_in(own, 4), (amount // 2,), 0, 1 << 20) % (slack + 1)
    lengths = lengths.at[source_of].add(-passed).at[receiver].add(passed)
    labels = jnp.searchsorted(jnp.cumsum(lengths), jnp.arange(rows * top), side="right").astype(jnp.int32)
    listing = labels.reshape(top, rows).T
    listing = listing[jax.random.permutation(jax.random.fold_in(own, 1), rows)]
    rotation = jax.random.randint(jax.random.fold_in(own, 2), (rows, 1), 0, top)
    return jnp.take_along_axis(listing, (jnp.arange(top)[None, :] + rotation) % top, axis=1)


def portions_of(amount, total, reach, slope, full):
    portions = [(1 << 20) // math.isqrt(rank ** slope) + 1 for rank in range(1, amount + 1)]
    largest = reach if full else min(reach, max(-(-total // amount), total * portions[0] // sum(portions)))
    least = 1 if total - largest >= amount - 1 else 0
    given, surplus = [largest] + [least] * (amount - 1), total - largest - least * (amount - 1)
    while surplus > 0:
        candidates = [i for i in range(1, amount) if given[i] < largest] or [i for i in range(1, amount) if given[i] < reach]
        pool, remaining = sum([portions[i] for i in candidates]), surplus
        for i in candidates:
            addition = min(reach - given[i], max(1, remaining * portions[i] // pool), surplus)
            given[i] = given[i] + addition
            surplus = surplus - addition
    return np.array(given)


def bell_draw(stream_key, dims, width, limit, cuts=(), held_as=jnp.bfloat16):
    values = width * jax.random.normal(stream_key, dims, jnp.float32)
    if cuts:
        values = values * block_levels(stream_key, dims, cuts, -0.22, 0.18)
    return jnp.clip(values, -limit, limit).astype(held_as)


def setup_inputs(seed: int = 0) -> dict:
    arg_keys = jax.random.split(jax.random.key(seed), 14)
    tokens = bell_draw(arg_keys[0], (SEQS, SEQ, D), 1.0, 6.0, ((0, 16), (1, 8)))
    norm_attn = jnp.clip(1.0 + 0.1 * jax.random.normal(arg_keys[1], (D,), jnp.float32), 0.5, 1.5).astype(jnp.bfloat16)
    w_query = bell_draw(arg_keys[2], (D, QW), D ** -0.5, 0.1875, ((0, 128),))
    w_key = bell_draw(arg_keys[3], (D, KVW), D ** -0.5, 0.1875, ((0, 128),))
    w_value = bell_draw(arg_keys[4], (D, KVW), D ** -0.5, 0.1875, ((0, 128),))
    w_out = bell_draw(arg_keys[5], (QW, D), (max(QW // 512, 1)) ** -0.5, 4.0, ((0, 128),))
    norm_moe = jnp.clip(1.0 + 0.1 * jax.random.normal(arg_keys[6], (D,), jnp.float32), 0.5, 1.5).astype(jnp.bfloat16)
    w_router = bell_draw(arg_keys[7], (D, EXPERTS), (4 * D) ** -0.5, 0.09375, ((0, 128),))
    w_gate = bell_draw(arg_keys[8], (EXPERTS, D, FF), D ** -0.5, 0.1875, ((0, 16), (1, 8)))
    w_up = bell_draw(arg_keys[9], (EXPERTS, D, FF), D ** -0.5, 0.1875, ((0, 16), (1, 8)))
    w_down = bell_draw(arg_keys[10], (EXPERTS, FF, D), (FF // 16) ** -0.5, 1.0, ((0, 16), (2, 8)))
    routes_keys = jax.random.split(jax.random.fold_in(arg_keys[11], 1), SEQS * SEQ // TOK_DEV)
    routes_turns = jax.random.permutation(jax.random.fold_in(arg_keys[11], 3), SEQS * SEQ // TOK_DEV)
    routes = jax.vmap(lambda own, number: shared_out(jax.random.fold_in(arg_keys[11], 2), own, number, TOK_DEV, EXPERTS, TOP, CAP, 1))(routes_keys, routes_turns).reshape((SEQS, SEQ, TOP))
    cotangent = bell_draw(arg_keys[12], (SEQS, SEQ, D), 1.0, 6.0, ((0, 16), (1, 8)))
    return {"tokens": tokens, "norm_attn": norm_attn, "w_query": w_query, "w_key": w_key, "w_value": w_value, "w_out": w_out, "norm_moe": norm_moe, "w_router": w_router, "w_gate": w_gate, "w_up": w_up, "w_down": w_down, "routes": routes, "cotangent": cotangent}


EPSILON = 1e-06
PRECISE = lax.Precision.HIGHEST

@jax.custom_vjp
def low(v):
    return lax.optimization_barrier(v.astype(jnp.bfloat16)).astype(jnp.float32)

@jax.custom_vjp
def low_back(v):
    return v

def low_keep(v):
    return (low(v), None)

def low_pass(kept, grad):
    return (grad,)

def back_keep(v):
    return (v, None)

def back_low(kept, grad):
    return (low(grad),)
low.defvjp(low_keep, low_pass)
low_back.defvjp(back_keep, back_low)

def rms_scale(values, gain):
    return values * lax.rsqrt(lax.optimization_barrier(jnp.mean(values * values, axis=-1, keepdims=True)) + EPSILON) * gain

def matmul(left, right):
    return jnp.dot(left, right, precision=PRECISE, preferred_element_type=jnp.float32)

def rounded(values):
    return low(low_back(values))

def attend(inputs):
    queries, key_rows, value_rows = inputs
    length = queries.shape[0]
    query_heads = queries.reshape(length, KV_HEADS, HEADS // KV_HEADS, HEAD)
    key_heads = key_rows.reshape(length, KV_HEADS, HEAD)
    value_heads = value_rows.reshape(length, KV_HEADS, HEAD)
    scores = low_back(jnp.einsum('qgjd,kgd->qgjk', query_heads, key_heads, precision=PRECISE) * HEAD ** (-0.5))
    position = jnp.arange(length)
    causal = (position[None, :] <= position[:, None])[:, None, None, :]
    scores = jnp.where(causal, scores, -1e+30)
    weights = low(jax.nn.softmax(scores, axis=-1))
    mixed_rows = jnp.einsum('qgjk,kgd->qgjd', weights, value_heads, precision=PRECISE)
    return mixed_rows.reshape(length, HEADS * HEAD)

def expert_block(inputs, w_gate, w_up, w_down):
    normed, route_rows, gate_weights = inputs
    flat_routes = route_rows.reshape(-1)
    onehot = (flat_routes[:, None] == jnp.arange(EXPERTS, dtype=jnp.int32)[None, :]).astype(jnp.int32)
    position = lax.optimization_barrier(jnp.sum((jnp.cumsum(onehot, axis=0) - onehot) * onehot, axis=1)).astype(jnp.int32)
    slot_index = (flat_routes * CAP + position).astype(jnp.int32)
    copies = low_back(jnp.repeat(normed, TOP, axis=0))
    buffer = jnp.zeros((EXPERTS * CAP, D), jnp.float32).at[slot_index].set(copies).reshape(EXPERTS, CAP, D)
    gate_part = low_back(jnp.einsum('ecd,edf->ecf', buffer, w_gate, precision=PRECISE))
    up_part = low_back(jnp.einsum('ecd,edf->ecf', buffer, w_up, precision=PRECISE))
    hidden = low(jax.nn.silu(gate_part) * up_part)
    produced = rounded(jnp.einsum('ecf,efd->ecd', hidden, w_down, precision=PRECISE))
    picked = produced.reshape(EXPERTS * CAP, D)[slot_index].reshape(route_rows.shape[0], TOP, D)
    return lax.optimization_barrier(jnp.sum(picked * gate_weights[:, :, None], axis=1))

def forward(tokens, norm_attn, w_query, w_key, w_value, w_out, norm_moe, w_router, w_gate, w_up, w_down, routes):
    token_rows = tokens.reshape(-1, D)
    attn_in = low(rms_scale(token_rows, norm_attn))
    queries = rounded(matmul(attn_in, w_query)).reshape(SEQS, SEQ, QW)
    key_rows = rounded(matmul(attn_in, w_key)).reshape(SEQS, SEQ, KVW)
    value_rows = rounded(matmul(attn_in, w_value)).reshape(SEQS, SEQ, KVW)
    mixed_rows = lax.map(jax.checkpoint(attend), (queries, key_rows, value_rows)).reshape(-1, QW)
    mixed_rows = rounded(mixed_rows)
    resid = token_rows + low_back(matmul(mixed_rows, w_out))
    moe_in = low(rms_scale(resid, norm_moe))
    logits = matmul(moe_in, w_router)
    route_rows = routes.reshape(-1, TOP)
    chosen = jnp.take_along_axis(logits, route_rows, axis=1)
    gate_weights = jax.nn.softmax(chosen, axis=-1)
    block_count = route_rows.shape[0] // TOK_DEV
    blocks = (moe_in.reshape(block_count, TOK_DEV, D), route_rows.reshape(block_count, TOK_DEV, TOP), gate_weights.reshape(block_count, TOK_DEV, TOP))

    def one_block(part):
        return expert_block(part, w_gate, w_up, w_down)
    expert_out = lax.map(jax.checkpoint(one_block), blocks).reshape(-1, D)
    return (resid + expert_out).reshape(tokens.shape)

def reference(tokens, norm_attn, w_query, w_key, w_value, w_out, norm_moe, w_router, w_gate, w_up, w_down, routes, cotangent):
    floats = [item.astype(jnp.float32) for item in (tokens, norm_attn, w_query, w_key, w_value, w_out, norm_moe, w_router, w_gate, w_up, w_down)]

    def closed(*weights):
        return forward(*weights, routes)
    result, pull = jax.vjp(closed, *floats)
    grads = pull(cotangent.astype(jnp.float32))
    return (result.astype(jnp.bfloat16), grads[0].astype(jnp.bfloat16), grads[1], grads[2], grads[3], grads[4], grads[5], grads[6], grads[7], grads[8], grads[9], grads[10])
```

```python
import jax
import jax.numpy as jnp
from jax import lax
from jax.experimental import pallas as pl
from jax.experimental.pallas import tpu as pltpu
from jax.sharding import PartitionSpec as P

EPSILON = 1e-06
PRECISE = lax.Precision.HIGHEST
F32, BF16 = jnp.float32, jnp.bfloat16
VMEM = pltpu.VMEM
MESH = pl.DeviceIdType.MESH
SIDE = 4
ROWS = 256
CAP = 96
GROUP = 4


def exp_block(first, second, half, inner):
    index = lax.axis_index("exp")
    z, x = lax.div(index, SIDE), lax.rem(index, SIDE)
    by_x, by_z = (first, second) if half == inner else (second, first)
    return lax.rem(z + by_z + SIDE, SIDE) * SIDE + lax.rem(x + by_x + SIDE, SIDE)


def greet_exp():
    barrier = pltpu.get_barrier_semaphore()
    for half in range(2):
        for step in (1, -1):
            pl.semaphore_signal(
                barrier, inc=1, device_id={"exp": exp_block(step, 0, half, 0)}, device_id_type=MESH
            )
    pl.semaphore_wait(barrier, 4)


def gather_exp_copy(own, out, send, recv, rows, half, axis, k, s):
    part = rows // 4
    step = (1, -1, 1, -1)[s]
    off = (0, 0, -1, 1)[s]
    origin = exp_block(off, 0, half, 0) if axis == 1 else exp_block(k, off, half, 0)
    target = exp_block(step, 0, half, 0) if axis == 1 else exp_block(0, step, half, 0)
    lines = (
        pl.ds(half * 2 * part, 2 * part)
        if s < 2
        else pl.ds((half * 2 + s - 2) * part, part)
    )
    mine = s < 2 and (axis == 1 or k == 0)
    at = half * 20 + (s if axis == 1 else 4 + 4 * (k % 4) + s)
    return pltpu.make_async_remote_copy(
        src_ref=own.at[lines] if mine else out.at[origin, lines],
        dst_ref=out.at[origin, lines],
        send_sem=send.at[at],
        recv_sem=recv.at[at],
        device_id={"exp": target},
        device_id_type=MESH,
    )


def gather_exp_kernel(own, out, send, recv, local):
    rows = own.shape[0]
    greet_exp()
    copies = {
        (half, axis, k, s): gather_exp_copy(own, out, send, recv, rows, half, axis, k, s)
        for half in range(2)
        for axis, k in ((1, 0), (2, 0), (2, 1), (2, -1), (2, 2))
        for s in range(4)
    }
    keep = pltpu.make_async_copy(own, out.at[exp_block(0, 0, 0, 0)], local)
    keep.start()
    for axis in (1, 2):
        for s in (0, 1):
            for half in range(2):
                copies[half, axis, 0, s].start()
    for s, k in ((0, -1), (1, 1)):
        for half in range(2):
            copies[half, 1, 0, s].wait_recv()
            copies[half, 1, 0, s + 2].start()
            copies[half, 2, k, 0].start()
            copies[half, 2, k, 1].start()
    for s in (0, 1):
        for half in range(2):
            copies[half, 2, 0, s].wait_recv()
            copies[half, 2, 0, s + 2].start()
    for half in range(2):
        copies[half, 1, 0, 2].wait_recv()
        copies[half, 1, 0, 3].wait_recv()
        copies[half, 2, 2, 0].start()
        copies[half, 2, 2, 1].start()
    for k in (-1, 1, 2):
        for s in (0, 1):
            for half in range(2):
                copies[half, 2, k, s].wait_recv()
                copies[half, 2, k, s + 2].start()
    for k in (0, -1, 1, 2):
        for s in (2, 3):
            for half in range(2):
                copies[half, 2, k, s].wait_recv()
    for copy in copies.values():
        copy.wait_send()
    keep.wait()


def gather_exp(block, collective_id):
    rows, width = block.shape
    return pl.pallas_call(
        gather_exp_kernel,
        out_shape=jax.ShapeDtypeStruct((16, rows, width), block.dtype),
        in_specs=[pl.BlockSpec(memory_space=pl.ANY)],
        out_specs=pl.BlockSpec(memory_space=pl.ANY),
        scratch_shapes=[
            pltpu.SemaphoreType.DMA((40,)),
            pltpu.SemaphoreType.DMA((40,)),
            pltpu.SemaphoreType.DMA,
        ],
        compiler_params=pltpu.CompilerParams(collective_id=collective_id, has_side_effects=True),
    )(block)


def reduce_exp_copy(parts, landed, send, recv, half, axis, k, s):
    step = (1, -1, 1, -1)[s]
    dest = (2, 2, 1, -1)[s]
    block = exp_block(dest, k, half, 1) if axis == 1 else exp_block(0, dest, half, 1)
    target = exp_block(step, 0, half, 1) if axis == 1 else exp_block(0, step, half, 1)
    row = half * 5 + (k % 4 if axis == 1 else 4)
    source = (
        parts.at[block, pl.ds(2 * half + s, 1)] if s < 2 else parts.at[block, pl.ds(2 * half, 2)]
    )
    place = (pl.ds(0, 1), pl.ds(1, 1), pl.ds(2, 2), pl.ds(4, 2))[s]
    at = row * 4 + s
    return pltpu.make_async_remote_copy(
        src_ref=source,
        dst_ref=landed.at[row, place],
        send_sem=send.at[at],
        recv_sem=recv.at[at],
        device_id={"exp": target},
        device_id_type=MESH,
    )


def add_lines(total, others, step):
    lines = total.shape[0]

    @pl.loop(0, lines // step)
    def _(i):
        at = pl.ds(pl.multiple_of(i * step, step), step)
        value = total[at].astype(jnp.float32)
        for other in others:
            value = value + other[at].astype(jnp.float32)
        total[at] = value.astype(total.dtype)


def reduce_exp_kernel(given, out, parts, landed, send, recv, local, done):
    greet_exp()
    lines = given.shape[2]
    step = 16
    load = pltpu.make_async_copy(given, parts, local)
    load.start()
    load.wait()
    copies = {
        (half, axis, k, s): reduce_exp_copy(parts, landed, send, recv, half, axis, k, s)
        for half in range(2)
        for axis, k in ((1, 0), (1, 1), (1, -1), (1, 2), (2, 0))
        for s in range(4)
    }

    def row_of(half, axis, k):
        return half * 5 + (k % 4 if axis == 1 else 4)

    def block_of(half, axis, k, dest):
        return exp_block(dest, k, half, 1) if axis == 1 else exp_block(0, dest, half, 1)

    def pass_on(half, axis, k):
        for s, dest in ((0, 1), (1, -1)):
            copies[half, axis, k, s].wait_recv()
            add_lines(
                parts.at[block_of(half, axis, k, dest), 2 * half + s],
                [landed.at[row_of(half, axis, k), s]],
                step,
            )
            copies[half, axis, k, s + 2].start()

    def finish(half, axis, k):
        copies[half, axis, k, 2].wait_recv()
        copies[half, axis, k, 3].wait_recv()
        for part in range(2):
            add_lines(
                parts.at[block_of(half, axis, k, 0), 2 * half + part],
                [
                    landed.at[row_of(half, axis, k), 2 + part],
                    landed.at[row_of(half, axis, k), 4 + part],
                ],
                step,
            )

    order = (2, 1, -1, 0)
    for k in order:
        for half in range(2):
            for s in (0, 1):
                copies[half, 1, k, s].start()
    for k in order:
        for half in range(2):
            pass_on(half, 1, k)
    for k in order:
        for half in range(2):
            finish(half, 1, k)
            if k == 2:
                copies[half, 2, 0, 0].start()
                copies[half, 2, 0, 1].start()
    for half in range(2):
        pass_on(half, 2, 0)
    for half in range(2):
        finish(half, 2, 0)
    store = pltpu.make_async_copy(parts.at[exp_block(0, 0, 0, 0)], out, done)
    store.start()
    for copy in copies.values():
        copy.wait_send()
    store.wait()


def reduce_exp(parts, collective_id):
    _, quarters, lines, width = parts.shape
    return pl.pallas_call(
        reduce_exp_kernel,
        out_shape=jax.ShapeDtypeStruct((quarters, lines, width), parts.dtype),
        in_specs=[pl.BlockSpec(memory_space=pl.ANY)],
        out_specs=pl.BlockSpec(memory_space=pl.ANY),
        scratch_shapes=[
            pltpu.VMEM(parts.shape, parts.dtype),
            pltpu.VMEM((10, 6, lines, width), parts.dtype),
            pltpu.SemaphoreType.DMA((40,)),
            pltpu.SemaphoreType.DMA((40,)),
            pltpu.SemaphoreType.DMA,
            pltpu.SemaphoreType.DMA,
        ],
        compiler_params=pltpu.CompilerParams(
            collective_id=collective_id, has_side_effects=True, vmem_limit_bytes=40 << 20
        ),
    )(parts)


def ctx_block(step, other):
    index = lax.axis_index("ctx")
    y, core = lax.div(index, 2), lax.rem(index, 2)
    if other:
        core = 1 - core
    return lax.rem(y + step + SIDE, SIDE) * 2 + core


def greet_ctx():
    barrier = pltpu.get_barrier_semaphore()
    for step, other in ((1, False), (-1, False), (0, True)):
        pl.semaphore_signal(
            barrier, inc=1, device_id={"ctx": ctx_block(step, other)}, device_id_type=MESH
        )
    pl.semaphore_wait(barrier, 3)


def gather_ctx_copies(own, out, send, recv):
    half = own.shape[0] // 2
    every, first, second = pl.ds(0, 2 * half), pl.ds(0, half), pl.ds(half, half)
    plan = (
        (0, every, 0, True),
        (0, every, 1, False),
        (0, every, -1, False),
        (-1, first, 1, False),
        (1, second, -1, False),
        (-1, every, 0, True),
        (1, every, 0, True),
        (2, first, 0, True),
        (2, second, 0, True),
    )
    copies = []
    for at, (origin, lines, step, other) in enumerate(plan):
        slot = out.at[ctx_block(origin, False), lines]
        copies.append(
            pltpu.make_async_remote_copy(
                src_ref=own.at[lines] if origin == 0 else slot,
                dst_ref=slot,
                send_sem=send.at[at],
                recv_sem=recv.at[at],
                device_id={"ctx": ctx_block(step, other)},
                device_id_type=MESH,
            )
        )
    return copies


def gather_ctx_kernel(own, out, send, recv, local):
    greet_ctx()
    copies = gather_ctx_copies(own, out, send, recv)
    for at in (1, 2, 0):
        copies[at].start()
    keep = pltpu.make_async_copy(own, out.at[ctx_block(0, False)], local)
    keep.start()
    for arrival, follow in ((1, (3, 5)), (2, (4, 6)), (3, (7,)), (4, (8,))):
        copies[arrival].wait_recv()
        for at in follow:
            copies[at].start()
    for at in (0, 5, 6, 7, 8):
        copies[at].wait_recv()
    for copy in copies:
        copy.wait_send()
    keep.wait()


def gather_ctx(block, collective_id):
    return pl.pallas_call(
        gather_ctx_kernel,
        out_shape=jax.ShapeDtypeStruct((8,) + block.shape, block.dtype),
        in_specs=[pl.BlockSpec(memory_space=pl.ANY)],
        out_specs=pl.BlockSpec(memory_space=pl.ANY),
        scratch_shapes=[
            pltpu.SemaphoreType.DMA((9,)),
            pltpu.SemaphoreType.DMA((9,)),
            pltpu.SemaphoreType.DMA,
        ],
        compiler_params=pltpu.CompilerParams(collective_id=collective_id, has_side_effects=True),
    )(block)


def reduce_ctx_kernel(given, out, parts, landed, near, send, recv, local, done):
    lines = given.shape[1]
    half = lines // 2
    greet_ctx()
    first, second, every = pl.ds(0, half), pl.ds(half, half), pl.ds(0, lines)

    def remote(src, dst, at, step, other):
        return pltpu.make_async_remote_copy(
            src_ref=src,
            dst_ref=dst,
            send_sem=send.at[at],
            recv_sem=recv.at[at],
            device_id={"ctx": ctx_block(step, other)},
            device_id_type=MESH,
        )

    swaps, loads = {}, {}
    for at, step in enumerate((2, 1, -1, 0)):
        swaps[step] = remote(given.at[ctx_block(step, True)], near.at[at], at, 0, True)
        swaps[step].start()
        loads[step] = pltpu.make_async_copy(
            given.at[ctx_block(step, False)], parts.at[at], local.at[at]
        )
        loads[step].start()
    hops = (
        remote(parts.at[0, first], landed.at[0, first], 4, 1, False),
        remote(parts.at[0, second], landed.at[0, second], 5, -1, False),
        remote(parts.at[1], landed.at[1], 6, 1, False),
        remote(parts.at[2], landed.at[2], 7, -1, False),
    )
    for at, step in enumerate((2, 1, -1, 0)):
        loads[step].wait()
        swaps[step].wait_recv()
        add_lines(parts.at[at], [near.at[at]], 16)
        if step == 2:
            hops[0].start()
            hops[1].start()
        if step == 1:
            hops[0].wait_recv()
            add_lines(parts.at[1, first], [landed.at[0, first]], 16)
            hops[2].start()
        if step == -1:
            hops[1].wait_recv()
            add_lines(parts.at[2, second], [landed.at[0, second]], 16)
            hops[3].start()
    hops[2].wait_recv()
    hops[3].wait_recv()
    add_lines(parts.at[3], [landed.at[1], landed.at[2]], 16)
    store = pltpu.make_async_copy(parts.at[3], out, done)
    store.start()
    for copy in (*swaps.values(), *hops):
        copy.wait_send()
    store.wait()


def reduce_ctx(parts, collective_id):
    _, lines, width = parts.shape
    return pl.pallas_call(
        reduce_ctx_kernel,
        out_shape=jax.ShapeDtypeStruct((lines, width), parts.dtype),
        in_specs=[pl.BlockSpec(memory_space=pl.ANY)],
        out_specs=pl.BlockSpec(memory_space=pl.ANY),
        scratch_shapes=[
            pltpu.VMEM((4, lines, width), parts.dtype),
            pltpu.VMEM((3, lines, width), parts.dtype),
            pltpu.VMEM((4, lines, width), parts.dtype),
            pltpu.SemaphoreType.DMA((8,)),
            pltpu.SemaphoreType.DMA((8,)),
            pltpu.SemaphoreType.DMA((4,)),
            pltpu.SemaphoreType.DMA,
        ],
        compiler_params=pltpu.CompilerParams(
            collective_id=collective_id, has_side_effects=True, vmem_limit_bytes=40 << 20
        ),
    )(parts)


def dot(a, b, dims=((1,), (0,))):
    return lax.dot_general(a, b, (dims, ((), ())), preferred_element_type=F32)


def vmem(shape=None, index=None):
    return pl.BlockSpec(memory_space=VMEM)


def whole(*shape):
    return pl.BlockSpec(shape, lambda *_: (0,) * len(shape), pipeline_mode=pl.Buffered(1))


def side_by_side(a):
    return jnp.concatenate([a[:64], a[64:]], axis=1)


def one_below(a):
    return jnp.concatenate([a[:, :64], a[:, 64:]], axis=0)


def attend_kernel(
    tokens, gain, weights, attn_in, q_t, q_s, k_s, k_t, v_s, v_t, lse, exact, mixed
):
    scale = gain[...]

    @pl.loop(0, 8)
    def _(i):
        at = pl.ds(pl.multiple_of(i * ROWS, ROWS), ROWS)
        x = tokens[at].astype(F32)
        x = x * lax.rsqrt(jnp.mean(x * x, axis=1, keepdims=True) + EPSILON) * scale
        x = x.astype(BF16)
        attn_in[at] = x
        qkv = dot(x, weights[...]).astype(BF16).astype(F32)
        q = qkv[:, :128] * 0.125
        k, v = qkv[:, 128:192], qkv[:, 192:]
        q_s[i] = one_below(q).astype(BF16)
        q_t[i] = side_by_side(q.T).astype(BF16)
        k_s[i] = k.astype(BF16)
        v_s[i] = v.astype(BF16)
        kv_t = qkv[:, 128:].T
        k_t[i] = kv_t[:64].astype(BF16)
        v_t[i] = kv_t[64:].astype(BF16)

    key_row = lax.broadcasted_iota(jnp.int32, (ROWS, 2 * ROWS), 0)
    query_row = lax.rem(lax.broadcasted_iota(jnp.int32, (ROWS, 2 * ROWS), 1), ROWS)
    seen = key_row <= query_row

    @pl.loop(0, 8)
    def _(i):
        query = q_t[i]

        def add_block(j, carry, diagonal):
            top, total, acc = carry
            scores = dot(k_s[j], query)
            if diagonal:
                scores = jnp.where(seen, scores, -1e30)
            new_top = jnp.maximum(top, jnp.max(scores, axis=0, keepdims=True))
            fade = jnp.exp(top - new_top)
            weights = jnp.exp(scores - new_top)
            total = total * fade + jnp.sum(weights, axis=0, keepdims=True)
            acc = acc * fade + dot(v_t[j], weights.astype(BF16))
            return new_top, total, acc

        carry = (
            jnp.full((1, 2 * ROWS), -1e30, F32),
            jnp.zeros((1, 2 * ROWS), F32),
            jnp.zeros((64, 2 * ROWS), F32),
        )
        carry = lax.fori_loop(0, i, lambda j, c: add_block(j, c, False), carry)
        top, total, acc = add_block(i, carry, True)
        lse[i] = top + jnp.log(total)
        value = acc / total
        exact[i] = value
        both = jnp.concatenate([value[:, :ROWS], value[:, ROWS:]], axis=0)
        at = pl.ds(pl.multiple_of(i * ROWS, ROWS), ROWS)
        mixed[at] = both.T.astype(BF16)


def attend(tokens, gain, weights):
    shapes = [
        ((2048, 1024), BF16),
        ((8, 64, 512), BF16),
        ((8, 512, 64), BF16),
        ((8, 256, 64), BF16),
        ((8, 64, 256), BF16),
        ((8, 256, 64), BF16),
        ((8, 64, 256), BF16),
        ((8, 1, 512), F32),
        ((8, 64, 512), F32),
        ((2048, 128), BF16),
    ]
    return pl.pallas_call(
        attend_kernel,
        out_shape=[jax.ShapeDtypeStruct(s, t) for s, t in shapes],
        in_specs=[vmem()] * 3,
        out_specs=[vmem()] * len(shapes),
        compiler_params=pltpu.CompilerParams(vmem_limit_bytes=50 << 20),
    )(tokens, gain, weights)


def attend_back_kernel(
    mixed_grad, q_t, q_s, k_s, k_t, v_s, lse, exact, d, out_s, out_t, delta, dq
):
    @pl.loop(0, 8)
    def _(i):
        at = pl.ds(pl.multiple_of(i * ROWS, ROWS), ROWS)
        g = mixed_grad[at].astype(F32)
        out_s[i] = one_below(g).astype(BF16)
        g = side_by_side(g.T)
        out_t[i] = g.astype(BF16)
        delta[i] = jnp.sum(g * exact[i], axis=0, keepdims=True)
        dq[i] = jnp.zeros_like(dq[i])

    key_row = lax.broadcasted_iota(jnp.int32, (ROWS, 2 * ROWS), 0)
    query_row = lax.rem(lax.broadcasted_iota(jnp.int32, (ROWS, 2 * ROWS), 1), ROWS)
    seen = key_row <= query_row

    @pl.loop(0, 8)
    def _(j):
        key, key_t, value = k_s[j], k_t[j], v_s[j]

        def add_block(i, carry, diagonal):
            dk, dv = carry
            probs = jnp.exp(dot(key, q_t[i]) - lse[i])
            if diagonal:
                probs = jnp.where(seen, probs, 0.0)
            grad = probs * (dot(value, out_t[i]) - delta[i])
            grad = grad.astype(BF16)
            dv = dv + dot(probs.astype(BF16), out_s[i])
            dk = dk + dot(grad, q_s[i])
            dq[i] += dot(key_t, grad)
            return dk, dv

        zero = jnp.zeros((ROWS, 64), F32)
        carry = add_block(j, (zero, zero), True)
        dk, dv = lax.fori_loop(j + 1, 8, lambda i, c: add_block(i, c, False), carry)
        at = pl.ds(pl.multiple_of(j * ROWS, ROWS), ROWS)
        d[at, 128:256] = jnp.concatenate([dk, dv], axis=1).astype(BF16)

    @pl.loop(0, 8)
    def _(i):
        at = pl.ds(pl.multiple_of(i * ROWS, ROWS), ROWS)
        g = dq[i] * 0.125
        g = jnp.concatenate([g[:, :ROWS], g[:, ROWS:]], axis=0)
        d[at, 0:128] = g.T.astype(BF16)


def attend_back(mixed_grad, q_t, q_s, k_s, k_t, v_s, lse, exact):
    return pl.pallas_call(
        attend_back_kernel,
        out_shape=jax.ShapeDtypeStruct((2048, 256), BF16),
        in_specs=[vmem()] * 8,
        out_specs=vmem(),
        scratch_shapes=[
            VMEM((8, 512, 64), BF16),
            VMEM((8, 64, 512), BF16),
            VMEM((8, 1, 512), F32),
            VMEM((8, 64, 512), F32),
        ],
        compiler_params=pltpu.CompilerParams(vmem_limit_bytes=50 << 20),
    )(mixed_grad, q_t, q_s, k_s, k_t, v_s, lse, exact)


def experts_kernel(
    owner, moe, cot, routes, router, weights,
    out_parts, grad_parts, rows, slot_grads, hidden, gate_grads, up_grads,
):
    own = owner[0]
    w_gate, w_up, w_down = weights.at[0], weights.at[1], weights.at[2]
    expert = lax.broadcasted_iota(jnp.int32, (32, ROWS), 0)
    named = [[None, None] for _ in range(GROUP)]
    gates = [[None, None] for _ in range(GROUP)]
    for b in range(GROUP):
        logits = dot(router[...], moe[b], ((1,), (1,)))
        chosen = expert < 0
        for j in range(8):
            chosen = chosen | (routes[b, j : j + 1, :] == expert)
        logits = jnp.where(chosen, logits, -1e30)
        weight = jnp.where(chosen, jnp.exp(logits - jnp.max(logits, axis=0, keepdims=True)), 0.0)
        weight = weight / jnp.sum(weight, axis=0, keepdims=True)
        for k in range(2):
            mine = expert == 2 * own + k
            gates[b][k] = jnp.sum(jnp.where(mine, weight, 0.0), axis=0, keepdims=True)
            named[b][k] = jnp.sum(
                jnp.where(mine & chosen, 1.0, 0.0), axis=0, keepdims=True
            )
    before = lax.broadcasted_iota(jnp.int32, (ROWS, ROWS), 0) < lax.broadcasted_iota(
        jnp.int32, (ROWS, ROWS), 1
    )
    flat = jnp.concatenate([named[b][k] for b in range(GROUP) for k in range(2)], axis=0)
    place = dot(flat.astype(BF16), before.astype(BF16))
    slot = lax.broadcasted_iota(jnp.int32, (CAP, ROWS), 0).astype(F32)
    spread = [[None, None] for _ in range(GROUP)]
    slot_gates = [[None, None] for _ in range(GROUP)]
    for b in range(GROUP):
        for k in range(2):
            at = 2 * b + k
            hit = (slot == place[at : at + 1]) & (flat[at : at + 1] > 0.5)
            spread[b][k] = jnp.where(hit, 1.0, 0.0).astype(BF16)
            slot_gates[b][k] = jnp.sum(
                jnp.where(hit, gates[b][k], 0.0), axis=1, keepdims=True
            )
    pick = [jnp.concatenate(spread[b], axis=0) for b in range(GROUP)]
    cots = [None] * GROUP
    for b in range(GROUP):
        both = dot(pick[b], moe[b]).astype(BF16)
        rows[0, b] = both[:CAP]
        rows[1, b] = both[CAP:]
        cots[b] = dot(pick[b], cot[b])
        for k in range(2):
            slot_grads[k, b] = (slot_gates[b][k] * cots[b][k * CAP : (k + 1) * CAP]).astype(BF16)
    gated = [None, None]
    row_grads = [None, None]
    weight_grads = [None, None]
    for k in range(2):
        x = rows[k].reshape(GROUP * CAP, 1024)
        dy = slot_grads[k].reshape(GROUP * CAP, 1024)
        g = dot(x, w_gate[k])
        u = dot(x, w_up[k])
        s = jax.nn.sigmoid(g)
        silu = g * s
        h = (silu * u).astype(BF16)
        hidden[k] = h.reshape(GROUP, CAP, 512)
        y = dot(h, w_down[k], ((1,), (1,))).astype(BF16).astype(F32)
        gate = jnp.concatenate([slot_gates[b][k] for b in range(GROUP)], axis=0)
        gated[k] = (gate * y).astype(BF16)
        upstream = jnp.concatenate(
            [cots[b][k * CAP : (k + 1) * CAP] for b in range(GROUP)], axis=0
        )
        weight_grads[k] = jnp.sum(upstream * y, axis=1, keepdims=True)
        dh = dot(dy, w_down[k])
        gg = (dh * u * s * (1.0 + g * (1.0 - s))).astype(BF16)
        ug = (dh * silu).astype(BF16)
        gate_grads[k] = gg.reshape(GROUP, CAP, 512)
        up_grads[k] = ug.reshape(GROUP, CAP, 512)
        row_grads[k] = (
            dot(gg, w_gate[k], ((1,), (1,))) + dot(ug, w_up[k], ((1,), (1,)))
        ).astype(BF16)
    owner_row = lax.broadcasted_iota(jnp.int32, (16, ROWS), 0) == own
    for b in range(GROUP):
        at = slice(b * CAP, (b + 1) * CAP)
        for source, target in ((gated, out_parts), (row_grads, grad_parts)):
            both = jnp.concatenate([source[0][at], source[1][at]], axis=0)
            total = dot(pick[b], both, ((0,), (0,))).astype(BF16)
            for q in range(4):
                target[b, q, 0:ROWS] = total[:, q * 256 : (q + 1) * 256]
        for k in range(2):
            vector = jnp.sum(
                spread[b][k].astype(F32) * weight_grads[k][at], axis=0, keepdims=True
            )
            high = vector.astype(BF16)
            low = (vector - high.astype(F32)).astype(BF16)
            grad_parts[b, 2 * k, ROWS : ROWS + 16] = jnp.where(
                owner_row, high.astype(F32), 0.0
            ).astype(BF16)
            grad_parts[b, 2 * k + 1, ROWS : ROWS + 16] = jnp.where(
                owner_row, low.astype(F32), 0.0
            ).astype(BF16)


def experts(owner, moe, cot, routes, router, weights):
    steps = 16 // GROUP

    def block(*shape, dim=0):
        def index(g, owner):
            return tuple(g if i == dim else 0 for i in range(len(shape)))

        return pl.BlockSpec(shape, index)

    outs = [
        ((16, 4, 256, 256), BF16),
        ((16, 4, 272, 256), BF16),
        ((2, 16, CAP, 1024), BF16),
        ((2, 16, CAP, 1024), BF16),
        ((2, 16, CAP, 512), BF16),
        ((2, 16, CAP, 512), BF16),
        ((2, 16, CAP, 512), BF16),
    ]
    return pl.pallas_call(
        experts_kernel,
        grid_spec=pltpu.PrefetchScalarGridSpec(
            num_scalar_prefetch=1,
            grid=(steps,),
            in_specs=[
                block(GROUP, 256, 1024),
                block(GROUP, 256, 1024),
                block(GROUP, 8, 256),
                whole(32, 1024),
                whole(3, 2, 1024, 512),
            ],
            out_specs=[
                block(GROUP, 4, 256, 256),
                block(GROUP, 4, 272, 256),
                block(2, GROUP, CAP, 1024, dim=1),
                block(2, GROUP, CAP, 1024, dim=1),
                block(2, GROUP, CAP, 512, dim=1),
                block(2, GROUP, CAP, 512, dim=1),
                block(2, GROUP, CAP, 512, dim=1),
            ],
        ),
        out_shape=[jax.ShapeDtypeStruct(s, t) for s, t in outs],
        compiler_params=pltpu.CompilerParams(vmem_limit_bytes=58 << 20),
    )(owner, moe, cot, routes, router, weights)


def rms_scale(values, gain):
    return values * lax.rsqrt(jnp.mean(values * values, axis=-1, keepdims=True) + EPSILON) * gain


def per_device(
    tokens,
    norm_attn,
    w_query,
    w_key,
    w_value,
    w_out,
    norm_moe,
    w_router,
    w_gate,
    w_up,
    w_down,
    routes,
    cotangent,
):
    exp = lax.axis_index("exp")
    narrow = jnp.concatenate(
        [w_query, w_key, w_value, w_out, w_router, norm_moe[:, None], norm_attn[:, None]], axis=1
    )
    group_rows = lax.all_gather(narrow, "exp", axis=0, tiled=True)
    everyone = gather_ctx(tokens[0], 1).reshape(2048, 1024)
    by_head = jnp.concatenate(
        [
            group_rows[:, :1024].reshape(128, 8, 128),
            group_rows[:, 1024:1536].reshape(128, 8, 64),
            group_rows[:, 1536:2048].reshape(128, 8, 64),
            jnp.broadcast_to(group_rows[:, None, 3105:3106], (128, 8, 128)),
        ],
        axis=2,
    )
    by_head = lax.all_to_all(
        by_head.transpose(1, 0, 2), "ctx", split_axis=0, concat_axis=0, tiled=True
    ).reshape(1024, 384)
    head_weights = by_head[:, :256]
    gain_attn = by_head[:, 256].astype(F32)[None, :]
    wide = lax.all_gather(group_rows[:, 2048:3105], "ctx", axis=0, tiled=True)
    full_out, full_router = wide[:, :1024], wide[:, 1024:1056]
    gain_moe = wide[:, 1056].astype(F32)
    router_t = full_router.T
    all_cot = lax.all_gather(cotangent[0], "exp", axis=0, tiled=True).reshape(16, 256, 1024)
    all_routes = lax.all_gather(routes[0].T, "exp", axis=0, tiled=True).reshape(16, 8, 256)
    own_experts = jnp.stack([w_gate, w_up, w_down.transpose(0, 2, 1)]).reshape(768, 512)
    all_experts = gather_ctx(own_experts, 2).reshape(8, 3, 2, 128, 512)
    all_experts = all_experts.transpose(1, 2, 0, 3, 4).reshape(3, 2, 1024, 512)

    attn_in, q_t, q_s, k_s, k_t, v_s, v_t, lse, exact, mixed = attend(
        everyone, gain_attn, head_weights
    )
    mixed_rows = lax.all_to_all(
        mixed.reshape(8, 256, 128), "ctx", split_axis=0, concat_axis=0, tiled=True
    )
    mixed_rows = mixed_rows.transpose(1, 0, 2).reshape(256, 1024)
    token_rows = tokens[0].astype(F32)
    resid = token_rows + jnp.dot(mixed_rows, full_out, preferred_element_type=F32)
    moe_in = rms_scale(resid, gain_moe).astype(BF16)
    all_moe = gather_exp(moe_in, 3)
    out_parts, grad_parts, rows, slot_grads, hidden, gate_grads, up_grads = experts(
        exp.reshape(1).astype(jnp.int32), all_moe, all_cot, all_routes, router_t, all_experts
    )
    grad_total = reduce_exp(grad_parts, 4)
    expert_out = lax.psum_scatter(
        out_parts.reshape(-1, 256), "exp", scatter_dimension=0, tiled=True
    )
    expert_out = expert_out.reshape(4, 256, 256).transpose(1, 0, 2).reshape(256, 1024)
    output = (resid + expert_out.astype(F32)).astype(BF16)[None]

    flat = (2, 16 * CAP, -1)
    rows, slot_grads = rows.reshape(flat), slot_grads.reshape(flat)
    hidden, gate_grads, up_grads = (a.reshape(flat) for a in (hidden, gate_grads, up_grads))

    def expert_term(left, right):
        term = jnp.einsum("erd,erf->edf", left, right, preferred_element_type=F32).astype(BF16)
        return term.reshape(2, 8, 128, 512).transpose(1, 0, 2, 3)

    expert_terms = jnp.stack(
        [
            expert_term(rows, gate_grads),
            expert_term(rows, up_grads),
            expert_term(slot_grads, hidden),
        ],
        axis=1,
    ).reshape(8 * 768, 512)
    expert_sum = (
        lax.psum_scatter(expert_terms, "ctx", scatter_dimension=0, tiled=True)
        .astype(F32)
        .reshape(3, 2, 128, 512)
    )

    logits = jnp.dot(moe_in, full_router, preferred_element_type=F32)
    chosen = jnp.any(
        routes[0][:, :, None] == jnp.arange(32, dtype=jnp.int32)[None, None, :], axis=1
    )
    gates = jax.nn.softmax(jnp.where(chosen, logits, -1e30), axis=-1)
    weight_grad = (
        grad_total[:, ROWS:].astype(F32).reshape(2, 2, 16, 256).sum(axis=1)
    )
    weight_grad = weight_grad.transpose(2, 1, 0).reshape(256, 32)
    logit_grad = jnp.where(
        chosen,
        gates * (weight_grad - jnp.sum(gates * weight_grad, axis=-1, keepdims=True)),
        0.0,
    )
    router_term = jnp.dot(moe_in.astype(F32).T, logit_grad, precision=PRECISE)
    moe_in_grad = grad_total[:, :ROWS].astype(F32).transpose(1, 0, 2).reshape(256, 1024)
    moe_in_grad = moe_in_grad + jnp.dot(
        logit_grad, full_router.astype(F32).T, precision=PRECISE
    )
    unused_moe, pull_moe = jax.vjp(rms_scale, resid, gain_moe)
    resid_grad, norm_moe_term = pull_moe(moe_in_grad)
    resid_grad = resid_grad + cotangent[0].astype(F32)
    attn_grad = resid_grad.astype(BF16)
    mixed_grad = jnp.einsum(
        "td,qd->tq", attn_grad, full_out, preferred_element_type=F32
    ).astype(BF16)
    mixed_grad = lax.all_to_all(
        mixed_grad.reshape(256, 8, 128).transpose(1, 0, 2),
        "ctx",
        split_axis=0,
        concat_axis=0,
        tiled=True,
    ).reshape(2048, 128)
    all_attn_grad = gather_ctx(attn_grad, 5).reshape(2048, 1024)
    out_term = jnp.einsum("tq,td->qd", mixed, all_attn_grad, preferred_element_type=F32)
    head_grads = attend_back(mixed_grad, q_t, q_s, k_s, k_t, v_s, lse, exact)
    head_term = jnp.einsum("td,tq->dq", attn_in, head_grads, preferred_element_type=F32)
    attn_in_parts = jnp.einsum(
        "tq,dq->td", head_grads, head_weights, preferred_element_type=F32
    ).astype(BF16)
    attn_in_grad = reduce_ctx(attn_in_parts.reshape(8, 256, 1024), 6).astype(F32)

    small_term = jnp.concatenate([router_term, norm_moe_term[:, None]], axis=1)

    def by_exp(term):
        return term.reshape(-1, 16, 8, term.shape[1]).transpose(1, 0, 2, 3).reshape(16, -1)

    sums = jnp.concatenate([by_exp(head_term), by_exp(out_term), by_exp(small_term)], axis=1)
    sums = jnp.pad(sums.astype(BF16), ((0, 0), (0, 32768 - sums.shape[1])))
    sums = reduce_exp(sums.reshape(16, 4, 32, 256), 7).reshape(-1).astype(F32)
    out_sum = sums[16384:24576].reshape(8, 1024)
    spread = jnp.concatenate(
        [sums[:16384].reshape(8, 8, 256), sums[24576:26688].reshape(8, 8, 33)], axis=2
    )
    spread = lax.all_to_all(spread, "ctx", split_axis=0, concat_axis=0, tiled=True)
    small_sum = jnp.sum(spread[:, :, 256:], axis=0)
    query_sum = spread[:, :, :128].transpose(1, 0, 2).reshape(8, 1024)
    key_sum = spread[:, :, 128:192].transpose(1, 0, 2).reshape(8, 512)
    value_sum = spread[:, :, 192:256].transpose(1, 0, 2).reshape(8, 512)
    norm_attn_sum = (
        jnp.sum(query_sum * w_query.astype(F32), axis=1)
        + jnp.sum(key_sum * w_key.astype(F32), axis=1)
        + jnp.sum(value_sum * w_value.astype(F32), axis=1)
    ) / norm_attn.astype(F32)
    unused_attn, pull_attn = jax.vjp(lambda v: rms_scale(v, gain_attn), token_rows)
    (token_grad,) = pull_attn(attn_in_grad)
    token_grad = (token_grad + resid_grad).astype(BF16)[None]
    return (
        output,
        token_grad,
        norm_attn_sum,
        query_sum,
        key_sum,
        value_sum,
        out_sum,
        small_sum[:, 32],
        small_sum[:, :32],
        expert_sum[0],
        expert_sum[1],
        expert_sum[2].transpose(0, 2, 1),
    )


def solution(mesh):
    in_specs = (
        P("exp", "ctx", None),
        P(("ctx", "exp")),
        P(("ctx", "exp"), None),
        P(("ctx", "exp"), None),
        P(("ctx", "exp"), None),
        P(("ctx", "exp"), None),
        P(("ctx", "exp")),
        P(("ctx", "exp"), None),
        P("exp", "ctx", None),
        P("exp", "ctx", None),
        P("exp", None, "ctx"),
        P("exp", "ctx", None),
        P("exp", "ctx", None),
    )
    out_specs = (
        P("exp", "ctx", None),
        P("exp", "ctx", None),
        P(("ctx", "exp")),
        P(("ctx", "exp"), None),
        P(("ctx", "exp"), None),
        P(("ctx", "exp"), None),
        P(("ctx", "exp"), None),
        P(("ctx", "exp")),
        P(("ctx", "exp"), None),
        P("exp", "ctx", None),
        P("exp", "ctx", None),
        P("exp", None, "ctx"),
    )
    return jax.shard_map(
        per_device, mesh=mesh, in_specs=in_specs, out_specs=out_specs, check_vma=False
    )
```

```python
import jax
import jax.numpy as jnp
from jax import lax
from jax.experimental import pallas as pl
from jax.experimental.pallas import tpu as pltpu
from jax.sharding import PartitionSpec as P

EPSILON = 1e-06
PRECISE = lax.Precision.HIGHEST
F32, BF16 = jnp.float32, jnp.bfloat16
VMEM = pltpu.VMEM
MESH = pl.DeviceIdType.MESH
SIDE = 4
ROWS = 256
CAP = 96
GROUP = 4


def exp_block(first, second, half, inner):
    index = lax.axis_index("exp")
    z, x = lax.div(index, SIDE), lax.rem(index, SIDE)
    by_x, by_z = (first, second) if half == inner else (second, first)
    return lax.rem(z + by_z + SIDE, SIDE) * SIDE + lax.rem(x + by_x + SIDE, SIDE)


def greet_exp():
    barrier = pltpu.get_barrier_semaphore()
    for half in range(2):
        for step in (1, -1):
            pl.semaphore_signal(
                barrier, inc=1, device_id={"exp": exp_block(step, 0, half, 0)}, device_id_type=MESH
            )
    pl.semaphore_wait(barrier, 4)


def gather_exp_copy(own, out, send, recv, rows, half, axis, k, s):
    part = rows // 4
    step = (1, -1, 1, -1)[s]
    off = (0, 0, -1, 1)[s]
    origin = exp_block(off, 0, half, 0) if axis == 1 else exp_block(k, off, half, 0)
    target = exp_block(step, 0, half, 0) if axis == 1 else exp_block(0, step, half, 0)
    lines = (
        pl.ds(half * 2 * part, 2 * part)
        if s < 2
        else pl.ds((half * 2 + s - 2) * part, part)
    )
    mine = s < 2 and (axis == 1 or k == 0)
    at = half * 20 + (s if axis == 1 else 4 + 4 * (k % 4) + s)
    return pltpu.make_async_remote_copy(
        src_ref=own.at[lines] if mine else out.at[origin, lines],
        dst_ref=out.at[origin, lines],
        send_sem=send.at[at],
        recv_sem=recv.at[at],
        device_id={"exp": target},
        device_id_type=MESH,
    )


def gather_exp_kernel(own, out, send, recv, local):
    rows = own.shape[0]
    greet_exp()
    copies = {
        (half, axis, k, s): gather_exp_copy(own, out, send, recv, rows, half, axis, k, s)
        for half in range(2)
        for axis, k in ((1, 0), (2, 0), (2, 1), (2, -1), (2, 2))
        for s in range(4)
    }
    keep = pltpu.make_async_copy(own, out.at[exp_block(0, 0, 0, 0)], local)
    keep.start()
    for axis in (1, 2):
        for s in (0, 1):
            for half in range(2):
                copies[half, axis, 0, s].start()
    for s, k in ((0, -1), (1, 1)):
        for half in range(2):
            copies[half, 1, 0, s].wait_recv()
            copies[half, 1, 0, s + 2].start()
            copies[half, 2, k, 0].start()
            copies[half, 2, k, 1].start()
    for s in (0, 1):
        for half in range(2):
            copies[half, 2, 0, s].wait_recv()
            copies[half, 2, 0, s + 2].start()
    for half in range(2):
        copies[half, 1, 0, 2].wait_recv()
        copies[half, 1, 0, 3].wait_recv()
        copies[half, 2, 2, 0].start()
        copies[half, 2, 2, 1].start()
    for k in (-1, 1, 2):
        for s in (0, 1):
            for half in range(2):
                copies[half, 2, k, s].wait_recv()
                copies[half, 2, k, s + 2].start()
    for k in (0, -1, 1, 2):
        for s in (2, 3):
            for half in range(2):
                copies[half, 2, k, s].wait_recv()
    for copy in copies.values():
        copy.wait_send()
    keep.wait()


def gather_exp(block, collective_id):
    rows, width = block.shape
    return pl.pallas_call(
        gather_exp_kernel,
        out_shape=jax.ShapeDtypeStruct((16, rows, width), block.dtype),
        in_specs=[pl.BlockSpec(memory_space=pl.ANY)],
        out_specs=pl.BlockSpec(memory_space=pl.ANY),
        scratch_shapes=[
            pltpu.SemaphoreType.DMA((40,)),
            pltpu.SemaphoreType.DMA((40,)),
            pltpu.SemaphoreType.DMA,
        ],
        compiler_params=pltpu.CompilerParams(collective_id=collective_id, has_side_effects=True),
    )(block)


def reduce_exp_copy(parts, landed, send, recv, half, axis, k, s):
    step = (1, -1, 1, -1)[s]
    dest = (2, 2, 1, -1)[s]
    block = exp_block(dest, k, half, 1) if axis == 1 else exp_block(0, dest, half, 1)
    target = exp_block(step, 0, half, 1) if axis == 1 else exp_block(0, step, half, 1)
    row = half * 5 + (k % 4 if axis == 1 else 4)
    source = (
        parts.at[block, pl.ds(2 * half + s, 1)] if s < 2 else parts.at[block, pl.ds(2 * half, 2)]
    )
    place = (pl.ds(0, 1), pl.ds(1, 1), pl.ds(2, 2), pl.ds(4, 2))[s]
    at = row * 4 + s
    return pltpu.make_async_remote_copy(
        src_ref=source,
        dst_ref=landed.at[row, place],
        send_sem=send.at[at],
        recv_sem=recv.at[at],
        device_id={"exp": target},
        device_id_type=MESH,
    )


def add_lines(total, others, step):
    lines = total.shape[0]

    @pl.loop(0, lines // step)
    def _(i):
        at = pl.ds(pl.multiple_of(i * step, step), step)
        value = total[at].astype(jnp.float32)
        for other in others:
            value = value + other[at].astype(jnp.float32)
        total[at] = value.astype(total.dtype)


def reduce_exp_kernel(given, out, parts, landed, send, recv, local, done):
    greet_exp()
    lines = given.shape[2]
    step = 16
    load = pltpu.make_async_copy(given, parts, local)
    load.start()
    load.wait()
    copies = {
        (half, axis, k, s): reduce_exp_copy(parts, landed, send, recv, half, axis, k, s)
        for half in range(2)
        for axis, k in ((1, 0), (1, 1), (1, -1), (1, 2), (2, 0))
        for s in range(4)
    }

    def row_of(half, axis, k):
        return half * 5 + (k % 4 if axis == 1 else 4)

    def block_of(half, axis, k, dest):
        return exp_block(dest, k, half, 1) if axis == 1 else exp_block(0, dest, half, 1)

    def pass_on(half, axis, k):
        for s, dest in ((0, 1), (1, -1)):
            copies[half, axis, k, s].wait_recv()
            add_lines(
                parts.at[block_of(half, axis, k, dest), 2 * half + s],
                [landed.at[row_of(half, axis, k), s]],
                step,
            )
            copies[half, axis, k, s + 2].start()

    def finish(half, axis, k):
        copies[half, axis, k, 2].wait_recv()
        copies[half, axis, k, 3].wait_recv()
        for part in range(2):
            add_lines(
                parts.at[block_of(half, axis, k, 0), 2 * half + part],
                [
                    landed.at[row_of(half, axis, k), 2 + part],
                    landed.at[row_of(half, axis, k), 4 + part],
                ],
                step,
            )

    order = (2, 1, -1, 0)
    for k in order:
        for half in range(2):
            for s in (0, 1):
                copies[half, 1, k, s].start()
    for k in order:
        for half in range(2):
            pass_on(half, 1, k)
    for k in order:
        for half in range(2):
            finish(half, 1, k)
            if k == 2:
                copies[half, 2, 0, 0].start()
                copies[half, 2, 0, 1].start()
    for half in range(2):
        pass_on(half, 2, 0)
    for half in range(2):
        finish(half, 2, 0)
    store = pltpu.make_async_copy(parts.at[exp_block(0, 0, 0, 0)], out, done)
    store.start()
    for copy in copies.values():
        copy.wait_send()
    store.wait()


def reduce_exp(parts, collective_id):
    _, quarters, lines, width = parts.shape
    return pl.pallas_call(
        reduce_exp_kernel,
        out_shape=jax.ShapeDtypeStruct((quarters, lines, width), parts.dtype),
        in_specs=[pl.BlockSpec(memory_space=pl.ANY)],
        out_specs=pl.BlockSpec(memory_space=pl.ANY),
        scratch_shapes=[
            pltpu.VMEM(parts.shape, parts.dtype),
            pltpu.VMEM((10, 6, lines, width), parts.dtype),
            pltpu.SemaphoreType.DMA((40,)),
            pltpu.SemaphoreType.DMA((40,)),
            pltpu.SemaphoreType.DMA,
            pltpu.SemaphoreType.DMA,
        ],
        compiler_params=pltpu.CompilerParams(
            collective_id=collective_id, has_side_effects=True, vmem_limit_bytes=40 << 20
        ),
    )(parts)


def ctx_block(step, other):
    index = lax.axis_index("ctx")
    y, core = lax.div(index, 2), lax.rem(index, 2)
    if other:
        core = 1 - core
    return lax.rem(y + step + SIDE, SIDE) * 2 + core


def greet_ctx():
    barrier = pltpu.get_barrier_semaphore()
    for step, other in ((1, False), (-1, False), (0, True)):
        pl.semaphore_signal(
            barrier, inc=1, device_id={"ctx": ctx_block(step, other)}, device_id_type=MESH
        )
    pl.semaphore_wait(barrier, 3)


def gather_ctx_copies(own, out, send, recv):
    half = own.shape[0] // 2
    every, first, second = pl.ds(0, 2 * half), pl.ds(0, half), pl.ds(half, half)
    plan = (
        (0, every, 0, True),
        (0, every, 1, False),
        (0, every, -1, False),
        (-1, first, 1, False),
        (1, second, -1, False),
        (-1, every, 0, True),
        (1, every, 0, True),
        (2, first, 0, True),
        (2, second, 0, True),
    )
    copies = []
    for at, (origin, lines, step, other) in enumerate(plan):
        slot = out.at[ctx_block(origin, False), lines]
        copies.append(
            pltpu.make_async_remote_copy(
                src_ref=own.at[lines] if origin == 0 else slot,
                dst_ref=slot,
                send_sem=send.at[at],
                recv_sem=recv.at[at],
                device_id={"ctx": ctx_block(step, other)},
                device_id_type=MESH,
            )
        )
    return copies


def gather_ctx_kernel(own, out, send, recv, local):
    greet_ctx()
    copies = gather_ctx_copies(own, out, send, recv)
    for at in (1, 2, 0):
        copies[at].start()
    keep = pltpu.make_async_copy(own, out.at[ctx_block(0, False)], local)
    keep.start()
    for arrival, follow in ((1, (3, 5)), (2, (4, 6)), (3, (7,)), (4, (8,))):
        copies[arrival].wait_recv()
        for at in follow:
            copies[at].start()
    for at in (0, 5, 6, 7, 8):
        copies[at].wait_recv()
    for copy in copies:
        copy.wait_send()
    keep.wait()


def gather_ctx(block, collective_id):
    return pl.pallas_call(
        gather_ctx_kernel,
        out_shape=jax.ShapeDtypeStruct((8,) + block.shape, block.dtype),
        in_specs=[pl.BlockSpec(memory_space=pl.ANY)],
        out_specs=pl.BlockSpec(memory_space=pl.ANY),
        scratch_shapes=[
            pltpu.SemaphoreType.DMA((9,)),
            pltpu.SemaphoreType.DMA((9,)),
            pltpu.SemaphoreType.DMA,
        ],
        compiler_params=pltpu.CompilerParams(collective_id=collective_id, has_side_effects=True),
    )(block)


def reduce_ctx_kernel(given, out, parts, landed, near, send, recv, local, done):
    lines = given.shape[1]
    half = lines // 2
    greet_ctx()
    first, second, every = pl.ds(0, half), pl.ds(half, half), pl.ds(0, lines)

    def remote(src, dst, at, step, other):
        return pltpu.make_async_remote_copy(
            src_ref=src,
            dst_ref=dst,
            send_sem=send.at[at],
            recv_sem=recv.at[at],
            device_id={"ctx": ctx_block(step, other)},
            device_id_type=MESH,
        )

    swaps, loads = {}, {}
    for at, step in enumerate((2, 1, -1, 0)):
        swaps[step] = remote(given.at[ctx_block(step, True)], near.at[at], at, 0, True)
        swaps[step].start()
        loads[step] = pltpu.make_async_copy(
            given.at[ctx_block(step, False)], parts.at[at], local.at[at]
        )
        loads[step].start()
    hops = (
        remote(parts.at[0, first], landed.at[0, first], 4, 1, False),
        remote(parts.at[0, second], landed.at[0, second], 5, -1, False),
        remote(parts.at[1], landed.at[1], 6, 1, False),
        remote(parts.at[2], landed.at[2], 7, -1, False),
    )
    for at, step in enumerate((2, 1, -1, 0)):
        loads[step].wait()
        swaps[step].wait_recv()
        add_lines(parts.at[at], [near.at[at]], 16)
        if step == 2:
            hops[0].start()
            hops[1].start()
        if step == 1:
            hops[0].wait_recv()
            add_lines(parts.at[1, first], [landed.at[0, first]], 16)
            hops[2].start()
        if step == -1:
            hops[1].wait_recv()
            add_lines(parts.at[2, second], [landed.at[0, second]], 16)
            hops[3].start()
    hops[2].wait_recv()
    hops[3].wait_recv()
    add_lines(parts.at[3], [landed.at[1], landed.at[2]], 16)
    store = pltpu.make_async_copy(parts.at[3], out, done)
    store.start()
    for copy in (*swaps.values(), *hops):
        copy.wait_send()
    store.wait()


def reduce_ctx(parts, collective_id):
    _, lines, width = parts.shape
    return pl.pallas_call(
        reduce_ctx_kernel,
        out_shape=jax.ShapeDtypeStruct((lines, width), parts.dtype),
        in_specs=[pl.BlockSpec(memory_space=pl.ANY)],
        out_specs=pl.BlockSpec(memory_space=pl.ANY),
        scratch_shapes=[
            pltpu.VMEM((4, lines, width), parts.dtype),
            pltpu.VMEM((3, lines, width), parts.dtype),
            pltpu.VMEM((4, lines, width), parts.dtype),
            pltpu.SemaphoreType.DMA((8,)),
            pltpu.SemaphoreType.DMA((8,)),
            pltpu.SemaphoreType.DMA((4,)),
            pltpu.SemaphoreType.DMA,
        ],
        compiler_params=pltpu.CompilerParams(
            collective_id=collective_id, has_side_effects=True, vmem_limit_bytes=40 << 20
        ),
    )(parts)


def dot(a, b, dims=((1,), (0,))):
    return lax.dot_general(a, b, (dims, ((), ())), preferred_element_type=F32)


def vmem(shape=None, index=None):
    return pl.BlockSpec(memory_space=VMEM)


def whole(*shape):
    return pl.BlockSpec(shape, lambda *_: (0,) * len(shape), pipeline_mode=pl.Buffered(1))


def side_by_side(a):
    return jnp.concatenate([a[:64], a[64:]], axis=1)


def one_below(a):
    return jnp.concatenate([a[:, :64], a[:, 64:]], axis=0)


def attend_kernel(
    tokens, gain, weights, attn_in, q_t, q_s, k_s, k_t, v_s, v_t, lse, exact, mixed
):
    scale = gain[...]

    @pl.loop(0, 8)
    def _(i):
        at = pl.ds(pl.multiple_of(i * ROWS, ROWS), ROWS)
        x = tokens[at].astype(F32)
        x = x * lax.rsqrt(jnp.mean(x * x, axis=1, keepdims=True) + EPSILON) * scale
        x = x.astype(BF16)
        attn_in[at] = x
        qkv = dot(x, weights[...]).astype(BF16).astype(F32)
        q = qkv[:, :128] * 0.125
        k, v = qkv[:, 128:192], qkv[:, 192:]
        q_s[i] = one_below(q).astype(BF16)
        q_t[i] = side_by_side(q.T).astype(BF16)
        k_s[i] = k.astype(BF16)
        v_s[i] = v.astype(BF16)
        kv_t = qkv[:, 128:].T
        k_t[i] = kv_t[:64].astype(BF16)
        v_t[i] = kv_t[64:].astype(BF16)

    key_row = lax.broadcasted_iota(jnp.int32, (ROWS, 2 * ROWS), 0)
    query_row = lax.rem(lax.broadcasted_iota(jnp.int32, (ROWS, 2 * ROWS), 1), ROWS)
    seen = key_row <= query_row

    @pl.loop(0, 8)
    def _(i):
        query = q_t[i]

        def add_block(j, carry, diagonal):
            top, total, acc = carry
            scores = dot(k_s[j], query)
            if diagonal:
                scores = jnp.where(seen, scores, -1e30)
            new_top = jnp.maximum(top, jnp.max(scores, axis=0, keepdims=True))
            fade = jnp.exp(top - new_top)
            weights = jnp.exp(scores - new_top)
            total = total * fade + jnp.sum(weights, axis=0, keepdims=True)
            acc = acc * fade + dot(v_t[j], weights.astype(BF16))
            return new_top, total, acc

        carry = (
            jnp.full((1, 2 * ROWS), -1e30, F32),
            jnp.zeros((1, 2 * ROWS), F32),
            jnp.zeros((64, 2 * ROWS), F32),
        )
        carry = lax.fori_loop(0, i, lambda j, c: add_block(j, c, False), carry)
        top, total, acc = add_block(i, carry, True)
        lse[i] = top + jnp.log(total)
        value = acc / total
        exact[i] = value
        both = jnp.concatenate([value[:, :ROWS], value[:, ROWS:]], axis=0)
        at = pl.ds(pl.multiple_of(i * ROWS, ROWS), ROWS)
        mixed[at] = both.T.astype(BF16)


def attend(tokens, gain, weights):
    shapes = [
        ((2048, 1024), BF16),
        ((8, 64, 512), BF16),
        ((8, 512, 64), BF16),
        ((8, 256, 64), BF16),
        ((8, 64, 256), BF16),
        ((8, 256, 64), BF16),
        ((8, 64, 256), BF16),
        ((8, 1, 512), F32),
        ((8, 64, 512), F32),
        ((2048, 128), BF16),
    ]
    return pl.pallas_call(
        attend_kernel,
        out_shape=[jax.ShapeDtypeStruct(s, t) for s, t in shapes],
        in_specs=[vmem()] * 3,
        out_specs=[vmem()] * len(shapes),
        compiler_params=pltpu.CompilerParams(vmem_limit_bytes=50 << 20),
    )(tokens, gain, weights)


def attend_back_kernel(
    mixed_grad, q_t, q_s, k_s, k_t, v_s, lse, exact, d, out_s, out_t, delta, dq
):
    @pl.loop(0, 8)
    def _(i):
        at = pl.ds(pl.multiple_of(i * ROWS, ROWS), ROWS)
        g = mixed_grad[at].astype(F32)
        out_s[i] = one_below(g).astype(BF16)
        g = side_by_side(g.T)
        out_t[i] = g.astype(BF16)
        delta[i] = jnp.sum(g * exact[i], axis=0, keepdims=True)
        dq[i] = jnp.zeros_like(dq[i])

    key_row = lax.broadcasted_iota(jnp.int32, (ROWS, 2 * ROWS), 0)
    query_row = lax.rem(lax.broadcasted_iota(jnp.int32, (ROWS, 2 * ROWS), 1), ROWS)
    seen = key_row <= query_row

    @pl.loop(0, 8)
    def _(j):
        key, key_t, value = k_s[j], k_t[j], v_s[j]

        def add_block(i, carry, diagonal):
            dk, dv = carry
            probs = jnp.exp(dot(key, q_t[i]) - lse[i])
            if diagonal:
                probs = jnp.where(seen, probs, 0.0)
            grad = probs * (dot(value, out_t[i]) - delta[i])
            grad = grad.astype(BF16)
            dv = dv + dot(probs.astype(BF16), out_s[i])
            dk = dk + dot(grad, q_s[i])
            dq[i] += dot(key_t, grad)
            return dk, dv

        zero = jnp.zeros((ROWS, 64), F32)
        carry = add_block(j, (zero, zero), True)
        dk, dv = lax.fori_loop(j + 1, 8, lambda i, c: add_block(i, c, False), carry)
        at = pl.ds(pl.multiple_of(j * ROWS, ROWS), ROWS)
        d[at, 128:256] = jnp.concatenate([dk, dv], axis=1).astype(BF16)

    @pl.loop(0, 8)
    def _(i):
        at = pl.ds(pl.multiple_of(i * ROWS, ROWS), ROWS)
        g = dq[i] * 0.125
        g = jnp.concatenate([g[:, :ROWS], g[:, ROWS:]], axis=0)
        d[at, 0:128] = g.T.astype(BF16)


def attend_back(mixed_grad, q_t, q_s, k_s, k_t, v_s, lse, exact):
    return pl.pallas_call(
        attend_back_kernel,
        out_shape=jax.ShapeDtypeStruct((2048, 256), BF16),
        in_specs=[vmem()] * 8,
        out_specs=vmem(),
        scratch_shapes=[
            VMEM((8, 512, 64), BF16),
            VMEM((8, 64, 512), BF16),
            VMEM((8, 1, 512), F32),
            VMEM((8, 64, 512), F32),
        ],
        compiler_params=pltpu.CompilerParams(vmem_limit_bytes=50 << 20),
    )(mixed_grad, q_t, q_s, k_s, k_t, v_s, lse, exact)


def experts_kernel(
    owner, moe, cot, routes, misc, weights,
    out_parts, grad_parts, rows, slot_grads, hidden, gate_grads, up_grads,
):
    own = owner[0]
    router = misc[0:32].astype(BF16)
    listed = [routes[b].astype(jnp.int32) for b in range(GROUP)]
    listed = [jnp.concatenate([r[:8], r[8:]], axis=1) for r in listed]

    def matrix(kind, k):
        return weights[:, 2 * kind + k].reshape(1024, 512)

    expert = lax.broadcasted_iota(jnp.int32, (32, ROWS), 0)
    named = [[None, None] for _ in range(GROUP)]
    gates = [[None, None] for _ in range(GROUP)]
    for b in range(GROUP):
        logits = dot(router, moe[b], ((1,), (1,)))
        chosen = expert < 0
        for j in range(8):
            chosen = chosen | (listed[b][j : j + 1] == expert)
        logits = jnp.where(chosen, logits, -1e30)
        weight = jnp.where(chosen, jnp.exp(logits - jnp.max(logits, axis=0, keepdims=True)), 0.0)
        weight = weight / jnp.sum(weight, axis=0, keepdims=True)
        for k in range(2):
            mine = expert == 2 * own + k
            gates[b][k] = jnp.sum(jnp.where(mine, weight, 0.0), axis=0, keepdims=True)
            named[b][k] = jnp.sum(
                jnp.where(mine & chosen, 1.0, 0.0), axis=0, keepdims=True
            )
    before = lax.broadcasted_iota(jnp.int32, (ROWS, ROWS), 0) < lax.broadcasted_iota(
        jnp.int32, (ROWS, ROWS), 1
    )
    flat = jnp.concatenate([named[b][k] for b in range(GROUP) for k in range(2)], axis=0)
    place = dot(flat.astype(BF16), before.astype(BF16))
    slot = lax.broadcasted_iota(jnp.int32, (CAP, ROWS), 0).astype(F32)
    spread = [[None, None] for _ in range(GROUP)]
    slot_gates = [[None, None] for _ in range(GROUP)]
    for b in range(GROUP):
        for k in range(2):
            at = 2 * b + k
            hit = (slot == place[at : at + 1]) & (flat[at : at + 1] > 0.5)
            spread[b][k] = jnp.where(hit, 1.0, 0.0).astype(BF16)
            slot_gates[b][k] = jnp.sum(
                jnp.where(hit, gates[b][k], 0.0), axis=1, keepdims=True
            )
    pick = [jnp.concatenate(spread[b], axis=0) for b in range(GROUP)]
    cots = [None] * GROUP
    for b in range(GROUP):
        both = dot(pick[b], moe[b]).astype(BF16)
        rows[0, b] = both[:CAP]
        rows[1, b] = both[CAP:]
        cots[b] = dot(pick[b], cot[b])
        for k in range(2):
            slot_grads[k, b] = (slot_gates[b][k] * cots[b][k * CAP : (k + 1) * CAP]).astype(BF16)
    gated = [None, None]
    row_grads = [None, None]
    weight_grads = [None, None]
    for k in range(2):
        x = rows[k].reshape(GROUP * CAP, 1024)
        dy = slot_grads[k].reshape(GROUP * CAP, 1024)
        g = dot(x, matrix(0, k))
        u = dot(x, matrix(1, k))
        s = jax.nn.sigmoid(g)
        silu = g * s
        h = (silu * u).astype(BF16)
        hidden[k] = h.reshape(GROUP, CAP, 512)
        y = dot(h, matrix(2, k), ((1,), (1,))).astype(BF16).astype(F32)
        gate = jnp.concatenate([slot_gates[b][k] for b in range(GROUP)], axis=0)
        gated[k] = (gate * y).astype(BF16)
        upstream = jnp.concatenate(
            [cots[b][k * CAP : (k + 1) * CAP] for b in range(GROUP)], axis=0
        )
        weight_grads[k] = jnp.sum(upstream * y, axis=1, keepdims=True)
        dh = dot(dy, matrix(2, k))
        gg = (dh * u * s * (1.0 + g * (1.0 - s))).astype(BF16)
        ug = (dh * silu).astype(BF16)
        gate_grads[k] = gg.reshape(GROUP, CAP, 512)
        up_grads[k] = ug.reshape(GROUP, CAP, 512)
        row_grads[k] = (
            dot(gg, matrix(0, k), ((1,), (1,))) + dot(ug, matrix(1, k), ((1,), (1,)))
        ).astype(BF16)
    owner_row = lax.broadcasted_iota(jnp.int32, (16, ROWS), 0) == own
    for b in range(GROUP):
        at = slice(b * CAP, (b + 1) * CAP)
        for source, target in ((gated, out_parts), (row_grads, grad_parts)):
            both = jnp.concatenate([source[0][at], source[1][at]], axis=0)
            total = dot(pick[b], both, ((0,), (0,))).astype(BF16)
            for q in range(4):
                target[b, q, 0:ROWS] = total[:, q * 256 : (q + 1) * 256]
        for k in range(2):
            vector = jnp.sum(
                spread[b][k].astype(F32) * weight_grads[k][at], axis=0, keepdims=True
            )
            high = vector.astype(BF16)
            low = (vector - high.astype(F32)).astype(BF16)
            grad_parts[b, 2 * k, ROWS : ROWS + 16] = jnp.where(
                owner_row, high.astype(F32), 0.0
            ).astype(BF16)
            grad_parts[b, 2 * k + 1, ROWS : ROWS + 16] = jnp.where(
                owner_row, low.astype(F32), 0.0
            ).astype(BF16)


def experts(owner, moe, cot, routes, misc, weights):
    steps = 16 // GROUP

    def block(*shape, dim=0):
        def index(g, owner):
            return tuple(g if i == dim else 0 for i in range(len(shape)))

        return pl.BlockSpec(shape, index)

    outs = [
        ((16, 4, 256, 256), BF16),
        ((16, 4, 272, 256), BF16),
        ((2, 16, CAP, 1024), BF16),
        ((2, 16, CAP, 1024), BF16),
        ((2, 16, CAP, 512), BF16),
        ((2, 16, CAP, 512), BF16),
        ((2, 16, CAP, 512), BF16),
    ]
    return pl.pallas_call(
        experts_kernel,
        grid_spec=pltpu.PrefetchScalarGridSpec(
            num_scalar_prefetch=1,
            grid=(steps,),
            in_specs=[
                block(GROUP, 256, 1024),
                block(GROUP, 256, 1024),
                block(GROUP, 16, 128),
                whole(40, 1024),
                whole(8, 6, 128, 512),
            ],
            out_specs=[
                block(GROUP, 4, 256, 256),
                block(GROUP, 4, 272, 256),
                block(2, GROUP, CAP, 1024, dim=1),
                block(2, GROUP, CAP, 1024, dim=1),
                block(2, GROUP, CAP, 512, dim=1),
                block(2, GROUP, CAP, 512, dim=1),
                block(2, GROUP, CAP, 512, dim=1),
            ],
        ),
        out_shape=[jax.ShapeDtypeStruct(s, t) for s, t in outs],
        compiler_params=pltpu.CompilerParams(vmem_limit_bytes=58 << 20),
    )(owner, moe, cot, routes, misc, weights)

PEERS = ((2, False), (2, True), (1, False), (1, True), (-1, False), (-1, True), (0, True))


def greet(ctx_peers, exp_steps):
    barrier = pltpu.get_barrier_semaphore()
    for step, other in ctx_peers:
        pl.semaphore_signal(
            barrier, inc=1, device_id={"ctx": ctx_block(step, other)}, device_id_type=MESH
        )
    for first, second in exp_steps:
        pl.semaphore_signal(
            barrier, inc=1, device_id={"exp": exp_block(first, second, 0, 0)}, device_id_type=MESH
        )
    pl.semaphore_wait(barrier, len(ctx_peers) + len(exp_steps))


NEIGHBOURS = ((1, 0), (-1, 0), (0, 1), (0, -1))


def to_ctx(src, dst, send, recv, peer):
    return pltpu.make_async_remote_copy(
        src_ref=src,
        dst_ref=dst,
        send_sem=send,
        recv_sem=recv,
        device_id={"ctx": ctx_block(*peer)},
        device_id_type=MESH,
    )


def gather_exp_stages(own, out, send, recv):
    rows = own.shape[0]
    copies = {
        (half, axis, k, s): gather_exp_copy(own, out, send, recv, rows, half, axis, k, s)
        for half in range(2)
        for axis, k in ((1, 0), (2, 0), (2, 1), (2, -1), (2, 2))
        for s in range(4)
    }

    def begin():
        for axis in (1, 2):
            for s in (0, 1):
                for half in range(2):
                    copies[half, axis, 0, s].start()

    def first(s, k):
        for half in range(2):
            copies[half, 1, 0, s].wait_recv()
            copies[half, 1, 0, s + 2].start()
            copies[half, 2, k, 0].start()
            copies[half, 2, k, 1].start()

    def middle():
        for half in range(2):
            copies[half, 1, 0, 2].wait_recv()
            copies[half, 1, 0, 3].wait_recv()
            copies[half, 2, 2, 0].start()
            copies[half, 2, 2, 1].start()

    def forward(k):
        for s in (0, 1):
            for half in range(2):
                copies[half, 2, k, s].wait_recv()
                copies[half, 2, k, s + 2].start()

    def last():
        for k in (0, -1, 1, 2):
            for s in (2, 3):
                for half in range(2):
                    copies[half, 2, k, s].wait_recv()

    def sent():
        for copy in copies.values():
            copy.wait_send()

    steps = [
        begin,
        lambda: first(0, -1),
        lambda: first(1, 1),
        lambda: forward(0),
        middle,
        lambda: forward(-1),
        lambda: forward(1),
        lambda: forward(2),
        last,
    ]
    return steps, sent


def start_kernel(
    tokens, cot, w_gate, w_up, w_down, pieces, out_piece, routes,
    attn_in, q_t, q_s, k_s, k_t, v_s, lse, exact, mixed,
    head_w, misc_t, full_out, resid, moe_in, all_cot, all_routes, all_experts,
    land, own_experts, down_in, w_block, w_all, o_block, o_all, w_wide, o_wide, misc, v_t, mixed_land,
    exp_send, exp_recv, ctx_send, ctx_recv, ring_send, ring_recv, local,
):
    me = lax.axis_index("ctx")
    own = exp_block(0, 0, 0, 0)
    loads = [
        pltpu.make_async_copy(w_gate, own_experts.at[pl.ds(0, 2)], local.at[0]),
        pltpu.make_async_copy(w_up, own_experts.at[pl.ds(2, 2)], local.at[1]),
        pltpu.make_async_copy(w_down, down_in, local.at[2]),
        pltpu.make_async_copy(tokens, land.at[me], local.at[3]),
        pltpu.make_async_copy(pieces.at[me], w_block.at[pl.ds(me * 32, 32)], local.at[4]),
        pltpu.make_async_copy(routes, w_block.at[pl.ds(256, 64)], local.at[5]),
        pltpu.make_async_copy(out_piece, o_block.at[pl.ds(me * 64, 64)], local.at[6]),
        pltpu.make_async_copy(cot, all_cot.at[own], local.at[7]),
    ]
    for load in loads:
        load.start()
    greet(PEERS, NEIGHBOURS)
    piece_copies = [
        to_ctx(
            pieces.at[ctx_block(*peer)], w_block.at[pl.ds(me * 32, 32)],
            ctx_send.at[0, at], ctx_recv.at[0, at], peer,
        )
        for at, peer in enumerate(PEERS)
    ]
    out_copies = [
        to_ctx(
            out_piece, o_block.at[pl.ds(me * 64, 64)],
            ctx_send.at[1, at], ctx_recv.at[1, at], peer,
        )
        for at, peer in enumerate(PEERS)
    ]
    for copy in piece_copies + out_copies:
        copy.start()
    ring = gather_ctx_copies(tokens, land, ring_send.at[0], ring_recv.at[0])
    for at in (1, 2, 0):
        ring[at].start()
    w_steps, w_sent = gather_exp_stages(w_block, w_all, exp_send.at[0], exp_recv.at[0])
    o_steps, o_sent = gather_exp_stages(o_block, o_all, exp_send.at[1], exp_recv.at[1])
    c_steps, c_sent = gather_exp_stages(cot, all_cot, exp_send.at[2], exp_recv.at[2])
    for copy in piece_copies:
        copy.wait_recv()
    loads[4].wait()
    loads[5].wait()
    w_steps[0]()
    w_keep = pltpu.make_async_copy(w_block, w_all.at[own], local.at[8])
    w_keep.start()
    for copy in out_copies:
        copy.wait_recv()
    loads[6].wait()
    o_steps[0]()
    o_keep = pltpu.make_async_copy(o_block, o_all.at[own], local.at[9])
    o_keep.start()
    c_steps[0]()
    for at in (0, 1, 2):
        loads[at].wait()
    for k in range(2):
        own_experts[4 + k] = down_in[k].astype(F32).T.astype(BF16)
    for step in w_steps[1:]:
        step()
    w_keep.wait()
    ring[1].wait_recv()
    ring[3].start()
    ring[5].start()
    ring[2].wait_recv()
    ring[4].start()
    ring[6].start()

    @pl.loop(0, 128)
    def _(i):
        x, c = lax.div(i, 8), lax.rem(i, 8)
        at = pl.ds(pl.multiple_of(c * 128 + x * 8, 8), 8)
        line = pl.multiple_of(c * 32, 32)
        first = w_all[x, pl.ds(line, 16)].astype(F32)
        second = w_all[x, pl.ds(line + 16, 16)].astype(F32)
        w_wide[at, 0:128] = first[:8]
        w_wide[at, 128:256] = first[8:]
        misc[at] = second[:8]

    all_routes[...] = w_all[:, 256:272]
    head_w[...] = w_wide[...].astype(BF16)

    @pl.loop(0, 8)
    def _(c):
        at = pl.ds(pl.multiple_of(c * 128, 128), 128)
        misc_t[:, at] = misc[at].T[:40]

    def project(i):
        at = pl.ds(pl.multiple_of(i * ROWS, ROWS), ROWS)
        x = land[i].astype(F32)
        x = x * lax.rsqrt(jnp.mean(x * x, axis=1, keepdims=True) + EPSILON) * misc_t[33:34]
        x = x.astype(BF16)
        attn_in[at] = x
        qkv = dot(x, head_w[...]).astype(BF16).astype(F32)
        q = qkv[:, :128] * 0.125
        k, v = qkv[:, 128:192], qkv[:, 192:]
        q_s[i] = one_below(q).astype(BF16)
        q_t[i] = side_by_side(q.T).astype(BF16)
        k_s[i] = k.astype(BF16)
        v_s[i] = v.astype(BF16)
        kv_t = qkv[:, 128:].T
        k_t[i] = kv_t[:64].astype(BF16)
        v_t[i] = kv_t[64:].astype(BF16)

    o_steps[1]()
    o_steps[2]()
    loads[3].wait()
    project(ctx_block(0, False))
    ring[0].wait_recv()
    project(ctx_block(0, True))
    ring[3].wait_recv()
    ring[7].start()
    ring[4].wait_recv()
    ring[8].start()
    w_ring = gather_ctx_copies(own_experts, all_experts, ring_send.at[1], ring_recv.at[1])
    for at in (1, 2, 0):
        w_ring[at].start()
    w_ring_keep = pltpu.make_async_copy(own_experts, all_experts.at[me], local.at[10])
    w_ring_keep.start()
    o_steps[3]()
    o_steps[4]()
    c_steps[1]()
    c_steps[2]()
    project(ctx_block(-1, False))
    project(ctx_block(1, False))
    ring[5].wait_recv()
    project(ctx_block(-1, True))
    ring[6].wait_recv()
    project(ctx_block(1, True))
    project(ctx_block(2, False))
    ring[7].wait_recv()
    ring[8].wait_recv()
    project(ctx_block(2, True))

    key_row = lax.broadcasted_iota(jnp.int32, (ROWS, 2 * ROWS), 0)
    query_row = lax.rem(lax.broadcasted_iota(jnp.int32, (ROWS, 2 * ROWS), 1), ROWS)
    seen = key_row <= query_row

    def tile(i):
        query = q_t[i]

        def add_block(j, carry, diagonal):
            top, total, acc = carry
            scores = dot(k_s[j], query)
            if diagonal:
                scores = jnp.where(seen, scores, -1e30)
            new_top = jnp.maximum(top, jnp.max(scores, axis=0, keepdims=True))
            fade = jnp.exp(top - new_top)
            weights = jnp.exp(scores - new_top)
            total = total * fade + jnp.sum(weights, axis=0, keepdims=True)
            acc = acc * fade + dot(v_t[j], weights.astype(BF16))
            return new_top, total, acc

        carry = (
            jnp.full((1, 2 * ROWS), -1e30, F32),
            jnp.zeros((1, 2 * ROWS), F32),
            jnp.zeros((64, 2 * ROWS), F32),
        )
        carry = lax.fori_loop(0, i, lambda j, c: add_block(j, c, False), carry)
        top, total, acc = add_block(i, carry, True)
        lse[i] = top + jnp.log(total)
        value = acc / total
        exact[i] = value
        both = jnp.concatenate([value[:, :ROWS], value[:, ROWS:]], axis=0)
        mixed[i] = both.T.astype(BF16)

    def unpack_out():
        o_keep.wait()

        @pl.loop(0, 128)
        def _(i):
            x, c = lax.div(i, 8), lax.rem(i, 8)
            at = pl.ds(pl.multiple_of(c * 128 + x * 8, 8), 8)
            for t in range(4):
                line = pl.multiple_of(c * 64 + t * 16, 16)
                both = o_all[x, pl.ds(line, 16)].astype(F32)
                o_wide[at, 256 * t : 256 * t + 128] = both[:8]
                o_wide[at, 256 * t + 128 : 256 * t + 256] = both[8:]

        full_out[...] = o_wide[...].astype(BF16)

    def ring_first():
        w_ring[1].wait_recv()
        w_ring[3].start()
        w_ring[5].start()
        w_ring[2].wait_recv()
        w_ring[4].start()
        w_ring[6].start()

    def ring_second():
        w_ring[3].wait_recv()
        w_ring[7].start()
        w_ring[4].wait_recv()
        w_ring[8].start()

    between = (
        (o_steps[5], o_steps[6]),
        (o_steps[7], c_steps[3]),
        (c_steps[4], ring_first),
        (c_steps[5], o_steps[8]),
        (unpack_out,),
        (c_steps[6],),
        (c_steps[7], ring_second),
    )
    mixed_copies = []
    for at, peer in enumerate(PEERS):
        i = ctx_block(*peer)
        tile(i)
        copy = to_ctx(
            mixed.at[i], mixed_land.at[me], ctx_send.at[2, at], ctx_recv.at[2, at], peer
        )
        copy.start()
        mixed_copies.append(copy)
        for step in between[at]:
            step()
    tile(me)
    mixed_land[me] = mixed[me]
    total = tokens[...].astype(F32)
    for copy in mixed_copies:
        copy.wait_recv()
    for c in range(4):
        pair = jnp.concatenate([mixed_land[2 * c], mixed_land[2 * c + 1]], axis=1)
        total = total + dot(pair, full_out[c * 256 : (c + 1) * 256])
    resid[...] = total
    scaled = total * lax.rsqrt(jnp.mean(total * total, axis=1, keepdims=True) + EPSILON)
    moe_in[...] = (scaled * misc_t[32:33]).astype(BF16)
    c_steps[8]()
    for at in (0, 5, 6, 7, 8):
        w_ring[at].wait_recv()
    w_ring_keep.wait()
    loads[7].wait()
    w_sent()
    o_sent()
    c_sent()
    for copy in (*piece_copies, *out_copies, *ring, *w_ring, *mixed_copies):
        copy.wait_send()


def start(tokens, cot, w_gate, w_up, w_down, pieces, out_piece, routes, collective_id):
    anywhere = pl.BlockSpec(memory_space=pl.ANY)
    outs = [
        ((2048, 1024), BF16, vmem()),
        ((8, 64, 512), BF16, vmem()),
        ((8, 512, 64), BF16, vmem()),
        ((8, 256, 64), BF16, vmem()),
        ((8, 64, 256), BF16, vmem()),
        ((8, 256, 64), BF16, vmem()),
        ((8, 1, 512), F32, vmem()),
        ((8, 64, 512), F32, vmem()),
        ((8, 256, 128), BF16, vmem()),
        ((1024, 256), BF16, vmem()),
        ((40, 1024), F32, vmem()),
        ((1024, 1024), BF16, vmem()),
        ((256, 1024), F32, vmem()),
        ((256, 1024), BF16, vmem()),
        ((16, 256, 1024), BF16, anywhere),
        ((16, 16, 128), BF16, vmem()),
        ((8, 6, 128, 512), BF16, anywhere),
    ]
    dma = pltpu.SemaphoreType.DMA
    return pl.pallas_call(
        start_kernel,
        out_shape=[jax.ShapeDtypeStruct(s, t) for s, t, _ in outs],
        in_specs=[vmem(), anywhere, anywhere, anywhere, anywhere, vmem(), vmem(), vmem()],
        out_specs=[spec for _, _, spec in outs],
        scratch_shapes=[
            VMEM((8, 256, 1024), BF16),
            VMEM((6, 128, 512), BF16),
            VMEM((2, 512, 128), BF16),
            VMEM((320, 128), BF16),
            VMEM((16, 320, 128), BF16),
            VMEM((512, 128), BF16),
            VMEM((16, 512, 128), BF16),
            VMEM((1024, 256), F32),
            VMEM((1024, 1024), F32),
            VMEM((1024, 128), F32),
            VMEM((8, 64, 256), BF16),
            VMEM((8, 256, 128), BF16),
            dma((3, 40)),
            dma((3, 40)),
            dma((3, 7)),
            dma((3, 7)),
            dma((2, 9)),
            dma((2, 9)),
            dma((11,)),
        ],
        compiler_params=pltpu.CompilerParams(
            collective_id=collective_id, has_side_effects=True, vmem_limit_bytes=56 << 20
        ),
    )(tokens, cot, w_gate, w_up, w_down, pieces, out_piece, routes)


def rms_scale(values, gain):
    return values * lax.rsqrt(jnp.mean(values * values, axis=-1, keepdims=True) + EPSILON) * gain


def per_device(
    tokens,
    norm_attn,
    w_query,
    w_key,
    w_value,
    w_out,
    norm_moe,
    w_router,
    w_gate,
    w_up,
    w_down,
    routes,
    cotangent,
):
    exp = lax.axis_index("exp")
    by_head = jnp.concatenate(
        [w_query.reshape(8, 8, 128), w_key.reshape(8, 8, 64), w_value.reshape(8, 8, 64)], axis=2
    ).transpose(1, 0, 2)
    narrow = jnp.concatenate([w_router, norm_moe[:, None], norm_attn[:, None]], axis=1)
    narrow = jnp.broadcast_to(jnp.pad(narrow, ((0, 0), (0, 94))), (8, 8, 128))
    pieces = jnp.concatenate(
        [by_head[:, :, :128], by_head[:, :, 128:], narrow, jnp.zeros_like(narrow)], axis=1
    )
    out_piece = w_out.reshape(8, 8, 128).transpose(1, 0, 2).reshape(64, 128)
    route_rows = routes[0].T.reshape(8, 2, 128).transpose(1, 0, 2).reshape(16, 128)
    route_rows = jnp.pad(route_rows.astype(BF16), ((0, 48), (0, 0)))
    (
        attn_in, q_t, q_s, k_s, k_t, v_s, lse, exact, mixed,
        head_weights, misc_t, full_out, resid, moe_in, all_cot, all_routes, all_experts,
    ) = start(
        tokens[0], cotangent[0], w_gate, w_up, w_down, pieces, out_piece, route_rows, 1
    )
    mixed = mixed.reshape(2048, 128)
    token_rows = tokens[0].astype(F32)
    full_router = misc_t[:32].T
    gain_attn, gain_moe = misc_t[33:34], misc_t[32]
    all_moe = gather_exp(moe_in, 3)
    out_parts, grad_parts, rows, slot_grads, hidden, gate_grads, up_grads = experts(
        exp.reshape(1).astype(jnp.int32), all_moe, all_cot, all_routes, misc_t, all_experts
    )
    grad_total = reduce_exp(grad_parts, 4)
    expert_out = lax.psum_scatter(
        out_parts.reshape(-1, 256), "exp", scatter_dimension=0, tiled=True
    )
    expert_out = expert_out.reshape(4, 256, 256).transpose(1, 0, 2).reshape(256, 1024)
    output = (resid + expert_out.astype(F32)).astype(BF16)[None]

    flat = (2, 16 * CAP, -1)
    rows, slot_grads = rows.reshape(flat), slot_grads.reshape(flat)
    hidden, gate_grads, up_grads = (a.reshape(flat) for a in (hidden, gate_grads, up_grads))

    def expert_term(left, right):
        term = jnp.einsum("erd,erf->edf", left, right, preferred_element_type=F32).astype(BF16)
        return term.reshape(2, 8, 128, 512).transpose(1, 0, 2, 3)

    expert_terms = jnp.stack(
        [
            expert_term(rows, gate_grads),
            expert_term(rows, up_grads),
            expert_term(slot_grads, hidden),
        ],
        axis=1,
    ).reshape(8 * 768, 512)
    expert_sum = (
        lax.psum_scatter(expert_terms, "ctx", scatter_dimension=0, tiled=True)
        .astype(F32)
        .reshape(3, 2, 128, 512)
    )

    logits = jnp.dot(moe_in, full_router.astype(BF16), preferred_element_type=F32)
    chosen = jnp.any(
        routes[0][:, :, None] == jnp.arange(32, dtype=jnp.int32)[None, None, :], axis=1
    )
    gates = jax.nn.softmax(jnp.where(chosen, logits, -1e30), axis=-1)
    weight_grad = (
        grad_total[:, ROWS:].astype(F32).reshape(2, 2, 16, 256).sum(axis=1)
    )
    weight_grad = weight_grad.transpose(2, 1, 0).reshape(256, 32)
    logit_grad = jnp.where(
        chosen,
        gates * (weight_grad - jnp.sum(gates * weight_grad, axis=-1, keepdims=True)),
        0.0,
    )
    router_term = jnp.dot(moe_in.astype(F32).T, logit_grad, precision=PRECISE)
    moe_in_grad = grad_total[:, :ROWS].astype(F32).transpose(1, 0, 2).reshape(256, 1024)
    moe_in_grad = moe_in_grad + jnp.dot(
        logit_grad, misc_t[:32], precision=PRECISE
    )
    unused_moe, pull_moe = jax.vjp(rms_scale, resid, gain_moe)
    resid_grad, norm_moe_term = pull_moe(moe_in_grad)
    resid_grad = resid_grad + cotangent[0].astype(F32)
    attn_grad = resid_grad.astype(BF16)
    mixed_grad = jnp.einsum(
        "td,qd->tq", attn_grad, full_out, preferred_element_type=F32
    ).astype(BF16)
    mixed_grad = lax.all_to_all(
        mixed_grad.reshape(256, 8, 128).transpose(1, 0, 2),
        "ctx",
        split_axis=0,
        concat_axis=0,
        tiled=True,
    ).reshape(2048, 128)
    all_attn_grad = gather_ctx(attn_grad, 5).reshape(2048, 1024)
    out_term = jnp.einsum("tq,td->qd", mixed, all_attn_grad, preferred_element_type=F32)
    head_grads = attend_back(mixed_grad, q_t, q_s, k_s, k_t, v_s, lse, exact)
    head_term = jnp.einsum("td,tq->dq", attn_in, head_grads, preferred_element_type=F32)
    attn_in_parts = jnp.einsum(
        "tq,dq->td", head_grads, head_weights, preferred_element_type=F32
    ).astype(BF16)
    attn_in_grad = reduce_ctx(attn_in_parts.reshape(8, 256, 1024), 6).astype(F32)

    small_term = jnp.concatenate([router_term, norm_moe_term[:, None]], axis=1)

    def by_exp(term):
        return term.reshape(-1, 16, 8, term.shape[1]).transpose(1, 0, 2, 3).reshape(16, -1)

    sums = jnp.concatenate([by_exp(head_term), by_exp(out_term), by_exp(small_term)], axis=1)
    sums = jnp.pad(sums.astype(BF16), ((0, 0), (0, 32768 - sums.shape[1])))
    sums = reduce_exp(sums.reshape(16, 4, 32, 256), 7).reshape(-1).astype(F32)
    out_sum = sums[16384:24576].reshape(8, 1024)
    spread = jnp.concatenate(
        [sums[:16384].reshape(8, 8, 256), sums[24576:26688].reshape(8, 8, 33)], axis=2
    )
    spread = lax.all_to_all(spread, "ctx", split_axis=0, concat_axis=0, tiled=True)
    small_sum = jnp.sum(spread[:, :, 256:], axis=0)
    query_sum = spread[:, :, :128].transpose(1, 0, 2).reshape(8, 1024)
    key_sum = spread[:, :, 128:192].transpose(1, 0, 2).reshape(8, 512)
    value_sum = spread[:, :, 192:256].transpose(1, 0, 2).reshape(8, 512)
    norm_attn_sum = (
        jnp.sum(query_sum * w_query.astype(F32), axis=1)
        + jnp.sum(key_sum * w_key.astype(F32), axis=1)
        + jnp.sum(value_sum * w_value.astype(F32), axis=1)
    ) / norm_attn.astype(F32)
    unused_attn, pull_attn = jax.vjp(lambda v: rms_scale(v, gain_attn), token_rows)
    (token_grad,) = pull_attn(attn_in_grad)
    token_grad = (token_grad + resid_grad).astype(BF16)[None]
    return (
        output,
        token_grad,
        norm_attn_sum,
        query_sum,
        key_sum,
        value_sum,
        out_sum,
        small_sum[:, 32],
        small_sum[:, :32],
        expert_sum[0],
        expert_sum[1],
        expert_sum[2].transpose(0, 2, 1),
    )


def solution(mesh):
    in_specs = (
        P("exp", "ctx", None),
        P(("ctx", "exp")),
        P(("ctx", "exp"), None),
        P(("ctx", "exp"), None),
        P(("ctx", "exp"), None),
        P(("ctx", "exp"), None),
        P(("ctx", "exp")),
        P(("ctx", "exp"), None),
        P("exp", "ctx", None),
        P("exp", "ctx", None),
        P("exp", None, "ctx"),
        P("exp", "ctx", None),
        P("exp", "ctx", None),
    )
    out_specs = (
        P("exp", "ctx", None),
        P("exp", "ctx", None),
        P(("ctx", "exp")),
        P(("ctx", "exp"), None),
        P(("ctx", "exp"), None),
        P(("ctx", "exp"), None),
        P(("ctx", "exp"), None),
        P(("ctx", "exp")),
        P(("ctx", "exp"), None),
        P("exp", "ctx", None),
        P("exp", "ctx", None),
        P("exp", None, "ctx"),
    )
    return jax.shard_map(
        per_device, mesh=mesh, in_specs=in_specs, out_specs=out_specs, check_vma=False
    )
```

```python
import jax
import jax.numpy as jnp
from jax import lax
from jax.experimental import pallas as pl
from jax.experimental.pallas import tpu as pltpu
from jax.sharding import PartitionSpec as P

EPSILON = 1e-06
PRECISE = lax.Precision.HIGHEST
F32, BF16 = jnp.float32, jnp.bfloat16
VMEM = pltpu.VMEM
MESH = pl.DeviceIdType.MESH
SIDE = 4
ROWS = 256
CAP = 96
GROUP = 4


def exp_block(first, second, half, inner):
    index = lax.axis_index("exp")
    z, x = lax.div(index, SIDE), lax.rem(index, SIDE)
    by_x, by_z = (first, second) if half == inner else (second, first)
    return lax.rem(z + by_z + SIDE, SIDE) * SIDE + lax.rem(x + by_x + SIDE, SIDE)


def greet_exp():
    barrier = pltpu.get_barrier_semaphore()
    for half in range(2):
        for step in (1, -1):
            pl.semaphore_signal(
                barrier, inc=1, device_id={"exp": exp_block(step, 0, half, 0)}, device_id_type=MESH
            )
    pl.semaphore_wait(barrier, 4)


def gather_exp_copy(own, out, send, recv, rows, half, axis, k, s):
    part = rows // 4
    step = (1, -1, 1, -1)[s]
    off = (0, 0, -1, 1)[s]
    origin = exp_block(off, 0, half, 0) if axis == 1 else exp_block(k, off, half, 0)
    target = exp_block(step, 0, half, 0) if axis == 1 else exp_block(0, step, half, 0)
    lines = (
        pl.ds(half * 2 * part, 2 * part)
        if s < 2
        else pl.ds((half * 2 + s - 2) * part, part)
    )
    mine = s < 2 and (axis == 1 or k == 0)
    at = half * 20 + (s if axis == 1 else 4 + 4 * (k % 4) + s)
    return pltpu.make_async_remote_copy(
        src_ref=own.at[lines] if mine else out.at[origin, lines],
        dst_ref=out.at[origin, lines],
        send_sem=send.at[at],
        recv_sem=recv.at[at],
        device_id={"exp": target},
        device_id_type=MESH,
    )


def gather_exp_kernel(own, out, send, recv, local):
    rows = own.shape[0]
    greet_exp()
    copies = {
        (half, axis, k, s): gather_exp_copy(own, out, send, recv, rows, half, axis, k, s)
        for half in range(2)
        for axis, k in ((1, 0), (2, 0), (2, 1), (2, -1), (2, 2))
        for s in range(4)
    }
    keep = pltpu.make_async_copy(own, out.at[exp_block(0, 0, 0, 0)], local)
    keep.start()
    for axis in (1, 2):
        for s in (0, 1):
            for half in range(2):
                copies[half, axis, 0, s].start()
    for s, k in ((0, -1), (1, 1)):
        for half in range(2):
            copies[half, 1, 0, s].wait_recv()
            copies[half, 1, 0, s + 2].start()
            copies[half, 2, k, 0].start()
            copies[half, 2, k, 1].start()
    for s in (0, 1):
        for half in range(2):
            copies[half, 2, 0, s].wait_recv()
            copies[half, 2, 0, s + 2].start()
    for half in range(2):
        copies[half, 1, 0, 2].wait_recv()
        copies[half, 1, 0, 3].wait_recv()
        copies[half, 2, 2, 0].start()
        copies[half, 2, 2, 1].start()
    for k in (-1, 1, 2):
        for s in (0, 1):
            for half in range(2):
                copies[half, 2, k, s].wait_recv()
                copies[half, 2, k, s + 2].start()
    for k in (0, -1, 1, 2):
        for s in (2, 3):
            for half in range(2):
                copies[half, 2, k, s].wait_recv()
    for copy in copies.values():
        copy.wait_send()
    keep.wait()


def gather_exp(block, collective_id):
    rows, width = block.shape
    return pl.pallas_call(
        gather_exp_kernel,
        out_shape=jax.ShapeDtypeStruct((16, rows, width), block.dtype),
        in_specs=[pl.BlockSpec(memory_space=pl.ANY)],
        out_specs=pl.BlockSpec(memory_space=pl.ANY),
        scratch_shapes=[
            pltpu.SemaphoreType.DMA((40,)),
            pltpu.SemaphoreType.DMA((40,)),
            pltpu.SemaphoreType.DMA,
        ],
        compiler_params=pltpu.CompilerParams(collective_id=collective_id, has_side_effects=True),
    )(block)


def reduce_exp_copy(parts, landed, send, recv, half, axis, k, s):
    step = (1, -1, 1, -1)[s]
    dest = (2, 2, 1, -1)[s]
    block = exp_block(dest, k, half, 1) if axis == 1 else exp_block(0, dest, half, 1)
    target = exp_block(step, 0, half, 1) if axis == 1 else exp_block(0, step, half, 1)
    row = half * 5 + (k % 4 if axis == 1 else 4)
    source = (
        parts.at[block, pl.ds(2 * half + s, 1)] if s < 2 else parts.at[block, pl.ds(2 * half, 2)]
    )
    place = (pl.ds(0, 1), pl.ds(1, 1), pl.ds(2, 2), pl.ds(4, 2))[s]
    at = row * 4 + s
    return pltpu.make_async_remote_copy(
        src_ref=source,
        dst_ref=landed.at[row, place],
        send_sem=send.at[at],
        recv_sem=recv.at[at],
        device_id={"exp": target},
        device_id_type=MESH,
    )


def add_lines(total, others, step):
    lines = total.shape[0]

    @pl.loop(0, lines // step)
    def _(i):
        at = pl.ds(pl.multiple_of(i * step, step), step)
        value = total[at].astype(jnp.float32)
        for other in others:
            value = value + other[at].astype(jnp.float32)
        total[at] = value.astype(total.dtype)


def reduce_exp_kernel(given, out, parts, landed, send, recv, local, done):
    greet_exp()
    lines = given.shape[2]
    step = 16
    load = pltpu.make_async_copy(given, parts, local)
    load.start()
    load.wait()
    copies = {
        (half, axis, k, s): reduce_exp_copy(parts, landed, send, recv, half, axis, k, s)
        for half in range(2)
        for axis, k in ((1, 0), (1, 1), (1, -1), (1, 2), (2, 0))
        for s in range(4)
    }

    def row_of(half, axis, k):
        return half * 5 + (k % 4 if axis == 1 else 4)

    def block_of(half, axis, k, dest):
        return exp_block(dest, k, half, 1) if axis == 1 else exp_block(0, dest, half, 1)

    def pass_on(half, axis, k):
        for s, dest in ((0, 1), (1, -1)):
            copies[half, axis, k, s].wait_recv()
            add_lines(
                parts.at[block_of(half, axis, k, dest), 2 * half + s],
                [landed.at[row_of(half, axis, k), s]],
                step,
            )
            copies[half, axis, k, s + 2].start()

    def finish(half, axis, k):
        copies[half, axis, k, 2].wait_recv()
        copies[half, axis, k, 3].wait_recv()
        for part in range(2):
            add_lines(
                parts.at[block_of(half, axis, k, 0), 2 * half + part],
                [
                    landed.at[row_of(half, axis, k), 2 + part],
                    landed.at[row_of(half, axis, k), 4 + part],
                ],
                step,
            )

    order = (2, 1, -1, 0)
    for k in order:
        for half in range(2):
            for s in (0, 1):
                copies[half, 1, k, s].start()
    for k in order:
        for half in range(2):
            pass_on(half, 1, k)
    for k in order:
        for half in range(2):
            finish(half, 1, k)
            if k == 2:
                copies[half, 2, 0, 0].start()
                copies[half, 2, 0, 1].start()
    for half in range(2):
        pass_on(half, 2, 0)
    for half in range(2):
        finish(half, 2, 0)
    store = pltpu.make_async_copy(parts.at[exp_block(0, 0, 0, 0)], out, done)
    store.start()
    for copy in copies.values():
        copy.wait_send()
    store.wait()


def reduce_exp(parts, collective_id):
    _, quarters, lines, width = parts.shape
    return pl.pallas_call(
        reduce_exp_kernel,
        out_shape=jax.ShapeDtypeStruct((quarters, lines, width), parts.dtype),
        in_specs=[pl.BlockSpec(memory_space=pl.ANY)],
        out_specs=pl.BlockSpec(memory_space=pl.ANY),
        scratch_shapes=[
            pltpu.VMEM(parts.shape, parts.dtype),
            pltpu.VMEM((10, 6, lines, width), parts.dtype),
            pltpu.SemaphoreType.DMA((40,)),
            pltpu.SemaphoreType.DMA((40,)),
            pltpu.SemaphoreType.DMA,
            pltpu.SemaphoreType.DMA,
        ],
        compiler_params=pltpu.CompilerParams(
            collective_id=collective_id, has_side_effects=True, vmem_limit_bytes=40 << 20
        ),
    )(parts)


def ctx_block(step, other):
    index = lax.axis_index("ctx")
    y, core = lax.div(index, 2), lax.rem(index, 2)
    if other:
        core = 1 - core
    return lax.rem(y + step + SIDE, SIDE) * 2 + core


def greet_ctx():
    barrier = pltpu.get_barrier_semaphore()
    for step, other in ((1, False), (-1, False), (0, True)):
        pl.semaphore_signal(
            barrier, inc=1, device_id={"ctx": ctx_block(step, other)}, device_id_type=MESH
        )
    pl.semaphore_wait(barrier, 3)


def gather_ctx_copies(own, out, send, recv):
    half = own.shape[0] // 2
    every, first, second = pl.ds(0, 2 * half), pl.ds(0, half), pl.ds(half, half)
    plan = (
        (0, every, 0, True),
        (0, every, 1, False),
        (0, every, -1, False),
        (-1, first, 1, False),
        (1, second, -1, False),
        (-1, every, 0, True),
        (1, every, 0, True),
        (2, first, 0, True),
        (2, second, 0, True),
    )
    copies = []
    for at, (origin, lines, step, other) in enumerate(plan):
        slot = out.at[ctx_block(origin, False), lines]
        copies.append(
            pltpu.make_async_remote_copy(
                src_ref=own.at[lines] if origin == 0 else slot,
                dst_ref=slot,
                send_sem=send.at[at],
                recv_sem=recv.at[at],
                device_id={"ctx": ctx_block(step, other)},
                device_id_type=MESH,
            )
        )
    return copies


def gather_ctx_kernel(own, out, send, recv, local):
    greet_ctx()
    copies = gather_ctx_copies(own, out, send, recv)
    for at in (1, 2, 0):
        copies[at].start()
    keep = pltpu.make_async_copy(own, out.at[ctx_block(0, False)], local)
    keep.start()
    for arrival, follow in ((1, (3, 5)), (2, (4, 6)), (3, (7,)), (4, (8,))):
        copies[arrival].wait_recv()
        for at in follow:
            copies[at].start()
    for at in (0, 5, 6, 7, 8):
        copies[at].wait_recv()
    for copy in copies:
        copy.wait_send()
    keep.wait()


def gather_ctx(block, collective_id):
    return pl.pallas_call(
        gather_ctx_kernel,
        out_shape=jax.ShapeDtypeStruct((8,) + block.shape, block.dtype),
        in_specs=[pl.BlockSpec(memory_space=pl.ANY)],
        out_specs=pl.BlockSpec(memory_space=pl.ANY),
        scratch_shapes=[
            pltpu.SemaphoreType.DMA((9,)),
            pltpu.SemaphoreType.DMA((9,)),
            pltpu.SemaphoreType.DMA,
        ],
        compiler_params=pltpu.CompilerParams(collective_id=collective_id, has_side_effects=True),
    )(block)


def reduce_ctx_kernel(given, out, parts, landed, near, send, recv, local, done):
    lines = given.shape[1]
    half = lines // 2
    greet_ctx()
    first, second, every = pl.ds(0, half), pl.ds(half, half), pl.ds(0, lines)

    def remote(src, dst, at, step, other):
        return pltpu.make_async_remote_copy(
            src_ref=src,
            dst_ref=dst,
            send_sem=send.at[at],
            recv_sem=recv.at[at],
            device_id={"ctx": ctx_block(step, other)},
            device_id_type=MESH,
        )

    swaps, loads = {}, {}
    for at, step in enumerate((2, 1, -1, 0)):
        swaps[step] = remote(given.at[ctx_block(step, True)], near.at[at], at, 0, True)
        swaps[step].start()
        loads[step] = pltpu.make_async_copy(
            given.at[ctx_block(step, False)], parts.at[at], local.at[at]
        )
        loads[step].start()
    hops = (
        remote(parts.at[0, first], landed.at[0, first], 4, 1, False),
        remote(parts.at[0, second], landed.at[0, second], 5, -1, False),
        remote(parts.at[1], landed.at[1], 6, 1, False),
        remote(parts.at[2], landed.at[2], 7, -1, False),
    )
    for at, step in enumerate((2, 1, -1, 0)):
        loads[step].wait()
        swaps[step].wait_recv()
        add_lines(parts.at[at], [near.at[at]], 16)
        if step == 2:
            hops[0].start()
            hops[1].start()
        if step == 1:
            hops[0].wait_recv()
            add_lines(parts.at[1, first], [landed.at[0, first]], 16)
            hops[2].start()
        if step == -1:
            hops[1].wait_recv()
            add_lines(parts.at[2, second], [landed.at[0, second]], 16)
            hops[3].start()
    hops[2].wait_recv()
    hops[3].wait_recv()
    add_lines(parts.at[3], [landed.at[1], landed.at[2]], 16)
    store = pltpu.make_async_copy(parts.at[3], out, done)
    store.start()
    for copy in (*swaps.values(), *hops):
        copy.wait_send()
    store.wait()


def reduce_ctx(parts, collective_id):
    _, lines, width = parts.shape
    return pl.pallas_call(
        reduce_ctx_kernel,
        out_shape=jax.ShapeDtypeStruct((lines, width), parts.dtype),
        in_specs=[pl.BlockSpec(memory_space=pl.ANY)],
        out_specs=pl.BlockSpec(memory_space=pl.ANY),
        scratch_shapes=[
            pltpu.VMEM((4, lines, width), parts.dtype),
            pltpu.VMEM((3, lines, width), parts.dtype),
            pltpu.VMEM((4, lines, width), parts.dtype),
            pltpu.SemaphoreType.DMA((8,)),
            pltpu.SemaphoreType.DMA((8,)),
            pltpu.SemaphoreType.DMA((4,)),
            pltpu.SemaphoreType.DMA,
        ],
        compiler_params=pltpu.CompilerParams(
            collective_id=collective_id, has_side_effects=True, vmem_limit_bytes=40 << 20
        ),
    )(parts)


def dot(a, b, dims=((1,), (0,))):
    return lax.dot_general(a, b, (dims, ((), ())), preferred_element_type=F32)


def vmem(shape=None, index=None):
    return pl.BlockSpec(memory_space=VMEM)


def whole(*shape):
    return pl.BlockSpec(shape, lambda *_: (0,) * len(shape), pipeline_mode=pl.Buffered(1))


def side_by_side(a):
    return jnp.concatenate([a[:64], a[64:]], axis=1)


def one_below(a):
    return jnp.concatenate([a[:, :64], a[:, 64:]], axis=0)


def attend_kernel(
    tokens, gain, weights, attn_in, q_t, q_s, k_s, k_t, v_s, v_t, lse, exact, mixed
):
    scale = gain[...]

    @pl.loop(0, 8)
    def _(i):
        at = pl.ds(pl.multiple_of(i * ROWS, ROWS), ROWS)
        x = tokens[at].astype(F32)
        x = x * lax.rsqrt(jnp.mean(x * x, axis=1, keepdims=True) + EPSILON) * scale
        x = x.astype(BF16)
        attn_in[at] = x
        qkv = dot(x, weights[...]).astype(BF16).astype(F32)
        q = qkv[:, :128] * 0.125
        k, v = qkv[:, 128:192], qkv[:, 192:]
        q_s[i] = one_below(q).astype(BF16)
        q_t[i] = side_by_side(q.T).astype(BF16)
        k_s[i] = k.astype(BF16)
        v_s[i] = v.astype(BF16)
        kv_t = qkv[:, 128:].T
        k_t[i] = kv_t[:64].astype(BF16)
        v_t[i] = kv_t[64:].astype(BF16)

    key_row = lax.broadcasted_iota(jnp.int32, (ROWS, 2 * ROWS), 0)
    query_row = lax.rem(lax.broadcasted_iota(jnp.int32, (ROWS, 2 * ROWS), 1), ROWS)
    seen = key_row <= query_row

    @pl.loop(0, 8)
    def _(i):
        query = q_t[i]

        def add_block(j, carry, diagonal):
            top, total, acc = carry
            scores = dot(k_s[j], query)
            if diagonal:
                scores = jnp.where(seen, scores, -1e30)
            new_top = jnp.maximum(top, jnp.max(scores, axis=0, keepdims=True))
            fade = jnp.exp(top - new_top)
            weights = jnp.exp(scores - new_top)
            total = total * fade + jnp.sum(weights, axis=0, keepdims=True)
            acc = acc * fade + dot(v_t[j], weights.astype(BF16))
            return new_top, total, acc

        carry = (
            jnp.full((1, 2 * ROWS), -1e30, F32),
            jnp.zeros((1, 2 * ROWS), F32),
            jnp.zeros((64, 2 * ROWS), F32),
        )
        carry = lax.fori_loop(0, i, lambda j, c: add_block(j, c, False), carry)
        top, total, acc = add_block(i, carry, True)
        lse[i] = top + jnp.log(total)
        value = acc / total
        exact[i] = value
        both = jnp.concatenate([value[:, :ROWS], value[:, ROWS:]], axis=0)
        at = pl.ds(pl.multiple_of(i * ROWS, ROWS), ROWS)
        mixed[at] = both.T.astype(BF16)


def attend(tokens, gain, weights):
    shapes = [
        ((2048, 1024), BF16),
        ((8, 64, 512), BF16),
        ((8, 512, 64), BF16),
        ((8, 256, 64), BF16),
        ((8, 64, 256), BF16),
        ((8, 256, 64), BF16),
        ((8, 64, 256), BF16),
        ((8, 1, 512), F32),
        ((8, 64, 512), F32),
        ((2048, 128), BF16),
    ]
    return pl.pallas_call(
        attend_kernel,
        out_shape=[jax.ShapeDtypeStruct(s, t) for s, t in shapes],
        in_specs=[vmem()] * 3,
        out_specs=[vmem()] * len(shapes),
        compiler_params=pltpu.CompilerParams(vmem_limit_bytes=50 << 20),
    )(tokens, gain, weights)


def attend_back_kernel(
    mixed_grad, q_t, q_s, k_s, k_t, v_s, lse, exact, d, out_s, out_t, delta, dq
):
    @pl.loop(0, 8)
    def _(i):
        at = pl.ds(pl.multiple_of(i * ROWS, ROWS), ROWS)
        g = mixed_grad[at].astype(F32)
        out_s[i] = one_below(g).astype(BF16)
        g = side_by_side(g.T)
        out_t[i] = g.astype(BF16)
        delta[i] = jnp.sum(g * exact[i], axis=0, keepdims=True)
        dq[i] = jnp.zeros_like(dq[i])

    key_row = lax.broadcasted_iota(jnp.int32, (ROWS, 2 * ROWS), 0)
    query_row = lax.rem(lax.broadcasted_iota(jnp.int32, (ROWS, 2 * ROWS), 1), ROWS)
    seen = key_row <= query_row

    @pl.loop(0, 8)
    def _(j):
        key, key_t, value = k_s[j], k_t[j], v_s[j]

        def add_block(i, carry, diagonal):
            dk, dv = carry
            probs = jnp.exp(dot(key, q_t[i]) - lse[i])
            if diagonal:
                probs = jnp.where(seen, probs, 0.0)
            grad = probs * (dot(value, out_t[i]) - delta[i])
            grad = grad.astype(BF16)
            dv = dv + dot(probs.astype(BF16), out_s[i])
            dk = dk + dot(grad, q_s[i])
            dq[i] += dot(key_t, grad)
            return dk, dv

        zero = jnp.zeros((ROWS, 64), F32)
        carry = add_block(j, (zero, zero), True)
        dk, dv = lax.fori_loop(j + 1, 8, lambda i, c: add_block(i, c, False), carry)
        at = pl.ds(pl.multiple_of(j * ROWS, ROWS), ROWS)
        d[at, 128:256] = jnp.concatenate([dk, dv], axis=1).astype(BF16)

    @pl.loop(0, 8)
    def _(i):
        at = pl.ds(pl.multiple_of(i * ROWS, ROWS), ROWS)
        g = dq[i] * 0.125
        g = jnp.concatenate([g[:, :ROWS], g[:, ROWS:]], axis=0)
        d[at, 0:128] = g.T.astype(BF16)


def attend_back(mixed_grad, q_t, q_s, k_s, k_t, v_s, lse, exact):
    return pl.pallas_call(
        attend_back_kernel,
        out_shape=jax.ShapeDtypeStruct((2048, 256), BF16),
        in_specs=[vmem()] * 8,
        out_specs=vmem(),
        scratch_shapes=[
            VMEM((8, 512, 64), BF16),
            VMEM((8, 64, 512), BF16),
            VMEM((8, 1, 512), F32),
            VMEM((8, 64, 512), F32),
        ],
        compiler_params=pltpu.CompilerParams(vmem_limit_bytes=50 << 20),
    )(mixed_grad, q_t, q_s, k_s, k_t, v_s, lse, exact)


def experts_kernel(
    owner, moe, cot, routes, misc, weights,
    out_parts, grad_parts, rows, slot_grads, hidden, gate_grads, up_grads,
):
    own = owner[0]
    router = misc[0:32].astype(BF16)
    listed = [routes[b].astype(jnp.int32) for b in range(GROUP)]
    listed = [jnp.concatenate([r[:8], r[8:]], axis=1) for r in listed]

    def matrix(kind, k):
        return weights[:, 2 * kind + k].reshape(1024, 512)

    expert = lax.broadcasted_iota(jnp.int32, (32, ROWS), 0)
    named = [[None, None] for _ in range(GROUP)]
    gates = [[None, None] for _ in range(GROUP)]
    for b in range(GROUP):
        logits = dot(router, moe[b], ((1,), (1,)))
        chosen = expert < 0
        for j in range(8):
            chosen = chosen | (listed[b][j : j + 1] == expert)
        logits = jnp.where(chosen, logits, -1e30)
        weight = jnp.where(chosen, jnp.exp(logits - jnp.max(logits, axis=0, keepdims=True)), 0.0)
        weight = weight / jnp.sum(weight, axis=0, keepdims=True)
        for k in range(2):
            mine = expert == 2 * own + k
            gates[b][k] = jnp.sum(jnp.where(mine, weight, 0.0), axis=0, keepdims=True)
            named[b][k] = jnp.sum(
                jnp.where(mine & chosen, 1.0, 0.0), axis=0, keepdims=True
            )
    before = lax.broadcasted_iota(jnp.int32, (ROWS, ROWS), 0) < lax.broadcasted_iota(
        jnp.int32, (ROWS, ROWS), 1
    )
    flat = jnp.concatenate([named[b][k] for b in range(GROUP) for k in range(2)], axis=0)
    place = dot(flat.astype(BF16), before.astype(BF16))
    slot = lax.broadcasted_iota(jnp.int32, (CAP, ROWS), 0).astype(F32)
    spread = [[None, None] for _ in range(GROUP)]
    slot_gates = [[None, None] for _ in range(GROUP)]
    for b in range(GROUP):
        for k in range(2):
            at = 2 * b + k
            hit = (slot == place[at : at + 1]) & (flat[at : at + 1] > 0.5)
            spread[b][k] = jnp.where(hit, 1.0, 0.0).astype(BF16)
            slot_gates[b][k] = jnp.sum(
                jnp.where(hit, gates[b][k], 0.0), axis=1, keepdims=True
            )
    pick = [jnp.concatenate(spread[b], axis=0) for b in range(GROUP)]
    cots = [None] * GROUP
    for b in range(GROUP):
        both = dot(pick[b], moe[b]).astype(BF16)
        rows[0, b] = both[:CAP]
        rows[1, b] = both[CAP:]
        cots[b] = dot(pick[b], cot[b])
        for k in range(2):
            slot_grads[k, b] = (slot_gates[b][k] * cots[b][k * CAP : (k + 1) * CAP]).astype(BF16)
    gated = [None, None]
    row_grads = [None, None]
    weight_grads = [None, None]
    for k in range(2):
        x = rows[k].reshape(GROUP * CAP, 1024)
        dy = slot_grads[k].reshape(GROUP * CAP, 1024)
        g = dot(x, matrix(0, k))
        u = dot(x, matrix(1, k))
        s = jax.nn.sigmoid(g)
        silu = g * s
        h = (silu * u).astype(BF16)
        hidden[k] = h.reshape(GROUP, CAP, 512)
        y = dot(h, matrix(2, k), ((1,), (1,))).astype(BF16).astype(F32)
        gate = jnp.concatenate([slot_gates[b][k] for b in range(GROUP)], axis=0)
        gated[k] = (gate * y).astype(BF16)
        upstream = jnp.concatenate(
            [cots[b][k * CAP : (k + 1) * CAP] for b in range(GROUP)], axis=0
        )
        weight_grads[k] = jnp.sum(upstream * y, axis=1, keepdims=True)
        dh = dot(dy, matrix(2, k))
        gg = (dh * u * s * (1.0 + g * (1.0 - s))).astype(BF16)
        ug = (dh * silu).astype(BF16)
        gate_grads[k] = gg.reshape(GROUP, CAP, 512)
        up_grads[k] = ug.reshape(GROUP, CAP, 512)
        row_grads[k] = (
            dot(gg, matrix(0, k), ((1,), (1,))) + dot(ug, matrix(1, k), ((1,), (1,)))
        ).astype(BF16)
    owner_row = lax.broadcasted_iota(jnp.int32, (16, ROWS), 0) == own
    for b in range(GROUP):
        at = slice(b * CAP, (b + 1) * CAP)
        for source, target in ((gated, out_parts), (row_grads, grad_parts)):
            both = jnp.concatenate([source[0][at], source[1][at]], axis=0)
            total = dot(pick[b], both, ((0,), (0,))).astype(BF16)
            for q in range(4):
                target[b, q, 0:ROWS] = total[:, q * 256 : (q + 1) * 256]
        for k in range(2):
            vector = jnp.sum(
                spread[b][k].astype(F32) * weight_grads[k][at], axis=0, keepdims=True
            )
            high = vector.astype(BF16)
            low = (vector - high.astype(F32)).astype(BF16)
            grad_parts[b, 2 * k, ROWS : ROWS + 16] = jnp.where(
                owner_row, high.astype(F32), 0.0
            ).astype(BF16)
            grad_parts[b, 2 * k + 1, ROWS : ROWS + 16] = jnp.where(
                owner_row, low.astype(F32), 0.0
            ).astype(BF16)


def experts(owner, moe, cot, routes, misc, weights):
    steps = 16 // GROUP

    def block(*shape, dim=0):
        def index(g, owner):
            return tuple(g if i == dim else 0 for i in range(len(shape)))

        return pl.BlockSpec(shape, index)

    outs = [
        ((16, 4, 256, 256), BF16),
        ((16, 4, 272, 256), BF16),
        ((2, 16, CAP, 1024), BF16),
        ((2, 16, CAP, 1024), BF16),
        ((2, 16, CAP, 512), BF16),
        ((2, 16, CAP, 512), BF16),
        ((2, 16, CAP, 512), BF16),
    ]
    return pl.pallas_call(
        experts_kernel,
        grid_spec=pltpu.PrefetchScalarGridSpec(
            num_scalar_prefetch=1,
            grid=(steps,),
            in_specs=[
                block(GROUP, 256, 1024),
                block(GROUP, 256, 1024),
                block(GROUP, 16, 128),
                whole(40, 1024),
                whole(8, 6, 128, 512),
            ],
            out_specs=[
                block(GROUP, 4, 256, 256),
                block(GROUP, 4, 272, 256),
                block(2, GROUP, CAP, 1024, dim=1),
                block(2, GROUP, CAP, 1024, dim=1),
                block(2, GROUP, CAP, 512, dim=1),
                block(2, GROUP, CAP, 512, dim=1),
                block(2, GROUP, CAP, 512, dim=1),
            ],
        ),
        out_shape=[jax.ShapeDtypeStruct(s, t) for s, t in outs],
        compiler_params=pltpu.CompilerParams(vmem_limit_bytes=58 << 20),
    )(owner, moe, cot, routes, misc, weights)

PEERS = ((2, False), (2, True), (1, False), (1, True), (-1, False), (-1, True), (0, True))


def greet(ctx_peers, exp_steps):
    barrier = pltpu.get_barrier_semaphore()
    for step, other in ctx_peers:
        pl.semaphore_signal(
            barrier, inc=1, device_id={"ctx": ctx_block(step, other)}, device_id_type=MESH
        )
    for first, second in exp_steps:
        pl.semaphore_signal(
            barrier, inc=1, device_id={"exp": exp_block(first, second, 0, 0)}, device_id_type=MESH
        )
    pl.semaphore_wait(barrier, len(ctx_peers) + len(exp_steps))


NEIGHBOURS = ((1, 0), (-1, 0), (0, 1), (0, -1))


def to_ctx(src, dst, send, recv, peer):
    return pltpu.make_async_remote_copy(
        src_ref=src,
        dst_ref=dst,
        send_sem=send,
        recv_sem=recv,
        device_id={"ctx": ctx_block(*peer)},
        device_id_type=MESH,
    )


def gather_exp_stages(own, out, send, recv):
    rows = own.shape[0]
    copies = {
        (half, axis, k, s): gather_exp_copy(own, out, send, recv, rows, half, axis, k, s)
        for half in range(2)
        for axis, k in ((1, 0), (2, 0), (2, 1), (2, -1), (2, 2))
        for s in range(4)
    }

    def begin():
        for axis in (1, 2):
            for s in (0, 1):
                for half in range(2):
                    copies[half, axis, 0, s].start()

    def first(s, k):
        for half in range(2):
            copies[half, 1, 0, s].wait_recv()
            copies[half, 1, 0, s + 2].start()
            copies[half, 2, k, 0].start()
            copies[half, 2, k, 1].start()

    def middle():
        for half in range(2):
            copies[half, 1, 0, 2].wait_recv()
            copies[half, 1, 0, 3].wait_recv()
            copies[half, 2, 2, 0].start()
            copies[half, 2, 2, 1].start()

    def forward(k):
        for s in (0, 1):
            for half in range(2):
                copies[half, 2, k, s].wait_recv()
                copies[half, 2, k, s + 2].start()

    def last():
        for k in (0, -1, 1, 2):
            for s in (2, 3):
                for half in range(2):
                    copies[half, 2, k, s].wait_recv()

    def sent():
        for copy in copies.values():
            copy.wait_send()

    steps = [
        begin,
        lambda: first(0, -1),
        lambda: first(1, 1),
        lambda: forward(0),
        middle,
        lambda: forward(-1),
        lambda: forward(1),
        lambda: forward(2),
        last,
    ]
    return steps, sent


def start_kernel(
    tokens, cot, w_gate, w_up, w_down, pieces, out_piece, routes,
    attn_in, q_t, q_s, k_s, k_t, v_s, lse, exact, mixed_rows,
    head_w, misc_t, full_out, resid, moe_in, all_cot, all_routes, all_experts,
    land, own_experts, down_in, w_block, w_all, o_block, o_all, w_wide, o_wide, misc, v_t, mixed, mixed_land,
    exp_send, exp_recv, ctx_send, ctx_recv, ring_send, ring_recv, local,
):
    me = lax.axis_index("ctx")
    own = exp_block(0, 0, 0, 0)
    loads = [
        pltpu.make_async_copy(w_gate, own_experts.at[pl.ds(0, 2)], local.at[0]),
        pltpu.make_async_copy(w_up, own_experts.at[pl.ds(2, 2)], local.at[1]),
        pltpu.make_async_copy(w_down, down_in, local.at[2]),
        pltpu.make_async_copy(tokens, land.at[me], local.at[3]),
        pltpu.make_async_copy(pieces.at[me], w_block.at[pl.ds(me * 32, 32)], local.at[4]),
        pltpu.make_async_copy(routes, w_block.at[pl.ds(256, 64)], local.at[5]),
        pltpu.make_async_copy(out_piece, o_block.at[pl.ds(me * 64, 64)], local.at[6]),
        pltpu.make_async_copy(cot, all_cot.at[own], local.at[7]),
    ]
    for load in loads:
        load.start()
    greet(PEERS, NEIGHBOURS)
    piece_copies = [
        to_ctx(
            pieces.at[ctx_block(*peer)], w_block.at[pl.ds(me * 32, 32)],
            ctx_send.at[0, at], ctx_recv.at[0, at], peer,
        )
        for at, peer in enumerate(PEERS)
    ]
    out_copies = [
        to_ctx(
            out_piece, o_block.at[pl.ds(me * 64, 64)],
            ctx_send.at[1, at], ctx_recv.at[1, at], peer,
        )
        for at, peer in enumerate(PEERS)
    ]
    for copy in piece_copies + out_copies:
        copy.start()
    ring = gather_ctx_copies(tokens, land, ring_send.at[0], ring_recv.at[0])
    for at in (1, 2, 0):
        ring[at].start()
    w_steps, w_sent = gather_exp_stages(w_block, w_all, exp_send.at[0], exp_recv.at[0])
    o_steps, o_sent = gather_exp_stages(o_block, o_all, exp_send.at[1], exp_recv.at[1])
    c_steps, c_sent = gather_exp_stages(cot, all_cot, exp_send.at[2], exp_recv.at[2])
    for copy in piece_copies:
        copy.wait_recv()
    loads[4].wait()
    loads[5].wait()
    w_steps[0]()
    w_keep = pltpu.make_async_copy(w_block, w_all.at[own], local.at[8])
    w_keep.start()
    for copy in out_copies:
        copy.wait_recv()
    loads[6].wait()
    o_steps[0]()
    o_keep = pltpu.make_async_copy(o_block, o_all.at[own], local.at[9])
    o_keep.start()
    c_steps[0]()
    for at in (0, 1, 2):
        loads[at].wait()
    for k in range(2):
        own_experts[4 + k] = down_in[k].astype(F32).T.astype(BF16)
    for step in w_steps[1:]:
        step()
    w_keep.wait()
    ring[1].wait_recv()
    ring[3].start()
    ring[5].start()
    ring[2].wait_recv()
    ring[4].start()
    ring[6].start()

    @pl.loop(0, 128)
    def _(i):
        x, c = lax.div(i, 8), lax.rem(i, 8)
        at = pl.ds(pl.multiple_of(c * 128 + x * 8, 8), 8)
        line = pl.multiple_of(c * 32, 32)
        first = w_all[x, pl.ds(line, 16)].astype(F32)
        second = w_all[x, pl.ds(line + 16, 16)].astype(F32)
        w_wide[at, 0:128] = first[:8]
        w_wide[at, 128:256] = first[8:]
        misc[at] = second[:8]

    all_routes[...] = w_all[:, 256:272]
    head_w[...] = w_wide[...].astype(BF16)

    @pl.loop(0, 8)
    def _(c):
        at = pl.ds(pl.multiple_of(c * 128, 128), 128)
        misc_t[:, at] = misc[at].T[:40]

    def project(i):
        at = pl.ds(pl.multiple_of(i * ROWS, ROWS), ROWS)
        x = land[i].astype(F32)
        x = x * lax.rsqrt(jnp.mean(x * x, axis=1, keepdims=True) + EPSILON) * misc_t[33:34]
        x = x.astype(BF16)
        attn_in[at] = x
        qkv = dot(x, head_w[...]).astype(BF16).astype(F32)
        q = qkv[:, :128] * 0.125
        k, v = qkv[:, 128:192], qkv[:, 192:]
        q_s[i] = one_below(q).astype(BF16)
        q_t[i] = side_by_side(q.T).astype(BF16)
        k_s[i] = k.astype(BF16)
        v_s[i] = v.astype(BF16)
        kv_t = qkv[:, 128:].T
        k_t[i] = kv_t[:64].astype(BF16)
        v_t[i] = kv_t[64:].astype(BF16)

    o_steps[1]()
    o_steps[2]()
    loads[3].wait()
    project(ctx_block(0, False))
    ring[0].wait_recv()
    project(ctx_block(0, True))
    ring[3].wait_recv()
    ring[7].start()
    ring[4].wait_recv()
    ring[8].start()
    w_ring = gather_ctx_copies(own_experts, all_experts, ring_send.at[1], ring_recv.at[1])
    for at in (1, 2, 0):
        w_ring[at].start()
    w_ring_keep = pltpu.make_async_copy(own_experts, all_experts.at[me], local.at[10])
    w_ring_keep.start()
    o_steps[3]()
    o_steps[4]()
    c_steps[1]()
    c_steps[2]()
    project(ctx_block(-1, False))
    project(ctx_block(1, False))
    ring[5].wait_recv()
    project(ctx_block(-1, True))
    ring[6].wait_recv()
    project(ctx_block(1, True))
    project(ctx_block(2, False))
    ring[7].wait_recv()
    ring[8].wait_recv()
    project(ctx_block(2, True))

    key_row = lax.broadcasted_iota(jnp.int32, (ROWS, 2 * ROWS), 0)
    query_row = lax.rem(lax.broadcasted_iota(jnp.int32, (ROWS, 2 * ROWS), 1), ROWS)
    seen = key_row <= query_row

    def tile(i):
        query = q_t[i]

        def add_block(j, carry, diagonal):
            top, total, acc = carry
            scores = dot(k_s[j], query)
            if diagonal:
                scores = jnp.where(seen, scores, -1e30)
            new_top = jnp.maximum(top, jnp.max(scores, axis=0, keepdims=True))
            fade = jnp.exp(top - new_top)
            weights = jnp.exp(scores - new_top)
            total = total * fade + jnp.sum(weights, axis=0, keepdims=True)
            acc = acc * fade + dot(v_t[j], weights.astype(BF16))
            return new_top, total, acc

        carry = (
            jnp.full((1, 2 * ROWS), -1e30, F32),
            jnp.zeros((1, 2 * ROWS), F32),
            jnp.zeros((64, 2 * ROWS), F32),
        )
        carry = lax.fori_loop(0, i, lambda j, c: add_block(j, c, False), carry)
        top, total, acc = add_block(i, carry, True)
        lse[i] = top + jnp.log(total)
        value = acc / total
        exact[i] = value
        both = jnp.concatenate([value[:, :ROWS], value[:, ROWS:]], axis=0)
        mixed[i] = both.T.astype(BF16)

    def unpack_out():
        o_keep.wait()

        @pl.loop(0, 128)
        def _(i):
            x, c = lax.div(i, 8), lax.rem(i, 8)
            at = pl.ds(pl.multiple_of(c * 128 + x * 8, 8), 8)
            for t in range(4):
                line = pl.multiple_of(c * 64 + t * 16, 16)
                both = o_all[x, pl.ds(line, 16)].astype(F32)
                o_wide[at, 256 * t : 256 * t + 128] = both[:8]
                o_wide[at, 256 * t + 128 : 256 * t + 256] = both[8:]

        full_out[...] = o_wide[...].astype(BF16)

    def ring_first():
        w_ring[1].wait_recv()
        w_ring[3].start()
        w_ring[5].start()
        w_ring[2].wait_recv()
        w_ring[4].start()
        w_ring[6].start()

    def ring_second():
        w_ring[3].wait_recv()
        w_ring[7].start()
        w_ring[4].wait_recv()
        w_ring[8].start()

    between = (
        (o_steps[5], o_steps[6]),
        (o_steps[7], c_steps[3]),
        (c_steps[4], ring_first),
        (c_steps[5], o_steps[8]),
        (unpack_out,),
        (c_steps[6],),
        (c_steps[7], ring_second),
    )
    mixed_copies = []
    for at, peer in enumerate(PEERS):
        i = ctx_block(*peer)
        tile(i)
        copy = to_ctx(
            mixed.at[i], mixed_land.at[me], ctx_send.at[2, at], ctx_recv.at[2, at], peer
        )
        copy.start()
        mixed_copies.append(copy)
        for step in between[at]:
            step()
    tile(me)
    mixed_land[me] = mixed[me]
    total = tokens[...].astype(F32)
    for copy in mixed_copies:
        copy.wait_recv()
    for c in range(4):
        pair = jnp.concatenate([mixed_land[2 * c], mixed_land[2 * c + 1]], axis=1)
        total = total + dot(pair, full_out[c * 256 : (c + 1) * 256])
    mixed_rows[...] = mixed_land[...]
    resid[...] = total
    scaled = total * lax.rsqrt(jnp.mean(total * total, axis=1, keepdims=True) + EPSILON)
    scaled = (scaled * misc_t[32:33]).astype(BF16)
    for q in range(4):
        moe_in[q] = scaled[:, q * 256 : (q + 1) * 256]
    c_steps[8]()
    for at in (0, 5, 6, 7, 8):
        w_ring[at].wait_recv()
    w_ring_keep.wait()
    loads[7].wait()
    w_sent()
    o_sent()
    c_sent()
    for copy in (*piece_copies, *out_copies, *ring, *w_ring, *mixed_copies):
        copy.wait_send()


def start(tokens, cot, w_gate, w_up, w_down, pieces, out_piece, routes, collective_id):
    anywhere = pl.BlockSpec(memory_space=pl.ANY)
    outs = [
        ((2048, 1024), BF16, vmem()),
        ((8, 64, 512), BF16, vmem()),
        ((8, 512, 64), BF16, vmem()),
        ((8, 256, 64), BF16, vmem()),
        ((8, 64, 256), BF16, vmem()),
        ((8, 256, 64), BF16, vmem()),
        ((8, 1, 512), F32, vmem()),
        ((8, 64, 512), F32, vmem()),
        ((8, 256, 128), BF16, vmem()),
        ((1024, 256), BF16, vmem()),
        ((40, 1024), F32, vmem()),
        ((1024, 1024), BF16, vmem()),
        ((256, 1024), F32, vmem()),
        ((4, 256, 256), BF16, vmem()),
        ((16, 256, 1024), BF16, anywhere),
        ((16, 16, 128), BF16, vmem()),
        ((8, 6, 128, 512), BF16, anywhere),
    ]
    dma = pltpu.SemaphoreType.DMA
    return pl.pallas_call(
        start_kernel,
        out_shape=[jax.ShapeDtypeStruct(s, t) for s, t, _ in outs],
        in_specs=[vmem(), anywhere, anywhere, anywhere, anywhere, vmem(), vmem(), vmem()],
        out_specs=[spec for _, _, spec in outs],
        scratch_shapes=[
            VMEM((8, 256, 1024), BF16),
            VMEM((6, 128, 512), BF16),
            VMEM((2, 512, 128), BF16),
            VMEM((320, 128), BF16),
            VMEM((16, 320, 128), BF16),
            VMEM((512, 128), BF16),
            VMEM((16, 512, 128), BF16),
            VMEM((1024, 256), F32),
            VMEM((1024, 1024), F32),
            VMEM((1024, 128), F32),
            VMEM((8, 64, 256), BF16),
            VMEM((8, 256, 128), BF16),
            VMEM((8, 256, 128), BF16),
            dma((3, 40)),
            dma((3, 40)),
            dma((3, 7)),
            dma((3, 7)),
            dma((2, 9)),
            dma((2, 9)),
            dma((11,)),
        ],
        compiler_params=pltpu.CompilerParams(
            collective_id=collective_id, has_side_effects=True, vmem_limit_bytes=56 << 20
        ),
    )(tokens, cot, w_gate, w_up, w_down, pieces, out_piece, routes)

ORDER = (0, 2, 1, -1)
LINES = ROWS + 16


def part_gather_copies(own, held, send, recv):
    copies = {}
    for half in range(2):
        for axis, k in ((1, 0), (2, 0), (2, 1), (2, -1), (2, 2)):
            for s in range(4):
                step = (1, -1, 1, -1)[s]
                off = (0, 0, -1, 1)[s]
                origin = exp_block(off, 0, half, 0) if axis == 1 else exp_block(k, off, half, 0)
                target = exp_block(step, 0, half, 0) if axis == 1 else exp_block(0, step, half, 0)
                first, count = (2 * half, 2) if s < 2 else (2 * half + s - 2, 1)
                place = held.at[pl.ds(origin * 4 + first, count), pl.ds(0, ROWS)]
                mine = s < 2 and (axis == 1 or k == 0)
                at = half * 20 + (s if axis == 1 else 4 + 4 * (k % 4) + s)
                copies[half, axis, k, s] = pltpu.make_async_remote_copy(
                    src_ref=own.at[pl.ds(first, count)] if mine else place,
                    dst_ref=place,
                    send_sem=send.at[at],
                    recv_sem=recv.at[at],
                    device_id={"exp": target},
                    device_id_type=MESH,
                )
    return copies


def part_reduce_copies(parts, held, send, recv):
    copies = {}
    for half in range(2):
        for axis, k in ((1, 0), (1, 1), (1, -1), (1, 2), (2, 0)):
            row = half * 5 + (k % 4 if axis == 1 else 4)
            for s in range(4):
                step = (1, -1, 1, -1)[s]
                dest = (2, 2, 1, -1)[s]
                block = exp_block(dest, k, half, 1) if axis == 1 else exp_block(0, dest, half, 1)
                target = exp_block(step, 0, half, 1) if axis == 1 else exp_block(0, step, half, 1)
                first, count = (2 * half + s, 1) if s < 2 else (2 * half, 2)
                at = row * 4 + s
                copies[half, axis, k, s] = pltpu.make_async_remote_copy(
                    src_ref=parts.at[pl.ds(block * 4 + first, count)],
                    dst_ref=held.at[pl.ds(row * 6 + (0, 1, 2, 4)[s], count)],
                    send_sem=send.at[at],
                    recv_sem=recv.at[at],
                    device_id={"exp": target},
                    device_id_type=MESH,
                )
    return copies


def moe_kernel(
    moe, misc, routes, cot, experts,
    grad_total, out_parts, terms,
    held, parts, weights, cots, x_rows, c_rows, hidden, gate_g, up_g, pick,
    gated, row_g, stage, term_stage, slot_gates, slot_grads,
    gather_send, gather_recv, reduce_send, reduce_recv, cot_sem, stage_sem, term_sem, local, ready,
):
    own = exp_block(0, 0, 0, 0)

    def block_of(group, o):
        return exp_block(o, group, 0, 0)

    def cot_load(n, o):
        return pltpu.make_async_copy(cot.at[block_of(ORDER[n], o)], cots.at[o], cot_sem.at[o])

    weight_load = pltpu.make_async_copy(experts, weights, local.at[0])
    weight_load.start()
    for o in range(4):
        cot_load(0, o).start()
    keep = pltpu.make_async_copy(
        moe, held.at[pl.ds(own * 4, 4), pl.ds(0, ROWS)], local.at[1]
    )
    keep.start()
    greet((), NEIGHBOURS)
    gathers = part_gather_copies(moe, held, gather_send, gather_recv)
    reduces = part_reduce_copies(parts, held, reduce_send, reduce_recv)
    router = misc[0:32].astype(BF16)

    def dispatch(n):
        expert = lax.broadcasted_iota(jnp.int32, (32, ROWS), 0)
        before = lax.broadcasted_iota(jnp.int32, (ROWS, ROWS), 0) < lax.broadcasted_iota(
            jnp.int32, (ROWS, ROWS), 1
        )
        before = jnp.where(before, 1.0, 0.0).astype(BF16)
        slot = lax.broadcasted_iota(jnp.int32, (CAP, ROWS), 0).astype(F32)

        @pl.loop(0, 4)
        def _(o):
            b = block_of(ORDER[n], o)
            listed = routes[b].astype(F32).astype(jnp.int32)
            listed = jnp.concatenate([listed[:8], listed[8:]], axis=1)
            logits = jnp.zeros((32, ROWS), F32)
            for q in range(4):
                logits = logits + dot(
                    router[:, q * 256 : (q + 1) * 256], held[b * 4 + q, 0:ROWS], ((1,), (1,))
                )
            chosen = expert < 0
            for j in range(8):
                chosen = chosen | (listed[j : j + 1] == expert)
            logits = jnp.where(chosen, logits, -1e30)
            weight = jnp.exp(logits - jnp.max(logits, axis=0, keepdims=True))
            weight = jnp.where(chosen, weight, 0.0)
            weight = weight / jnp.sum(weight, axis=0, keepdims=True)
            named, gates = [], []
            for k in range(2):
                mine = expert == 2 * own + k
                gates.append(jnp.sum(jnp.where(mine, weight, 0.0), axis=0, keepdims=True))
                named.append(
                    jnp.sum(jnp.where(mine & chosen, 1.0, 0.0), axis=0, keepdims=True)
                )
            flat = jnp.concatenate(named + [jnp.zeros((6, ROWS), F32)], axis=0)
            place = dot(flat.astype(BF16), before)
            spread = []
            for k in range(2):
                hit = (slot == place[k : k + 1]) & (named[k] > 0.5)
                spread.append(jnp.where(hit, 1.0, 0.0).astype(BF16))
                lines = pl.ds(pl.multiple_of(o * CAP, CAP), CAP)
                slot_gates[n, k, lines] = jnp.sum(
                    jnp.where(hit, gates[k], 0.0), axis=1, keepdims=True
                )
            both = jnp.concatenate(spread, axis=0)
            pick[n, o] = both
            cot_load(n, o).wait()
            for q in range(4):
                at = slice(q * 256, (q + 1) * 256)
                rows = dot(both, held[b * 4 + q, 0:ROWS]).astype(BF16)
                grads = dot(both, cots[o, :, at]).astype(BF16)
                for k in range(2):
                    x_rows[k, n, o, :, at] = rows[k * CAP : (k + 1) * CAP]
                    c_rows[k, n, o, :, at] = grads[k * CAP : (k + 1) * CAP]
            if n < 3:
                cot_load(n + 1, o).start()

    def matrix(kind, k):
        return weights[:, 2 * kind + k].reshape(1024, 512)

    def expert(n, k):
        x = x_rows[k, n].reshape(GROUP * CAP, 1024)
        c = c_rows[k, n].reshape(GROUP * CAP, 1024)
        gate = slot_gates[n, k]
        g = dot(x, matrix(0, k))
        u = dot(x, matrix(1, k))
        s = jax.nn.sigmoid(g)
        silu = g * s
        h = (silu * u).astype(BF16)
        hidden[k, n] = h
        y = dot(h, matrix(2, k), ((1,), (1,))).astype(BF16).astype(F32)
        gated[k] = (gate * y).astype(BF16)
        c = c.astype(F32)
        slot_grads[k] = jnp.sum(c * y, axis=1, keepdims=True)
        dy = (gate * c).astype(BF16)
        c_rows[k, n] = dy.reshape(GROUP, CAP, 1024)
        dh = dot(dy, matrix(2, k))
        gg = (dh * u * s * (1.0 + g * (1.0 - s))).astype(BF16)
        ug = (dh * silu).astype(BF16)
        gate_g[k, n] = gg
        up_g[k, n] = ug
        row_g[k] = (
            dot(gg, matrix(0, k), ((1,), (1,))) + dot(ug, matrix(1, k), ((1,), (1,)))
        ).astype(BF16)

    def stage_copy(b, o):
        slot = lax.rem(o, 2)
        return pltpu.make_async_copy(stage.at[slot], out_parts.at[b], stage_sem.at[slot])

    def combine(n, first=False):
        owner_row = lax.broadcasted_iota(jnp.int32, (16, ROWS), 0) == own

        @pl.loop(0, 4)
        def _(o):
            b = block_of(ORDER[n], o)
            lines = pl.ds(pl.multiple_of(o * CAP, CAP), CAP)
            chosen = pick[n, o]

            def spread(rows):
                both = jnp.concatenate([rows[0, lines], rows[1, lines]], axis=0)
                return dot(chosen, both, ((0,), (0,))).astype(BF16)

            total = spread(row_g)
            for q in range(4):
                parts[b * 4 + q, 0:ROWS] = total[:, q * 256 : (q + 1) * 256]
            for k in range(2):
                hits = chosen[k * CAP : (k + 1) * CAP].astype(F32)
                vector = jnp.sum(hits * slot_grads[k, lines], axis=0, keepdims=True)
                high = vector.astype(BF16).astype(F32)
                for q, value in ((2 * k, high), (2 * k + 1, vector - high)):
                    parts[b * 4 + q, ROWS:LINES] = jnp.where(owner_row, value, 0.0).astype(BF16)
            total = spread(gated)
            if first:

                @pl.when(o >= 2)
                def _():
                    stage_copy(b, o).wait()

            else:
                stage_copy(b, o).wait()
            slot = lax.rem(o, 2)
            for q in range(4):
                stage[slot, q] = total[:, q * 256 : (q + 1) * 256]
            stage_copy(b, o).start()

    def add(target, *landed):
        value = parts[target].astype(F32)
        for at in landed:
            value = value + held[at].astype(F32)
        parts[target] = value.astype(BF16)

    def row_of(half, axis, k):
        return (half * 5 + (k % 4 if axis == 1 else 4)) * 6

    def block_at(half, axis, k, dest):
        return exp_block(dest, k, half, 1) if axis == 1 else exp_block(0, dest, half, 1)

    def send_far(half, axis, k):
        reduces[half, axis, k, 0].start()
        reduces[half, axis, k, 1].start()

    def pass_on(half, axis, k, s):
        reduces[half, axis, k, s].wait_recv()
        block = block_at(half, axis, k, 1 - 2 * s)
        add(block * 4 + 2 * half + s, row_of(half, axis, k) + s)
        reduces[half, axis, k, s + 2].start()

    def finish(half, axis, k):
        reduces[half, axis, k, 2].wait_recv()
        reduces[half, axis, k, 3].wait_recv()
        row = row_of(half, axis, k)
        for part in range(2):
            target = block_at(half, axis, k, 0) * 4 + 2 * half + part
            add(target, row + 2 + part, row + 4 + part)

    def term_copy(kind, k, tile):
        return pltpu.make_async_copy(
            term_stage.at[tile], terms.at[pl.ds(2 * tile, 2), 2 * kind + k], term_sem.at[tile]
        )

    def term(kind, k, first=False):
        left = c_rows if kind == 2 else x_rows
        right = (gate_g, up_g, hidden)[kind]

        @pl.loop(0, 4)
        def _(tile):
            at = pl.ds(pl.multiple_of(tile * 256, 256), 256)
            rows = left[k, :, :, :, at].reshape(16 * CAP, 256)
            value = dot(rows, right[k].reshape(16 * CAP, 512), ((0,), (0,)))
            if not first:
                term_copy(kind, k, tile).wait()
            term_stage[tile] = value.astype(BF16).reshape(2, 128, 512)
            term_copy(kind, k, tile).start()

    def forward(k):
        for s in (0, 1):
            for half in range(2):
                gathers[half, 2, k, s].wait_recv()
                gathers[half, 2, k, s + 2].start()

    for axis in (1, 2):
        for s in (0, 1):
            for half in range(2):
                gathers[half, axis, 0, s].start()
    for s, k in ((0, -1), (1, 1)):
        for half in range(2):
            gathers[half, 1, 0, s].wait_recv()
            gathers[half, 1, 0, s + 2].start()
            gathers[half, 2, k, 0].start()
            gathers[half, 2, k, 1].start()
    forward(0)
    for half in range(2):
        gathers[half, 1, 0, 2].wait_recv()
        gathers[half, 1, 0, 3].wait_recv()
        gathers[half, 2, 2, 0].start()
        gathers[half, 2, 2, 1].start()
    gathers[1, 2, 0, 2].wait_recv()
    gathers[1, 2, 0, 3].wait_recv()
    forward(-1)
    forward(1)
    keep.wait()
    weight_load.wait()
    dispatch(0)
    expert(0, 0)
    forward(2)
    expert(0, 1)
    combine(0, first=True)
    for half in range(2):
        for k in (0, -1, 1, 2):
            if (half, k) != (1, 0):
                gathers[half, 2, k, 2].wait_recv()
                gathers[half, 2, k, 3].wait_recv()
    dispatch(1)
    dispatch(2)
    dispatch(3)
    for copy in gathers.values():
        copy.wait_send()
    for first, second in NEIGHBOURS:
        pl.semaphore_signal(
            ready, inc=1, device_id={"exp": exp_block(first, second, 0, 0)}, device_id_type=MESH
        )
    expert(1, 0)
    expert(1, 1)
    combine(1)
    pl.semaphore_wait(ready, 4)
    send_far(1, 1, 2)
    send_far(0, 1, 2)
    send_far(0, 1, 1)
    send_far(0, 1, -1)
    send_far(0, 1, 0)
    send_far(1, 1, 0)
    expert(2, 0)
    pass_on(1, 1, 2, 0)
    pass_on(1, 1, 2, 1)
    expert(2, 1)
    combine(2)
    send_far(1, 1, 1)
    for k in (2, 1, -1, 0):
        pass_on(0, 1, k, 0)
    expert(3, 0)
    pass_on(1, 1, 0, 0)
    pass_on(1, 1, 0, 1)
    expert(3, 1)
    combine(3)
    send_far(1, 1, -1)
    for k in (2, 1, -1, 0):
        pass_on(0, 1, k, 1)
    pass_on(1, 1, 1, 0)
    pass_on(1, 1, 1, 1)
    term(0, 0, first=True)
    finish(1, 1, 2)
    send_far(1, 2, 0)
    pass_on(1, 1, -1, 0)
    pass_on(1, 1, -1, 1)
    term(0, 1)
    finish(0, 1, 2)
    send_far(0, 2, 0)
    finish(1, 1, 1)
    finish(0, 1, 1)
    term(1, 0)
    finish(1, 1, -1)
    finish(0, 1, -1)
    for half in (1, 0):
        pass_on(half, 2, 0, 0)
        pass_on(half, 2, 0, 1)
    term(1, 1)
    finish(1, 1, 0)
    finish(0, 1, 0)
    term(2, 0)
    term(2, 1)
    finish(1, 2, 0)
    finish(0, 2, 0)
    for q in range(4):
        grad_total[q] = parts[own * 4 + q]
    for copy in reduces.values():
        copy.wait_send()
    for o in range(2):
        stage_copy(own, o).wait()
    for tile in range(4):
        term_copy(0, 0, tile).wait()


def moe_block(moe, misc, routes, cot, experts, collective_id):
    anywhere = pl.BlockSpec(memory_space=pl.ANY)
    dma = pltpu.SemaphoreType.DMA
    return pl.pallas_call(
        moe_kernel,
        out_shape=[
            jax.ShapeDtypeStruct((4, LINES, 256), BF16),
            jax.ShapeDtypeStruct((16, 4, ROWS, 256), BF16),
            jax.ShapeDtypeStruct((8, 6, 128, 512), BF16),
        ],
        in_specs=[vmem(), vmem(), vmem(), anywhere, anywhere],
        out_specs=[vmem(), anywhere, anywhere],
        scratch_shapes=[
            VMEM((64, LINES, 256), BF16),
            VMEM((64, LINES, 256), BF16),
            VMEM((8, 6, 128, 512), BF16),
            VMEM((4, ROWS, 1024), BF16),
            VMEM((2, 4, GROUP, CAP, 1024), BF16),
            VMEM((2, 4, GROUP, CAP, 1024), BF16),
            VMEM((2, 4, GROUP * CAP, 512), BF16),
            VMEM((2, 4, GROUP * CAP, 512), BF16),
            VMEM((2, 4, GROUP * CAP, 512), BF16),
            VMEM((4, GROUP, 2 * CAP, ROWS), BF16),
            VMEM((2, GROUP * CAP, 1024), BF16),
            VMEM((2, GROUP * CAP, 1024), BF16),
            VMEM((2, 4, ROWS, 256), BF16),
            VMEM((4, 2, 128, 512), BF16),
            VMEM((4, 2, GROUP * CAP, 1), F32),
            VMEM((2, GROUP * CAP, 1), F32),
            dma((40,)),
            dma((40,)),
            dma((40,)),
            dma((40,)),
            dma((4,)),
            dma((2,)),
            dma((4,)),
            dma((2,)),
            pltpu.SemaphoreType.REGULAR,
        ],
        compiler_params=pltpu.CompilerParams(
            collective_id=collective_id, has_side_effects=True, vmem_limit_bytes=63 << 20
        ),
    )(moe, misc, routes, cot, experts)


def add_rows(target, others):
    shape = target.shape
    chunk = 1 if len(shape) == 3 else min(shape[0], 65536 // shape[1])

    def add(at):
        value = target[at].astype(F32)
        for other in others:
            value = value + other[at].astype(F32)
        target[at] = value.astype(target.dtype)

    if chunk == shape[0]:
        add(slice(None))
        return

    @pl.loop(0, shape[0] // chunk)
    def _(i):
        add(i if len(shape) == 3 else pl.ds(pl.multiple_of(i * chunk, chunk), chunk))


class ExpReduce:
    def __init__(self, parts, landed, send, recv):
        self.parts, self.landed = parts, landed
        self.copies = part_reduce_copies(parts, landed, send, recv)

    def block_at(self, half, axis, k, dest):
        return exp_block(dest, k, half, 1) if axis == 1 else exp_block(0, dest, half, 1)

    def row_of(self, half, axis, k):
        return (half * 5 + (k % 4 if axis == 1 else 4)) * 6

    def send_far(self, half, axis, k):
        self.copies[half, axis, k, 0].start()
        self.copies[half, axis, k, 1].start()

    def pass_on(self, half, axis, k):
        for s in (0, 1):
            self.copies[half, axis, k, s].wait_recv()
            line = self.block_at(half, axis, k, 1 - 2 * s) * 4 + 2 * half + s
            add_rows(self.parts.at[line], [self.landed.at[self.row_of(half, axis, k) + s]])
            self.copies[half, axis, k, s + 2].start()

    def finish(self, half, axis, k):
        self.copies[half, axis, k, 2].wait_recv()
        self.copies[half, axis, k, 3].wait_recv()
        row = self.row_of(half, axis, k)
        for part in range(2):
            line = self.block_at(half, axis, k, 0) * 4 + 2 * half + part
            add_rows(
                self.parts.at[line],
                [self.landed.at[row + 2 + part], self.landed.at[row + 4 + part]],
            )

    def steps(self):
        def begin():
            for k in (2, 1, -1, 0):
                for half in range(2):
                    self.send_far(half, 1, k)

        def both(action, axis, k):
            def run():
                for half in range(2):
                    action(half, axis, k)

            return run

        def far():
            for half in range(2):
                self.finish(half, 1, 2)
                self.send_far(half, 2, 0)

        return [
            begin,
            both(self.pass_on, 1, 2),
            both(self.pass_on, 1, 1),
            both(self.pass_on, 1, -1),
            both(self.pass_on, 1, 0),
            far,
            both(self.finish, 1, 1),
            both(self.finish, 1, -1),
            both(self.pass_on, 2, 0),
            both(self.finish, 1, 0),
            both(self.finish, 2, 0),
        ]

    def sent(self):
        for copy in self.copies.values():
            copy.wait_send()


class CtxReduce:
    STEPS = (2, 1, -1, 0)

    def __init__(self, given, mine, near, landed, send, recv):
        self.mine, self.near, self.landed = mine, near, landed
        half = near.shape[1] // 2
        self.first, self.second = pl.ds(0, half), pl.ds(half, half)
        self.swaps = [
            to_ctx(
                given.at[ctx_block(step, True)], near.at[at], send.at[at], recv.at[at], (0, True)
            )
            for at, step in enumerate(self.STEPS)
        ]
        self.hops = [
            to_ctx(src, dst, send.at[4 + at], recv.at[4 + at], (step, False))
            for at, (src, dst, step) in enumerate(
                (
                    (mine[0].at[self.first], landed.at[0, self.first], 1),
                    (mine[0].at[self.second], landed.at[0, self.second], -1),
                    (mine[1], landed.at[1], 1),
                    (mine[2], landed.at[2], -1),
                )
            )
        ]

    def swap(self):
        for copy in self.swaps:
            copy.start()

    def take(self, at):
        self.swaps[at].wait_recv()
        add_rows(self.mine[at], [self.near.at[at]])

    def far(self):
        self.take(0)
        self.hops[0].start()
        self.hops[1].start()

    def sides(self):
        self.take(1)
        self.take(2)

    def pass_on(self):
        for at, part in ((0, self.first), (1, self.second)):
            self.hops[at].wait_recv()
            add_rows(self.mine[1 + at].at[part], [self.landed.at[0, part]])
            self.hops[2 + at].start()

    def finish(self):
        self.take(3)
        self.hops[2].wait_recv()
        self.hops[3].wait_recv()
        add_rows(self.mine[3], [self.landed.at[1], self.landed.at[2]])

    def sent(self):
        for copy in (*self.swaps, *self.hops):
            copy.wait_send()


def split_dot(value, other, dims):
    high = value.astype(BF16)
    low = (value - high.astype(F32)).astype(BF16)
    return dot(high, other, dims) + dot(low, other, dims)


def norm_back(values, grads, gain):
    r = lax.rsqrt(jnp.mean(values * values, axis=1, keepdims=True) + EPSILON)
    n = values * r
    scaled = grads * gain
    back = r * (scaled - n * jnp.mean(scaled * n, axis=1, keepdims=True))
    return back, n


def finish_kernel(
    grad_total, resid, misc, router, routes, moe, cot, tokens, full_out, mixed_rows,
    q_t, q_s, k_s, k_t, v_s, lse, exact, head_w, attn_in, out_parts, terms,
    output, token_grad, head_sum, out_sum, gate_sum, up_sum, down_sum,
    o_parts, o_landed, t_mine, t_near, t_landed, attn_grad, resid_grad, mg_out, mg_land,
    p_given, p_near, p_landed, out_s, out_t, delta, dq, d, a_given, a_near, a_landed,
    head_acc, small, w_parts, w_landed, wide_small, f_given, f_land, attn_rows,
    o_send, o_recv, w_send, w_recv, ctx_send, ctx_recv, direct_send, direct_recv, local, rows_sem,
):
    me = lax.axis_index("ctx")
    own = exp_block(0, 0, 0, 0)
    o_load = pltpu.make_async_copy(out_parts, o_parts, local.at[0])
    o_load.start()
    t_loads = [
        pltpu.make_async_copy(terms.at[ctx_block(step, False)], t_mine.at[at], local.at[1 + at])
        for at, step in enumerate(CtxReduce.STEPS)
    ]
    for load in t_loads:
        load.start()

    def rows_load(j):
        return pltpu.make_async_copy(
            attn_in.at[pl.ds(j * ROWS, ROWS)], attn_rows.at[j % 2], rows_sem.at[j % 2]
        )

    rows_load(0).start()
    greet(PEERS, NEIGHBOURS)
    out_reduce = ExpReduce(o_parts, o_landed, o_send, o_recv)
    o_steps = out_reduce.steps()
    term_reduce = CtxReduce(
        terms, [t_mine.at[at] for at in range(4)], t_near, t_landed, ctx_send.at[0], ctx_recv.at[0]
    )
    proj_reduce = CtxReduce(
        p_given, [p_given.at[ctx_block(step, False)] for step in CtxReduce.STEPS],
        p_near, p_landed, ctx_send.at[1], ctx_recv.at[1],
    )
    attn_reduce = CtxReduce(
        a_given, [a_given.at[ctx_block(step, False)] for step in CtxReduce.STEPS],
        a_near, a_landed, ctx_send.at[2], ctx_recv.at[2],
    )
    o_load.wait()
    o_steps[0]()

    place = lax.broadcasted_iota(jnp.int32, (32, ROWS), 0)
    expert = 2 * lax.rem(place, 16) + lax.div(place, 16)
    listed = routes[own].astype(F32).astype(jnp.int32)
    listed = jnp.concatenate([listed[:8], listed[8:]], axis=1)
    chosen = expert < 0
    for j in range(8):
        chosen = chosen | (listed[j : j + 1] == expert)
    logits = jnp.zeros((32, ROWS), F32)
    for q in range(4):
        logits = logits + dot(router[:, q * 256 : (q + 1) * 256], moe[q], ((1,), (1,)))
    logits = jnp.where(chosen, logits, -1e30)
    gates = jnp.exp(logits - jnp.max(logits, axis=0, keepdims=True))
    gates = jnp.where(chosen, gates, 0.0)
    gates = gates / jnp.sum(gates, axis=0, keepdims=True)
    weight_grad = [grad_total[q, ROWS:LINES].astype(F32) for q in range(4)]
    weight_grad = jnp.concatenate(
        [weight_grad[0] + weight_grad[1], weight_grad[2] + weight_grad[3]], axis=0
    )
    logit_grad = gates * (weight_grad - jnp.sum(gates * weight_grad, axis=0, keepdims=True))
    logit_grad = jnp.where(chosen, logit_grad, 0.0)
    moe_in_grad = jnp.concatenate(
        [grad_total[q, 0:ROWS].astype(F32) for q in range(4)], axis=1
    )
    moe_in_grad = moe_in_grad + split_dot(logit_grad, router[...], ((0,), (0,)))
    back, n = norm_back(resid[...], moe_in_grad, misc[32:33])
    total = back + cot[...].astype(F32)
    resid_grad[...] = total
    attn_grad[...] = total.astype(BF16)
    mixed_grad = dot(attn_grad[...], full_out[...], ((1,), (1,))).astype(BF16)
    for c in range(8):
        mg_out[c] = mixed_grad[:, c * 128 : (c + 1) * 128]
    mg_copies = [
        to_ctx(
            mg_out.at[ctx_block(*peer)], mg_land.at[me],
            direct_send.at[0, at], direct_recv.at[0, at], peer,
        )
        for at, peer in enumerate(PEERS)
    ]
    for copy in mg_copies:
        copy.start()
    term_reduce.swap()
    mg_land[me] = mg_out[me]
    for c in range(8):
        p_given[c] = dot(mixed_rows[c], attn_grad[...], ((0,), (0,))).astype(BF16)
    proj_reduce.swap()
    for q in range(4):
        at = slice(q * 256, (q + 1) * 256)
        small[0:32, at] = split_dot(logit_grad, moe[q], ((1,), (0,)))
    small[32:40] = jnp.broadcast_to(jnp.sum(moe_in_grad * n, axis=0, keepdims=True), (8, 1024))
    o_steps[1]()
    for load in t_loads:
        load.wait()
    term_reduce.far()
    proj_reduce.far()
    term_reduce.sides()
    proj_reduce.sides()
    o_steps[2]()
    for copy in mg_copies:
        copy.wait_recv()

    @pl.loop(0, 8)
    def _(i):
        g = mg_land[i].astype(F32)
        out_s[i] = one_below(g).astype(BF16)
        g = side_by_side(g.T)
        out_t[i] = g.astype(BF16)
        delta[i] = jnp.sum(g * exact[i], axis=0, keepdims=True)
        dq[i] = jnp.zeros_like(dq[i])

    key_row = lax.broadcasted_iota(jnp.int32, (ROWS, 2 * ROWS), 0)
    query_row = lax.rem(lax.broadcasted_iota(jnp.int32, (ROWS, 2 * ROWS), 1), ROWS)
    seen = key_row <= query_row

    def key_block(j):
        key, key_t, value = k_s[j], k_t[j], v_s[j]

        def add_block(i, carry, diagonal):
            dk, dv = carry
            probs = jnp.exp(dot(key, q_t[i]) - lse[i])
            if diagonal:
                probs = jnp.where(seen, probs, 0.0)
            grad = probs * (dot(value, out_t[i]) - delta[i])
            grad = grad.astype(BF16)
            dv = dv + dot(probs.astype(BF16), out_s[i])
            dk = dk + dot(grad, q_s[i])
            dq[i] += dot(key_t, grad)
            return dk, dv

        zero = jnp.zeros((ROWS, 64), F32)
        carry = add_block(j, (zero, zero), True)
        dk, dv = lax.fori_loop(j + 1, 8, lambda i, c: add_block(i, c, False), carry)
        g = dq[j] * 0.125
        g = jnp.concatenate([g[:, :ROWS], g[:, ROWS:]], axis=0).T
        d[j] = jnp.concatenate([g, dk, dv], axis=1).astype(BF16)
        a_given[j] = dot(d[j], head_w[...], ((1,), (1,))).astype(BF16)

    def head_term(j):
        rows_load(j).wait()
        if j < 7:
            rows_load(j + 1).start()
        value = dot(attn_rows[j % 2], d[j], ((0,), (0,)))
        value = value.reshape(8, 16, 8, 256)
        head_acc[...] = value if j == 0 else head_acc[...] + value

    between = (
        (o_steps[3],),
        (term_reduce.pass_on, o_steps[4]),
        (proj_reduce.pass_on, o_steps[5]),
        (o_steps[6],),
        (o_steps[7], o_steps[8]),
        (proj_reduce.finish,),
        (o_steps[9],),
        (),
    )
    for j in range(8):
        key_block(j)
        if j < 7:
            head_term(j)
        for step in between[j]:
            step()
    attn_reduce.swap()
    head_term(7)
    attn_reduce.far()
    wide = jnp.concatenate([small[...], jnp.zeros((88, 1024), F32)], axis=0)
    for c in range(8):
        wide_small[c] = wide[:, c * 128 : (c + 1) * 128].T
    mine = proj_reduce.mine[3]

    for x in range(16):
        head = head_acc[:, x].reshape(64, 256)
        rows = mine[pl.ds((x // 2) * 16, 16)].astype(F32)[(x % 2) * 8 : (x % 2) * 8 + 8]
        rows = jnp.concatenate([rows[:, q * 256 : (q + 1) * 256] for q in range(4)], axis=0)
        rest = wide_small[:, x * 8 : x * 8 + 8].reshape(64, 128)
        rest = jnp.concatenate([rest[:32], rest[32:]], axis=1)
        w_parts[4 * x] = head[:32].astype(BF16)
        w_parts[4 * x + 1] = head[32:].astype(BF16)
        w_parts[4 * x + 2] = rows.astype(BF16)
        w_parts[4 * x + 3] = rest.astype(BF16)
    w_reduce = ExpReduce(w_parts, w_landed, w_send, w_recv)
    w_steps = w_reduce.steps()
    w_steps[0]()
    attn_reduce.sides()
    for step in w_steps[1:5]:
        step()
    attn_reduce.pass_on()
    for step in w_steps[5:9]:
        step()
    term_reduce.finish()
    sums = [t_mine[3, 2 * kind : 2 * kind + 2].astype(F32) for kind in range(3)]
    gate_sum[...] = sums[0]
    up_sum[...] = sums[1]
    for k in range(2):
        down_sum[k] = sums[2][k].T
    for step in w_steps[9:]:
        step()
    done = [w_parts[4 * own + q].astype(F32) for q in range(4)]
    for q in range(4):
        out_sum[:, q * 256 : (q + 1) * 256] = done[2][q * 8 : (q + 1) * 8]
    for c in range(8):
        source = done[c // 4][(c % 4) * 8 : (c % 4) * 8 + 8]
        f_send = jnp.concatenate(
            [
                source,
                done[3][(c % 4) * 8 : (c % 4) * 8 + 8, (c // 4) * 128 : (c // 4) * 128 + 128],
            ],
            axis=1,
        )
        f_given[c] = f_send
    f_copies = [
        to_ctx(
            f_given.at[ctx_block(*peer)], f_land.at[me],
            direct_send.at[1, at], direct_recv.at[1, at], peer,
        )
        for at, peer in enumerate(PEERS)
    ]
    for copy in f_copies:
        copy.start()
    f_land[me] = f_given[me]
    o_steps[10]()
    expert_out = jnp.concatenate([o_parts[4 * own + q].astype(F32) for q in range(4)], axis=1)
    output[...] = (resid[...] + expert_out).astype(BF16)
    for copy in f_copies:
        copy.wait_recv()
    for c in range(8):
        head_sum[c] = f_land[c]
    attn_reduce.finish()
    back, _ = norm_back(
        tokens[...].astype(F32), attn_reduce.mine[3][...].astype(F32), misc[33:34]
    )
    token_grad[...] = (back + resid_grad[...]).astype(BF16)
    out_reduce.sent()
    w_reduce.sent()
    for reduce in (term_reduce, proj_reduce, attn_reduce):
        reduce.sent()
    for copy in (*mg_copies, *f_copies):
        copy.wait_send()


def finish(args, collective_id):
    anywhere = pl.BlockSpec(memory_space=pl.ANY)
    dma = pltpu.SemaphoreType.DMA
    outs = [
        ((256, 1024), BF16),
        ((256, 1024), BF16),
        ((8, 8, 384), F32),
        ((8, 1024), F32),
        ((2, 128, 512), F32),
        ((2, 128, 512), F32),
        ((2, 512, 128), F32),
    ]
    return pl.pallas_call(
        finish_kernel,
        out_shape=[jax.ShapeDtypeStruct(s, t) for s, t in outs],
        in_specs=[vmem()] * 18 + [anywhere] * 3,
        out_specs=[vmem()] * len(outs),
        scratch_shapes=[
            VMEM((64, 256, 256), BF16),
            VMEM((60, 256, 256), BF16),
            VMEM((4, 6, 128, 512), BF16),
            VMEM((4, 6, 128, 512), BF16),
            VMEM((3, 6, 128, 512), BF16),
            VMEM((256, 1024), BF16),
            VMEM((256, 1024), F32),
            VMEM((8, 256, 128), BF16),
            VMEM((8, 256, 128), BF16),
            VMEM((8, 128, 1024), BF16),
            VMEM((4, 128, 1024), BF16),
            VMEM((3, 128, 1024), BF16),
            VMEM((8, 512, 64), BF16),
            VMEM((8, 64, 512), BF16),
            VMEM((8, 1, 512), F32),
            VMEM((8, 64, 512), F32),
            VMEM((8, 256, 256), BF16),
            VMEM((8, 256, 1024), BF16),
            VMEM((4, 256, 1024), BF16),
            VMEM((3, 256, 1024), BF16),
            VMEM((8, 16, 8, 256), F32),
            VMEM((40, 1024), F32),
            VMEM((64, 32, 256), BF16),
            VMEM((60, 32, 256), BF16),
            VMEM((8, 128, 128), F32),
            VMEM((8, 8, 384), F32),
            VMEM((8, 8, 384), F32),
            VMEM((2, 256, 1024), BF16),
            dma((40,)),
            dma((40,)),
            dma((40,)),
            dma((40,)),
            dma((3, 8)),
            dma((3, 8)),
            dma((2, 7)),
            dma((2, 7)),
            dma((5,)),
            dma((2,)),
        ],
        compiler_params=pltpu.CompilerParams(
            collective_id=collective_id, has_side_effects=True, vmem_limit_bytes=62 << 20
        ),
    )(*args)


def per_device(
    tokens,
    norm_attn,
    w_query,
    w_key,
    w_value,
    w_out,
    norm_moe,
    w_router,
    w_gate,
    w_up,
    w_down,
    routes,
    cotangent,
):
    by_head = jnp.concatenate(
        [w_query.reshape(8, 8, 128), w_key.reshape(8, 8, 64), w_value.reshape(8, 8, 64)], axis=2
    ).transpose(1, 0, 2)
    narrow = jnp.concatenate([w_router, norm_moe[:, None], norm_attn[:, None]], axis=1)
    narrow = jnp.broadcast_to(jnp.pad(narrow, ((0, 0), (0, 94))), (8, 8, 128))
    pieces = jnp.concatenate(
        [by_head[:, :, :128], by_head[:, :, 128:], narrow, jnp.zeros_like(narrow)], axis=1
    )
    out_piece = w_out.reshape(8, 8, 128).transpose(1, 0, 2).reshape(64, 128)
    route_rows = routes[0].T.reshape(8, 2, 128).transpose(1, 0, 2).reshape(16, 128)
    route_rows = jnp.pad(route_rows.astype(BF16), ((0, 48), (0, 0)))
    (
        attn_in, q_t, q_s, k_s, k_t, v_s, lse, exact, mixed_rows,
        head_weights, misc_t, full_out, resid, moe_in, all_cot, all_routes, all_experts,
    ) = start(
        tokens[0], cotangent[0], w_gate, w_up, w_down, pieces, out_piece, route_rows, 1
    )
    grad_total, out_parts, expert_terms = moe_block(
        moe_in, misc_t, all_routes, all_cot, all_experts, 2
    )
    router = misc_t[:32].astype(BF16).reshape(16, 2, 1024).transpose(1, 0, 2).reshape(32, 1024)
    output, token_grad, head_sum, out_sum, gate_sum, up_sum, down_sum = finish(
        (
            grad_total, resid, misc_t, router, all_routes, moe_in, cotangent[0], tokens[0],
            full_out, mixed_rows, q_t, q_s, k_s, k_t, v_s, lse, exact, head_weights, attn_in,
            out_parts.reshape(64, 256, 256), expert_terms,
        ),
        3,
    )
    query_sum = head_sum[:, :, :128].transpose(1, 0, 2).reshape(8, 1024)
    key_sum = head_sum[:, :, 128:192].transpose(1, 0, 2).reshape(8, 512)
    value_sum = head_sum[:, :, 192:256].transpose(1, 0, 2).reshape(8, 512)
    small_sum = jnp.sum(head_sum[:, :, 256:], axis=0)
    router_sum = small_sum[:, :32].reshape(8, 2, 16).transpose(0, 2, 1).reshape(8, 32)
    norm_attn_sum = (
        jnp.sum(query_sum * w_query.astype(F32), axis=1)
        + jnp.sum(key_sum * w_key.astype(F32), axis=1)
        + jnp.sum(value_sum * w_value.astype(F32), axis=1)
    ) / norm_attn.astype(F32)
    return (
        output[None],
        token_grad[None],
        norm_attn_sum,
        query_sum,
        key_sum,
        value_sum,
        out_sum,
        small_sum[:, 32],
        router_sum,
        gate_sum,
        up_sum,
        down_sum,
    )


def solution(mesh):
    in_specs = (
        P("exp", "ctx", None),
        P(("ctx", "exp")),
        P(("ctx", "exp"), None),
        P(("ctx", "exp"), None),
        P(("ctx", "exp"), None),
        P(("ctx", "exp"), None),
        P(("ctx", "exp")),
        P(("ctx", "exp"), None),
        P("exp", "ctx", None),
        P("exp", "ctx", None),
        P("exp", None, "ctx"),
        P("exp", "ctx", None),
        P("exp", "ctx", None),
    )
    out_specs = (
        P("exp", "ctx", None),
        P("exp", "ctx", None),
        P(("ctx", "exp")),
        P(("ctx", "exp"), None),
        P(("ctx", "exp"), None),
        P(("ctx", "exp"), None),
        P(("ctx", "exp"), None),
        P(("ctx", "exp")),
        P(("ctx", "exp"), None),
        P("exp", "ctx", None),
        P("exp", "ctx", None),
        P("exp", None, "ctx"),
    )
    return jax.shard_map(
        per_device, mesh=mesh, in_specs=in_specs, out_specs=out_specs, check_vma=False
    )
```

```python
import jax
import jax.numpy as jnp
from jax import lax
from jax.experimental import pallas as pl
from jax.experimental.pallas import tpu as pltpu
from jax.sharding import PartitionSpec as P

EPSILON = 1e-06
PRECISE = lax.Precision.HIGHEST
F32, BF16 = jnp.float32, jnp.bfloat16
VMEM = pltpu.VMEM
MESH = pl.DeviceIdType.MESH
SIDE = 4
ROWS = 256
CAP = 96
GROUP = 4


def exp_block(first, second, half, inner):
    index = lax.axis_index("exp")
    z, x = lax.div(index, SIDE), lax.rem(index, SIDE)
    by_x, by_z = (first, second) if half == inner else (second, first)
    return lax.rem(z + by_z + SIDE, SIDE) * SIDE + lax.rem(x + by_x + SIDE, SIDE)


def greet_exp():
    barrier = pltpu.get_barrier_semaphore()
    for half in range(2):
        for step in (1, -1):
            pl.semaphore_signal(
                barrier, inc=1, device_id={"exp": exp_block(step, 0, half, 0)}, device_id_type=MESH
            )
    pl.semaphore_wait(barrier, 4)


def gather_exp_copy(own, out, send, recv, rows, half, axis, k, s):
    part = rows // 4
    step = (1, -1, 1, -1)[s]
    off = (0, 0, -1, 1)[s]
    origin = exp_block(off, 0, half, 0) if axis == 1 else exp_block(k, off, half, 0)
    target = exp_block(step, 0, half, 0) if axis == 1 else exp_block(0, step, half, 0)
    lines = (
        pl.ds(half * 2 * part, 2 * part)
        if s < 2
        else pl.ds((half * 2 + s - 2) * part, part)
    )
    mine = s < 2 and (axis == 1 or k == 0)
    at = half * 20 + (s if axis == 1 else 4 + 4 * (k % 4) + s)
    return pltpu.make_async_remote_copy(
        src_ref=own.at[lines] if mine else out.at[origin, lines],
        dst_ref=out.at[origin, lines],
        send_sem=send.at[at],
        recv_sem=recv.at[at],
        device_id={"exp": target},
        device_id_type=MESH,
    )


def gather_exp_kernel(own, out, send, recv, local):
    rows = own.shape[0]
    greet_exp()
    copies = {
        (half, axis, k, s): gather_exp_copy(own, out, send, recv, rows, half, axis, k, s)
        for half in range(2)
        for axis, k in ((1, 0), (2, 0), (2, 1), (2, -1), (2, 2))
        for s in range(4)
    }
    keep = pltpu.make_async_copy(own, out.at[exp_block(0, 0, 0, 0)], local)
    keep.start()
    for axis in (1, 2):
        for s in (0, 1):
            for half in range(2):
                copies[half, axis, 0, s].start()
    for s, k in ((0, -1), (1, 1)):
        for half in range(2):
            copies[half, 1, 0, s].wait_recv()
            copies[half, 1, 0, s + 2].start()
            copies[half, 2, k, 0].start()
            copies[half, 2, k, 1].start()
    for s in (0, 1):
        for half in range(2):
            copies[half, 2, 0, s].wait_recv()
            copies[half, 2, 0, s + 2].start()
    for half in range(2):
        copies[half, 1, 0, 2].wait_recv()
        copies[half, 1, 0, 3].wait_recv()
        copies[half, 2, 2, 0].start()
        copies[half, 2, 2, 1].start()
    for k in (-1, 1, 2):
        for s in (0, 1):
            for half in range(2):
                copies[half, 2, k, s].wait_recv()
                copies[half, 2, k, s + 2].start()
    for k in (0, -1, 1, 2):
        for s in (2, 3):
            for half in range(2):
                copies[half, 2, k, s].wait_recv()
    for copy in copies.values():
        copy.wait_send()
    keep.wait()


def gather_exp(block, collective_id):
    rows, width = block.shape
    return pl.pallas_call(
        gather_exp_kernel,
        out_shape=jax.ShapeDtypeStruct((16, rows, width), block.dtype),
        in_specs=[pl.BlockSpec(memory_space=pl.ANY)],
        out_specs=pl.BlockSpec(memory_space=pl.ANY),
        scratch_shapes=[
            pltpu.SemaphoreType.DMA((40,)),
            pltpu.SemaphoreType.DMA((40,)),
            pltpu.SemaphoreType.DMA,
        ],
        compiler_params=pltpu.CompilerParams(collective_id=collective_id, has_side_effects=True),
    )(block)


def reduce_exp_copy(parts, landed, send, recv, half, axis, k, s):
    step = (1, -1, 1, -1)[s]
    dest = (2, 2, 1, -1)[s]
    block = exp_block(dest, k, half, 1) if axis == 1 else exp_block(0, dest, half, 1)
    target = exp_block(step, 0, half, 1) if axis == 1 else exp_block(0, step, half, 1)
    row = half * 5 + (k % 4 if axis == 1 else 4)
    source = (
        parts.at[block, pl.ds(2 * half + s, 1)] if s < 2 else parts.at[block, pl.ds(2 * half, 2)]
    )
    place = (pl.ds(0, 1), pl.ds(1, 1), pl.ds(2, 2), pl.ds(4, 2))[s]
    at = row * 4 + s
    return pltpu.make_async_remote_copy(
        src_ref=source,
        dst_ref=landed.at[row, place],
        send_sem=send.at[at],
        recv_sem=recv.at[at],
        device_id={"exp": target},
        device_id_type=MESH,
    )


def add_lines(total, others, step):
    lines = total.shape[0]

    @pl.loop(0, lines // step)
    def _(i):
        at = pl.ds(pl.multiple_of(i * step, step), step)
        value = total[at].astype(jnp.float32)
        for other in others:
            value = value + other[at].astype(jnp.float32)
        total[at] = value.astype(total.dtype)


def reduce_exp_kernel(given, out, parts, landed, send, recv, local, done):
    greet_exp()
    lines = given.shape[2]
    step = 16
    load = pltpu.make_async_copy(given, parts, local)
    load.start()
    load.wait()
    copies = {
        (half, axis, k, s): reduce_exp_copy(parts, landed, send, recv, half, axis, k, s)
        for half in range(2)
        for axis, k in ((1, 0), (1, 1), (1, -1), (1, 2), (2, 0))
        for s in range(4)
    }

    def row_of(half, axis, k):
        return half * 5 + (k % 4 if axis == 1 else 4)

    def block_of(half, axis, k, dest):
        return exp_block(dest, k, half, 1) if axis == 1 else exp_block(0, dest, half, 1)

    def pass_on(half, axis, k):
        for s, dest in ((0, 1), (1, -1)):
            copies[half, axis, k, s].wait_recv()
            add_lines(
                parts.at[block_of(half, axis, k, dest), 2 * half + s],
                [landed.at[row_of(half, axis, k), s]],
                step,
            )
            copies[half, axis, k, s + 2].start()

    def finish(half, axis, k):
        copies[half, axis, k, 2].wait_recv()
        copies[half, axis, k, 3].wait_recv()
        for part in range(2):
            add_lines(
                parts.at[block_of(half, axis, k, 0), 2 * half + part],
                [
                    landed.at[row_of(half, axis, k), 2 + part],
                    landed.at[row_of(half, axis, k), 4 + part],
                ],
                step,
            )

    order = (2, 1, -1, 0)
    for k in order:
        for half in range(2):
            for s in (0, 1):
                copies[half, 1, k, s].start()
    for k in order:
        for half in range(2):
            pass_on(half, 1, k)
    for k in order:
        for half in range(2):
            finish(half, 1, k)
            if k == 2:
                copies[half, 2, 0, 0].start()
                copies[half, 2, 0, 1].start()
    for half in range(2):
        pass_on(half, 2, 0)
    for half in range(2):
        finish(half, 2, 0)
    store = pltpu.make_async_copy(parts.at[exp_block(0, 0, 0, 0)], out, done)
    store.start()
    for copy in copies.values():
        copy.wait_send()
    store.wait()


def reduce_exp(parts, collective_id):
    _, quarters, lines, width = parts.shape
    return pl.pallas_call(
        reduce_exp_kernel,
        out_shape=jax.ShapeDtypeStruct((quarters, lines, width), parts.dtype),
        in_specs=[pl.BlockSpec(memory_space=pl.ANY)],
        out_specs=pl.BlockSpec(memory_space=pl.ANY),
        scratch_shapes=[
            pltpu.VMEM(parts.shape, parts.dtype),
            pltpu.VMEM((10, 6, lines, width), parts.dtype),
            pltpu.SemaphoreType.DMA((40,)),
            pltpu.SemaphoreType.DMA((40,)),
            pltpu.SemaphoreType.DMA,
            pltpu.SemaphoreType.DMA,
        ],
        compiler_params=pltpu.CompilerParams(
            collective_id=collective_id, has_side_effects=True, vmem_limit_bytes=40 << 20
        ),
    )(parts)


def ctx_block(step, other):
    index = lax.axis_index("ctx")
    y, core = lax.div(index, 2), lax.rem(index, 2)
    if other:
        core = 1 - core
    return lax.rem(y + step + SIDE, SIDE) * 2 + core


def greet_ctx():
    barrier = pltpu.get_barrier_semaphore()
    for step, other in ((1, False), (-1, False), (0, True)):
        pl.semaphore_signal(
            barrier, inc=1, device_id={"ctx": ctx_block(step, other)}, device_id_type=MESH
        )
    pl.semaphore_wait(barrier, 3)


def gather_ctx_copies(own, out, send, recv):
    half = own.shape[0] // 2
    every, first, second = pl.ds(0, 2 * half), pl.ds(0, half), pl.ds(half, half)
    plan = (
        (0, every, 0, True),
        (0, first, 1, False),
        (0, second, -1, False),
        (0, second, 1, False),
        (0, first, -1, False),
        (-1, first, 1, False),
        (1, second, -1, False),
        (-1, first, 0, True),
        (-1, second, 0, True),
        (1, second, 0, True),
        (1, first, 0, True),
        (2, first, 0, True),
        (2, second, 0, True),
    )
    copies = []
    for at, (origin, lines, step, other) in enumerate(plan):
        slot = out.at[ctx_block(origin, False), lines]
        copies.append(
            pltpu.make_async_remote_copy(
                src_ref=own.at[lines] if origin == 0 else slot,
                dst_ref=slot,
                send_sem=send.at[at],
                recv_sem=recv.at[at],
                device_id={"ctx": ctx_block(step, other)},
                device_id_type=MESH,
            )
        )
    return copies


RING_START = (1, 2, 3, 4, 0)
RING_FOLLOW = {1: (5, 7), 2: (6, 9), 3: (8,), 4: (10,), 5: (11,), 6: (12,)}


def ring_follow(copies, *arrivals):
    for arrival in arrivals:
        copies[arrival].wait_recv()
        for at in RING_FOLLOW[arrival]:
            copies[at].start()


def dot(a, b, dims=((1,), (0,))):
    return lax.dot_general(a, b, (dims, ((), ())), preferred_element_type=F32)


def vmem(shape=None, index=None):
    return pl.BlockSpec(memory_space=VMEM)


def whole(*shape):
    return pl.BlockSpec(shape, lambda *_: (0,) * len(shape), pipeline_mode=pl.Buffered(1))


def side_by_side(a):
    return jnp.concatenate([a[:64], a[64:]], axis=1)


def one_below(a):
    return jnp.concatenate([a[:, :64], a[:, 64:]], axis=0)


def attend_kernel(
    tokens, gain, weights, attn_in, q_t, q_s, k_s, k_t, v_s, v_t, lse, exact, mixed
):
    scale = gain[...]

    @pl.loop(0, 8)
    def _(i):
        at = pl.ds(pl.multiple_of(i * ROWS, ROWS), ROWS)
        x = tokens[at].astype(F32)
        x = x * lax.rsqrt(jnp.mean(x * x, axis=1, keepdims=True) + EPSILON) * scale
        x = x.astype(BF16)
        attn_in[at] = x
        qkv = dot(x, weights[...]).astype(BF16).astype(F32)
        q = qkv[:, :128] * 0.125
        k, v = qkv[:, 128:192], qkv[:, 192:]
        q_s[i] = one_below(q).astype(BF16)
        q_t[i] = side_by_side(q.T).astype(BF16)
        k_s[i] = k.astype(BF16)
        v_s[i] = v.astype(BF16)
        kv_t = qkv[:, 128:].T
        k_t[i] = kv_t[:64].astype(BF16)
        v_t[i] = kv_t[64:].astype(BF16)

    key_row = lax.broadcasted_iota(jnp.int32, (ROWS, 2 * ROWS), 0)
    query_row = lax.rem(lax.broadcasted_iota(jnp.int32, (ROWS, 2 * ROWS), 1), ROWS)
    seen = key_row <= query_row

    @pl.loop(0, 8)
    def _(i):
        query = q_t[i]

        def add_block(j, carry, diagonal):
            top, total, acc = carry
            scores = dot(k_s[j], query)
            if diagonal:
                scores = jnp.where(seen, scores, -1e30)
            new_top = jnp.maximum(top, jnp.max(scores, axis=0, keepdims=True))
            fade = jnp.exp(top - new_top)
            weights = jnp.exp(scores - new_top)
            total = total * fade + jnp.sum(weights, axis=0, keepdims=True)
            acc = acc * fade + dot(v_t[j], weights.astype(BF16))
            return new_top, total, acc

        carry = (
            jnp.full((1, 2 * ROWS), -1e30, F32),
            jnp.zeros((1, 2 * ROWS), F32),
            jnp.zeros((64, 2 * ROWS), F32),
        )
        carry = lax.fori_loop(0, i, lambda j, c: add_block(j, c, False), carry)
        top, total, acc = add_block(i, carry, True)
        lse[i] = top + jnp.log(total)
        value = acc / total
        exact[i] = value
        both = jnp.concatenate([value[:, :ROWS], value[:, ROWS:]], axis=0)
        at = pl.ds(pl.multiple_of(i * ROWS, ROWS), ROWS)
        mixed[at] = both.T.astype(BF16)


def attend(tokens, gain, weights):
    shapes = [
        ((2048, 1024), BF16),
        ((8, 64, 512), BF16),
        ((8, 512, 64), BF16),
        ((8, 256, 64), BF16),
        ((8, 64, 256), BF16),
        ((8, 256, 64), BF16),
        ((8, 64, 256), BF16),
        ((8, 1, 512), F32),
        ((8, 64, 512), F32),
        ((2048, 128), BF16),
    ]
    return pl.pallas_call(
        attend_kernel,
        out_shape=[jax.ShapeDtypeStruct(s, t) for s, t in shapes],
        in_specs=[vmem()] * 3,
        out_specs=[vmem()] * len(shapes),
        compiler_params=pltpu.CompilerParams(vmem_limit_bytes=50 << 20),
    )(tokens, gain, weights)


def attend_back_kernel(
    mixed_grad, q_t, q_s, k_s, k_t, v_s, lse, exact, d, out_s, out_t, delta, dq
):
    @pl.loop(0, 8)
    def _(i):
        at = pl.ds(pl.multiple_of(i * ROWS, ROWS), ROWS)
        g = mixed_grad[at].astype(F32)
        out_s[i] = one_below(g).astype(BF16)
        g = side_by_side(g.T)
        out_t[i] = g.astype(BF16)
        delta[i] = jnp.sum(g * exact[i], axis=0, keepdims=True)
        dq[i] = jnp.zeros_like(dq[i])

    key_row = lax.broadcasted_iota(jnp.int32, (ROWS, 2 * ROWS), 0)
    query_row = lax.rem(lax.broadcasted_iota(jnp.int32, (ROWS, 2 * ROWS), 1), ROWS)
    seen = key_row <= query_row

    @pl.loop(0, 8)
    def _(j):
        key, key_t, value = k_s[j], k_t[j], v_s[j]

        def add_block(i, carry, diagonal):
            dk, dv = carry
            probs = jnp.exp(dot(key, q_t[i]) - lse[i])
            if diagonal:
                probs = jnp.where(seen, probs, 0.0)
            grad = probs * (dot(value, out_t[i]) - delta[i])
            grad = grad.astype(BF16)
            dv = dv + dot(probs.astype(BF16), out_s[i])
            dk = dk + dot(grad, q_s[i])
            dq[i] += dot(key_t, grad)
            return dk, dv

        zero = jnp.zeros((ROWS, 64), F32)
        carry = add_block(j, (zero, zero), True)
        dk, dv = lax.fori_loop(j + 1, 8, lambda i, c: add_block(i, c, False), carry)
        at = pl.ds(pl.multiple_of(j * ROWS, ROWS), ROWS)
        d[at, 128:256] = jnp.concatenate([dk, dv], axis=1).astype(BF16)

    @pl.loop(0, 8)
    def _(i):
        at = pl.ds(pl.multiple_of(i * ROWS, ROWS), ROWS)
        g = dq[i] * 0.125
        g = jnp.concatenate([g[:, :ROWS], g[:, ROWS:]], axis=0)
        d[at, 0:128] = g.T.astype(BF16)


def attend_back(mixed_grad, q_t, q_s, k_s, k_t, v_s, lse, exact):
    return pl.pallas_call(
        attend_back_kernel,
        out_shape=jax.ShapeDtypeStruct((2048, 256), BF16),
        in_specs=[vmem()] * 8,
        out_specs=vmem(),
        scratch_shapes=[
            VMEM((8, 512, 64), BF16),
            VMEM((8, 64, 512), BF16),
            VMEM((8, 1, 512), F32),
            VMEM((8, 64, 512), F32),
        ],
        compiler_params=pltpu.CompilerParams(vmem_limit_bytes=50 << 20),
    )(mixed_grad, q_t, q_s, k_s, k_t, v_s, lse, exact)


def experts_kernel(
    owner, moe, cot, routes, misc, weights,
    out_parts, grad_parts, rows, slot_grads, hidden, gate_grads, up_grads,
):
    own = owner[0]
    router = misc[0:32].astype(BF16)
    listed = [routes[b].astype(jnp.int32) for b in range(GROUP)]
    listed = [jnp.concatenate([r[:8], r[8:]], axis=1) for r in listed]

    def matrix(kind, k):
        return weights[:, 2 * kind + k].reshape(1024, 512)

    expert = lax.broadcasted_iota(jnp.int32, (32, ROWS), 0)
    named = [[None, None] for _ in range(GROUP)]
    gates = [[None, None] for _ in range(GROUP)]
    for b in range(GROUP):
        logits = dot(router, moe[b], ((1,), (1,)))
        chosen = expert < 0
        for j in range(8):
            chosen = chosen | (listed[b][j : j + 1] == expert)
        logits = jnp.where(chosen, logits, -1e30)
        weight = jnp.where(chosen, jnp.exp(logits - jnp.max(logits, axis=0, keepdims=True)), 0.0)
        weight = weight / jnp.sum(weight, axis=0, keepdims=True)
        for k in range(2):
            mine = expert == 2 * own + k
            gates[b][k] = jnp.sum(jnp.where(mine, weight, 0.0), axis=0, keepdims=True)
            named[b][k] = jnp.sum(
                jnp.where(mine & chosen, 1.0, 0.0), axis=0, keepdims=True
            )
    before = lax.broadcasted_iota(jnp.int32, (ROWS, ROWS), 0) < lax.broadcasted_iota(
        jnp.int32, (ROWS, ROWS), 1
    )
    flat = jnp.concatenate([named[b][k] for b in range(GROUP) for k in range(2)], axis=0)
    place = dot(flat.astype(BF16), before.astype(BF16))
    slot = lax.broadcasted_iota(jnp.int32, (CAP, ROWS), 0).astype(F32)
    spread = [[None, None] for _ in range(GROUP)]
    slot_gates = [[None, None] for _ in range(GROUP)]
    for b in range(GROUP):
        for k in range(2):
            at = 2 * b + k
            hit = (slot == place[at : at + 1]) & (flat[at : at + 1] > 0.5)
            spread[b][k] = jnp.where(hit, 1.0, 0.0).astype(BF16)
            slot_gates[b][k] = jnp.sum(
                jnp.where(hit, gates[b][k], 0.0), axis=1, keepdims=True
            )
    pick = [jnp.concatenate(spread[b], axis=0) for b in range(GROUP)]
    cots = [None] * GROUP
    for b in range(GROUP):
        both = dot(pick[b], moe[b]).astype(BF16)
        rows[0, b] = both[:CAP]
        rows[1, b] = both[CAP:]
        cots[b] = dot(pick[b], cot[b])
        for k in range(2):
            slot_grads[k, b] = (slot_gates[b][k] * cots[b][k * CAP : (k + 1) * CAP]).astype(BF16)
    gated = [None, None]
    row_grads = [None, None]
    weight_grads = [None, None]
    for k in range(2):
        x = rows[k].reshape(GROUP * CAP, 1024)
        dy = slot_grads[k].reshape(GROUP * CAP, 1024)
        g = dot(x, matrix(0, k))
        u = dot(x, matrix(1, k))
        s = jax.nn.sigmoid(g)
        silu = g * s
        h = (silu * u).astype(BF16)
        hidden[k] = h.reshape(GROUP, CAP, 512)
        y = dot(h, matrix(2, k), ((1,), (1,))).astype(BF16).astype(F32)
        gate = jnp.concatenate([slot_gates[b][k] for b in range(GROUP)], axis=0)
        gated[k] = (gate * y).astype(BF16)
        upstream = jnp.concatenate(
            [cots[b][k * CAP : (k + 1) * CAP] for b in range(GROUP)], axis=0
        )
        weight_grads[k] = jnp.sum(upstream * y, axis=1, keepdims=True)
        dh = dot(dy, matrix(2, k))
        gg = (dh * u * s * (1.0 + g * (1.0 - s))).astype(BF16)
        ug = (dh * silu).astype(BF16)
        gate_grads[k] = gg.reshape(GROUP, CAP, 512)
        up_grads[k] = ug.reshape(GROUP, CAP, 512)
        row_grads[k] = (
            dot(gg, matrix(0, k), ((1,), (1,))) + dot(ug, matrix(1, k), ((1,), (1,)))
        ).astype(BF16)
    owner_row = lax.broadcasted_iota(jnp.int32, (16, ROWS), 0) == own
    for b in range(GROUP):
        at = slice(b * CAP, (b + 1) * CAP)
        for source, target in ((gated, out_parts), (row_grads, grad_parts)):
            both = jnp.concatenate([source[0][at], source[1][at]], axis=0)
            total = dot(pick[b], both, ((0,), (0,))).astype(BF16)
            for q in range(4):
                target[b, q, 0:ROWS] = total[:, q * 256 : (q + 1) * 256]
        for k in range(2):
            vector = jnp.sum(
                spread[b][k].astype(F32) * weight_grads[k][at], axis=0, keepdims=True
            )
            high = vector.astype(BF16)
            low = (vector - high.astype(F32)).astype(BF16)
            grad_parts[b, 2 * k, ROWS : ROWS + 16] = jnp.where(
                owner_row, high.astype(F32), 0.0
            ).astype(BF16)
            grad_parts[b, 2 * k + 1, ROWS : ROWS + 16] = jnp.where(
                owner_row, low.astype(F32), 0.0
            ).astype(BF16)


def experts(owner, moe, cot, routes, misc, weights):
    steps = 16 // GROUP

    def block(*shape, dim=0):
        def index(g, owner):
            return tuple(g if i == dim else 0 for i in range(len(shape)))

        return pl.BlockSpec(shape, index)

    outs = [
        ((16, 4, 256, 256), BF16),
        ((16, 4, 272, 256), BF16),
        ((2, 16, CAP, 1024), BF16),
        ((2, 16, CAP, 1024), BF16),
        ((2, 16, CAP, 512), BF16),
        ((2, 16, CAP, 512), BF16),
        ((2, 16, CAP, 512), BF16),
    ]
    return pl.pallas_call(
        experts_kernel,
        grid_spec=pltpu.PrefetchScalarGridSpec(
            num_scalar_prefetch=1,
            grid=(steps,),
            in_specs=[
                block(GROUP, 256, 1024),
                block(GROUP, 256, 1024),
                block(GROUP, 16, 128),
                whole(40, 1024),
                whole(8, 6, 128, 512),
            ],
            out_specs=[
                block(GROUP, 4, 256, 256),
                block(GROUP, 4, 272, 256),
                block(2, GROUP, CAP, 1024, dim=1),
                block(2, GROUP, CAP, 1024, dim=1),
                block(2, GROUP, CAP, 512, dim=1),
                block(2, GROUP, CAP, 512, dim=1),
                block(2, GROUP, CAP, 512, dim=1),
            ],
        ),
        out_shape=[jax.ShapeDtypeStruct(s, t) for s, t in outs],
        compiler_params=pltpu.CompilerParams(vmem_limit_bytes=58 << 20),
    )(owner, moe, cot, routes, misc, weights)

PEERS = ((2, False), (2, True), (1, False), (1, True), (-1, False), (-1, True), (0, True))


def greet_signal(ctx_peers, exp_steps):
    barrier = pltpu.get_barrier_semaphore()
    for step, other in ctx_peers:
        pl.semaphore_signal(
            barrier, inc=1, device_id={"ctx": ctx_block(step, other)}, device_id_type=MESH
        )
    for first, second in exp_steps:
        pl.semaphore_signal(
            barrier, inc=1, device_id={"exp": exp_block(first, second, 0, 0)}, device_id_type=MESH
        )


def greet_wait(ctx_peers, exp_steps):
    pl.semaphore_wait(pltpu.get_barrier_semaphore(), len(ctx_peers) + len(exp_steps))


NEIGHBOURS = ((1, 0), (-1, 0), (0, 1), (0, -1))
LINES_OF = NEIGHBOURS + ((2, 0), (0, 2))
STEPS = (1, -1, 2)


def to_ctx(src, dst, send, recv, peer):
    return pltpu.make_async_remote_copy(
        src_ref=src,
        dst_ref=dst,
        send_sem=send,
        recv_sem=recv,
        device_id={"ctx": ctx_block(*peer)},
        device_id_type=MESH,
    )


def gather_exp_stages(own, out, send, recv):
    rows = own.shape[0]
    copies = {
        (half, axis, k, s): gather_exp_copy(own, out, send, recv, rows, half, axis, k, s)
        for half in range(2)
        for axis, k in ((1, 0), (2, 0), (2, 1), (2, -1), (2, 2))
        for s in range(4)
    }

    def begin():
        for axis in (1, 2):
            for s in (0, 1):
                for half in range(2):
                    copies[half, axis, 0, s].start()

    def first(s, k):
        for half in range(2):
            copies[half, 1, 0, s].wait_recv()
            copies[half, 1, 0, s + 2].start()
            copies[half, 2, k, 0].start()
            copies[half, 2, k, 1].start()

    def middle():
        for half in range(2):
            copies[half, 1, 0, 2].wait_recv()
            copies[half, 1, 0, 3].wait_recv()
            copies[half, 2, 2, 0].start()
            copies[half, 2, 2, 1].start()

    def forward(k):
        for s in (0, 1):
            for half in range(2):
                copies[half, 2, k, s].wait_recv()
                copies[half, 2, k, s + 2].start()

    def last():
        for k in (0, -1, 1, 2):
            for s in (2, 3):
                for half in range(2):
                    copies[half, 2, k, s].wait_recv()

    def sent():
        for copy in copies.values():
            copy.wait_send()

    steps = [
        begin,
        lambda: first(0, -1),
        lambda: first(1, 1),
        lambda: forward(0),
        middle,
        lambda: forward(-1),
        lambda: forward(1),
        lambda: forward(2),
        last,
    ]
    return steps, sent


def relay_exp_steps(own, out, send, recv):
    part = own.shape[0] // 2
    copies = {}
    for half in range(2):
        lines = pl.ds(half * part, part)
        for axis, k in ((1, 0), (2, 0), (2, 1), (2, -1), (2, 2)):
            origin = exp_block(k, 0, half, 0)
            for s, step in enumerate(STEPS):
                target = exp_block(step, 0, half, 0) if axis == 1 else exp_block(0, step, half, 0)
                at = half * 15 + (s if axis == 1 else 3 + 3 * (k % 4) + s)
                copies[half, axis, k, s] = pltpu.make_async_remote_copy(
                    src_ref=own.at[lines] if k == 0 else out.at[origin, lines],
                    dst_ref=out.at[origin, lines],
                    send_sem=send.at[at],
                    recv_sem=recv.at[at],
                    device_id={"exp": target},
                    device_id_type=MESH,
                )

    def begin():
        for axis in (1, 2):
            for s in range(3):
                for half in range(2):
                    copies[half, axis, 0, s].start()

    def relay():
        for s, k in ((0, -1), (1, 1), (2, 2)):
            for half in range(2):
                copies[half, 1, 0, s].wait_recv()
                for t in range(3):
                    copies[half, 2, k, t].start()

    def last():
        for half in range(2):
            for k in (0, -1, 1, 2):
                for s in range(3):
                    copies[half, 2, k, s].wait_recv()

    def sent():
        for copy in copies.values():
            copy.wait_send()

    return begin, relay, last, sent


def start_kernel(
    tokens, cot, w_gate, w_up, w_down, w_query, w_key, w_value, w_out, narrow, routes,
    attn_in, q_t, q_s, k_s, k_t, v_s, lse, exact, mixed_rows,
    head_w, misc_t, full_out, resid, moe_in, all_cot, all_routes, all_experts,
    land, own_experts, down_in, w_block, w_all, o_rows, o_all, w_wide, o_wide, misc, v_t, mixed, mixed_land, pieces, out_piece,
    exp_send, exp_recv, ctx_send, ctx_recv, ring_send, ring_recv, local,
):
    me = lax.axis_index("ctx")
    own = exp_block(0, 0, 0, 0)
    greet_signal(PEERS, LINES_OF)
    loads = [
        pltpu.make_async_copy(w_gate, own_experts.at[pl.ds(0, 2)], local.at[0]),
        pltpu.make_async_copy(w_up, own_experts.at[pl.ds(2, 2)], local.at[1]),
        pltpu.make_async_copy(w_down, down_in, local.at[2]),
        pltpu.make_async_copy(tokens, land.at[me], local.at[3]),
        pltpu.make_async_copy(cot, all_cot.at[own], local.at[4]),
    ]
    for load in loads:
        load.start()
    query = w_query[...].astype(F32)
    key = w_key[...].astype(F32)
    value = w_value[...].astype(F32)
    rest = jnp.concatenate([narrow[...], jnp.zeros((8, 128), F32)], axis=0).astype(BF16)
    for c in range(8):
        pair = [key[:, c * 64 : (c + 1) * 64], value[:, c * 64 : (c + 1) * 64]]
        columns = [query[:, c * 128 : (c + 1) * 128], jnp.concatenate(pair, axis=1)]
        pieces[c, 0:16] = jnp.concatenate(columns, axis=0).astype(BF16)
        pieces[c, 16:32] = rest
    wide = w_out[...].astype(F32)
    for t in range(4):
        columns = [wide[:, 256 * t : 256 * t + 128], wide[:, 256 * t + 128 : 256 * t + 256]]
        out_piece[t * 16 : (t + 1) * 16] = jnp.concatenate(columns, axis=0).astype(BF16)
    listed = jnp.concatenate([routes[...].astype(F32), jnp.zeros((ROWS, 120), F32)], axis=1).T[:8]
    listed = jnp.concatenate([listed[:, :128], listed[:, 128:]], axis=0)
    w_block[256:288] = jnp.concatenate([listed, jnp.zeros((16, 128), F32)], axis=0).astype(BF16)
    greet_wait(PEERS, LINES_OF)
    piece_copies = [
        to_ctx(
            pieces.at[ctx_block(*peer)], w_block.at[pl.ds(me * 32, 32)],
            ctx_send.at[0, at], ctx_recv.at[0, at], peer,
        )
        for at, peer in enumerate(PEERS)
    ]
    for copy in piece_copies:
        copy.start()
    ring = gather_ctx_copies(tokens, land, ring_send.at[0], ring_recv.at[0])
    for at in RING_START:
        ring[at].start()
    w_block[pl.ds(pl.multiple_of(me * 32, 32), 32)] = pieces[me]
    w_begin, w_relay, w_last, w_sent = relay_exp_steps(
        w_block, w_all, exp_send.at[0], exp_recv.at[0]
    )
    o_begin, o_relay, o_last, o_sent = relay_exp_steps(
        out_piece, o_rows, exp_send.at[1], exp_recv.at[1]
    )
    c_steps, c_sent = gather_exp_stages(cot, all_cot, exp_send.at[2], exp_recv.at[2])
    c_steps[0]()
    o_begin()
    o_rows[own] = out_piece[...]
    for copy in piece_copies:
        copy.wait_recv()
    w_begin()
    w_keep = pltpu.make_async_copy(w_block, w_all.at[own], local.at[5])
    w_keep.start()
    o_relay()
    w_relay()
    ring_follow(ring, 1, 2)
    for at in (0, 1, 2):
        loads[at].wait()
    for k in range(2):
        own_experts[4 + k] = down_in[k].astype(F32).T.astype(BF16)
    w_ring = gather_ctx_copies(own_experts, all_experts, ring_send.at[1], ring_recv.at[1])
    w_ring[1].start()
    w_ring[2].start()
    w_ring_keep = pltpu.make_async_copy(own_experts, all_experts.at[me], local.at[7])
    w_ring_keep.start()
    c_steps[1]()
    c_steps[2]()
    w_last()
    w_keep.wait()

    @pl.loop(0, 128)
    def _(i):
        x, c = lax.div(i, 8), lax.rem(i, 8)
        at = pl.ds(pl.multiple_of(c * 128 + x * 8, 8), 8)
        line = pl.multiple_of(c * 32, 32)
        first = w_all[x, pl.ds(line, 16)].astype(F32)
        second = w_all[x, pl.ds(line + 16, 16)].astype(F32)
        w_wide[at, 0:128] = first[:8]
        w_wide[at, 128:256] = first[8:]
        misc[at] = second[:8]

    all_routes[...] = w_all[:, 256:272]
    head_w[...] = w_wide[...].astype(BF16)

    @pl.loop(0, 8)
    def _(c):
        at = pl.ds(pl.multiple_of(c * 128, 128), 128)
        misc_t[:, at] = misc[at].T[:40]

    def project(i):
        at = pl.ds(pl.multiple_of(i * ROWS, ROWS), ROWS)
        x = land[i].astype(F32)
        x = x * lax.rsqrt(jnp.mean(x * x, axis=1, keepdims=True) + EPSILON) * misc_t[33:34]
        x = x.astype(BF16)
        attn_in[at] = x
        qkv = dot(x, head_w[...]).astype(BF16).astype(F32)
        q = qkv[:, :128] * 0.125
        k, v = qkv[:, 128:192], qkv[:, 192:]
        q_s[i] = one_below(q).astype(BF16)
        q_t[i] = side_by_side(q.T).astype(BF16)
        k_s[i] = k.astype(BF16)
        v_s[i] = v.astype(BF16)
        kv_t = qkv[:, 128:].T
        k_t[i] = kv_t[:64].astype(BF16)
        v_t[i] = kv_t[64:].astype(BF16)

    loads[3].wait()
    ring_follow(ring, 3, 4)
    for at in (3, 4, 0):
        w_ring[at].start()
    o_last()
    o_ring = gather_ctx_copies(o_rows, o_all, ring_send.at[2], ring_recv.at[2])
    for at in RING_START:
        o_ring[at].start()
    o_keep = pltpu.make_async_copy(o_rows, o_all.at[me], local.at[6])
    o_keep.start()
    c_steps[3]()
    project(ctx_block(0, False))
    ring[0].wait_recv()
    project(ctx_block(0, True))
    ring_follow(ring, 5, 6)
    c_steps[4]()
    ring_follow(w_ring, 1, 2)
    project(ctx_block(-1, False))
    project(ctx_block(1, False))
    for at in (7, 8):
        ring[at].wait_recv()
    project(ctx_block(-1, True))
    for at in (9, 10):
        ring[at].wait_recv()
    project(ctx_block(1, True))
    c_steps[5]()
    project(ctx_block(2, False))
    for at in (11, 12):
        ring[at].wait_recv()
    project(ctx_block(2, True))
    ring_follow(w_ring, 3, 4)
    c_steps[6]()

    key_row = lax.broadcasted_iota(jnp.int32, (ROWS, 2 * ROWS), 0)
    query_row = lax.rem(lax.broadcasted_iota(jnp.int32, (ROWS, 2 * ROWS), 1), ROWS)
    seen = key_row <= query_row

    def tile(i):
        query = q_t[i]

        def add_block(j, carry, diagonal):
            top, total, acc = carry
            scores = dot(k_s[j], query)
            if diagonal:
                scores = jnp.where(seen, scores, -1e30)
            new_top = jnp.maximum(top, jnp.max(scores, axis=0, keepdims=True))
            fade = jnp.exp(top - new_top)
            weights = jnp.exp(scores - new_top)
            total = total * fade + jnp.sum(weights, axis=0, keepdims=True)
            acc = acc * fade + dot(v_t[j], weights.astype(BF16))
            return new_top, total, acc

        carry = (
            jnp.full((1, 2 * ROWS), -1e30, F32),
            jnp.zeros((1, 2 * ROWS), F32),
            jnp.zeros((64, 2 * ROWS), F32),
        )
        carry = lax.fori_loop(0, i, lambda j, c: add_block(j, c, False), carry)
        top, total, acc = add_block(i, carry, True)
        lse[i] = top + jnp.log(total)
        value = acc / total
        exact[i] = value
        both = jnp.concatenate([value[:, :ROWS], value[:, ROWS:]], axis=0)
        mixed[i] = both.T.astype(BF16)

    def unpack_out():
        o_keep.wait()
        for at in (0, 7, 8, 9, 10, 11, 12):
            o_ring[at].wait_recv()

        @pl.loop(0, 128)
        def _(i):
            x, c = lax.div(i, 8), lax.rem(i, 8)
            at = pl.ds(pl.multiple_of(c * 128 + x * 8, 8), 8)
            for t in range(4):
                both = o_all[c, x, t * 16 : t * 16 + 16].astype(F32)
                o_wide[at, 256 * t : 256 * t + 128] = both[:8]
                o_wide[at, 256 * t + 128 : 256 * t + 256] = both[8:]

        full_out[...] = o_wide[...].astype(BF16)

    between = (
        (lambda: ring_follow(o_ring, 1, 2),),
        (c_steps[7], lambda: ring_follow(o_ring, 3, 4)),
        (lambda: ring_follow(w_ring, 5, 6), lambda: ring_follow(o_ring, 5, 6)),
        (),
        (),
        (unpack_out,),
        (),
    )
    mixed_copies = []
    for at, peer in enumerate(PEERS):
        i = ctx_block(*peer)
        tile(i)
        copy = to_ctx(
            mixed.at[i], mixed_land.at[me], ctx_send.at[2, at], ctx_recv.at[2, at], peer
        )
        copy.start()
        mixed_copies.append(copy)
        for step in between[at]:
            step()
    tile(me)
    mixed_land[me] = mixed[me]
    total = tokens[...].astype(F32)
    for copy in mixed_copies:
        copy.wait_recv()
    for c in range(4):
        pair = jnp.concatenate([mixed_land[2 * c], mixed_land[2 * c + 1]], axis=1)
        total = total + dot(pair, full_out[c * 256 : (c + 1) * 256])
    mixed_rows[...] = mixed_land[...]
    resid[...] = total
    scaled = total * lax.rsqrt(jnp.mean(total * total, axis=1, keepdims=True) + EPSILON)
    scaled = (scaled * misc_t[32:33]).astype(BF16)
    for q in range(4):
        moe_in[q] = scaled[:, q * 256 : (q + 1) * 256]
    c_steps[8]()
    for at in (0, 7, 8, 9, 10, 11, 12):
        w_ring[at].wait_recv()
    w_ring_keep.wait()
    loads[4].wait()
    w_sent()
    o_sent()
    c_sent()
    for copy in (*piece_copies, *ring, *w_ring, *o_ring, *mixed_copies):
        copy.wait_send()


def start(args, collective_id):
    anywhere = pl.BlockSpec(memory_space=pl.ANY)
    outs = [
        ((2048, 1024), BF16, vmem()),
        ((8, 64, 512), BF16, vmem()),
        ((8, 512, 64), BF16, vmem()),
        ((8, 256, 64), BF16, vmem()),
        ((8, 64, 256), BF16, vmem()),
        ((8, 256, 64), BF16, vmem()),
        ((8, 1, 512), F32, vmem()),
        ((8, 64, 512), F32, vmem()),
        ((8, 256, 128), BF16, vmem()),
        ((1024, 256), BF16, vmem()),
        ((40, 1024), F32, vmem()),
        ((1024, 1024), BF16, vmem()),
        ((256, 1024), F32, vmem()),
        ((4, 256, 256), BF16, vmem()),
        ((16, 256, 1024), BF16, anywhere),
        ((16, 16, 128), BF16, vmem()),
        ((8, 6, 128, 512), BF16, anywhere),
    ]
    dma = pltpu.SemaphoreType.DMA
    return pl.pallas_call(
        start_kernel,
        out_shape=[jax.ShapeDtypeStruct(s, t) for s, t, _ in outs],
        in_specs=[vmem()] + [anywhere] * 4 + [vmem()] * 6,
        out_specs=[spec for _, _, spec in outs],
        scratch_shapes=[
            VMEM((8, 256, 1024), BF16),
            VMEM((6, 128, 512), BF16),
            VMEM((2, 512, 128), BF16),
            VMEM((288, 128), BF16),
            VMEM((16, 288, 128), BF16),
            VMEM((16, 64, 128), BF16),
            VMEM((8, 16, 64, 128), BF16),
            VMEM((1024, 256), F32),
            VMEM((1024, 1024), F32),
            VMEM((1024, 128), F32),
            VMEM((8, 64, 256), BF16),
            VMEM((8, 256, 128), BF16),
            VMEM((8, 256, 128), BF16),
            VMEM((8, 32, 128), BF16),
            VMEM((64, 128), BF16),
            dma((3, 40)),
            dma((3, 40)),
            dma((3, 7)),
            dma((3, 7)),
            dma((3, 13)),
            dma((3, 13)),
            dma((8,)),
        ],
        compiler_params=pltpu.CompilerParams(
            collective_id=collective_id, has_side_effects=True, vmem_limit_bytes=56 << 20
        ),
    )(*args)

ORDER = (0, 2, 1, -1)
LINES = ROWS + 16


def part_gather_copies(own, held, send, recv):
    copies = {}
    for half in range(2):
        for axis, k in ((1, 0), (2, 0), (2, 1), (2, -1), (2, 2)):
            for s in range(4):
                step = (1, -1, 1, -1)[s]
                off = (0, 0, -1, 1)[s]
                origin = exp_block(off, 0, half, 0) if axis == 1 else exp_block(k, off, half, 0)
                target = exp_block(step, 0, half, 0) if axis == 1 else exp_block(0, step, half, 0)
                first, count = (2 * half, 2) if s < 2 else (2 * half + s - 2, 1)
                place = held.at[pl.ds(origin * 4 + first, count), pl.ds(0, ROWS)]
                mine = s < 2 and (axis == 1 or k == 0)
                at = half * 20 + (s if axis == 1 else 4 + 4 * (k % 4) + s)
                copies[half, axis, k, s] = pltpu.make_async_remote_copy(
                    src_ref=own.at[pl.ds(first, count)] if mine else place,
                    dst_ref=place,
                    send_sem=send.at[at],
                    recv_sem=recv.at[at],
                    device_id={"exp": target},
                    device_id_type=MESH,
                )
    return copies


def part_reduce_copies(parts, held, send, recv):
    copies = {}
    for half in range(2):
        for axis, k in ((1, 0), (1, 1), (1, -1), (1, 2), (2, 0)):
            row = half * 5 + (k % 4 if axis == 1 else 4)
            for s in range(4):
                step = (1, -1, 1, -1)[s]
                dest = (2, 2, 1, -1)[s]
                block = exp_block(dest, k, half, 1) if axis == 1 else exp_block(0, dest, half, 1)
                target = exp_block(step, 0, half, 1) if axis == 1 else exp_block(0, step, half, 1)
                first, count = (2 * half + s, 1) if s < 2 else (2 * half, 2)
                at = row * 4 + s
                copies[half, axis, k, s] = pltpu.make_async_remote_copy(
                    src_ref=parts.at[pl.ds(block * 4 + first, count)],
                    dst_ref=held.at[pl.ds(row * 6 + (0, 1, 2, 4)[s], count)],
                    send_sem=send.at[at],
                    recv_sem=recv.at[at],
                    device_id={"exp": target},
                    device_id_type=MESH,
                )
    return copies


def moe_kernel(
    moe, misc, routes, cot, experts, head_w,
    grad_total, out_parts, terms, all_w,
    held, parts, weights, cots, x_rows, c_rows, hidden, gate_g, up_g, pick,
    gated, row_g, stage, term_stage, slot_gates, slot_grads,
    gather_send, gather_recv, reduce_send, reduce_recv, cot_sem, stage_sem, term_sem, local, ready, ring_send, ring_recv,
):
    own = exp_block(0, 0, 0, 0)
    beside = ((1, False), (-1, False), (0, True))
    greet_signal(beside, NEIGHBOURS)

    def block_of(group, o):
        return exp_block(o, group, 0, 0)

    def cot_load(n, o):
        return pltpu.make_async_copy(cot.at[block_of(ORDER[n], o)], cots.at[o], cot_sem.at[o])

    weight_load = pltpu.make_async_copy(experts, weights, local.at[0])
    weight_load.start()
    for o in range(4):
        cot_load(0, o).start()
    keep = pltpu.make_async_copy(
        moe, held.at[pl.ds(own * 4, 4), pl.ds(0, ROWS)], local.at[1]
    )
    keep.start()
    w_keep = pltpu.make_async_copy(head_w, all_w.at[lax.axis_index("ctx")], local.at[2])
    w_keep.start()
    greet_wait(beside, NEIGHBOURS)
    ring = gather_ctx_copies(head_w, all_w, ring_send, ring_recv)
    gathers = part_gather_copies(moe, held, gather_send, gather_recv)
    reduces = part_reduce_copies(parts, held, reduce_send, reduce_recv)
    router = misc[0:32].astype(BF16)

    def listed_at(b):
        listed = routes[b].astype(F32).astype(jnp.int32)
        return jnp.concatenate([listed[:8], listed[8:]], axis=1)

    def prepare(n):
        before = lax.broadcasted_iota(jnp.int32, (ROWS, ROWS), 0) < lax.broadcasted_iota(
            jnp.int32, (ROWS, ROWS), 1
        )
        before = jnp.where(before, 1.0, 0.0).astype(BF16)
        slot = lax.broadcasted_iota(jnp.int32, (CAP, ROWS), 0).astype(F32)

        @pl.loop(0, 4)
        def _(o):
            listed = listed_at(block_of(ORDER[n], o))
            named = [
                jnp.sum(jnp.where(listed == 2 * own + k, 1.0, 0.0), axis=0, keepdims=True)
                for k in range(2)
            ]
            flat = jnp.concatenate(named + [jnp.zeros((6, ROWS), F32)], axis=0)
            place = dot(flat.astype(BF16), before)
            spread = []
            for k in range(2):
                hit = (slot == place[k : k + 1]) & (named[k] > 0.5)
                spread.append(jnp.where(hit, 1.0, 0.0).astype(BF16))
            both = jnp.concatenate(spread, axis=0)
            pick[n, o] = both
            cot_load(n, o).wait()
            for q in range(4):
                at = slice(q * 256, (q + 1) * 256)
                grads = dot(both, cots[o, :, at]).astype(BF16)
                for k in range(2):
                    c_rows[k, n, o, :, at] = grads[k * CAP : (k + 1) * CAP]
            if n < 3:
                cot_load(n + 1, o).start()

    def dispatch(n):
        expert = lax.broadcasted_iota(jnp.int32, (32, ROWS), 0)

        @pl.loop(0, 4)
        def _(o):
            b = block_of(ORDER[n], o)
            both = pick[n, o]
            logits = jnp.zeros((32, ROWS), F32)
            for q in range(4):
                rows = held[b * 4 + q, 0:ROWS]
                logits = logits + dot(router[:, q * 256 : (q + 1) * 256], rows, ((1,), (1,)))
                rows = dot(both, rows).astype(BF16)
                for k in range(2):
                    x_rows[k, n, o, :, q * 256 : (q + 1) * 256] = rows[k * CAP : (k + 1) * CAP]
            listed = listed_at(b)
            chosen = expert < 0
            for j in range(8):
                chosen = chosen | (listed[j : j + 1] == expert)
            logits = jnp.where(chosen, logits, -1e30)
            weight = jnp.exp(logits - jnp.max(logits, axis=0, keepdims=True))
            weight = jnp.where(chosen, weight, 0.0)
            weight = weight / jnp.sum(weight, axis=0, keepdims=True)
            lines = pl.ds(pl.multiple_of(o * CAP, CAP), CAP)
            for k in range(2):
                mine = jnp.where(expert == 2 * own + k, weight, 0.0)
                gate = jnp.sum(mine, axis=0, keepdims=True)
                hits = both[k * CAP : (k + 1) * CAP].astype(F32)
                slot_gates[n, k, lines] = jnp.sum(hits * gate, axis=1, keepdims=True)

    def matrix(kind, k):
        return weights[:, 2 * kind + k].reshape(1024, 512)

    def expert(n, k):
        x = x_rows[k, n].reshape(GROUP * CAP, 1024)
        c = c_rows[k, n].reshape(GROUP * CAP, 1024)
        gate = slot_gates[n, k]
        g = dot(x, matrix(0, k))
        u = dot(x, matrix(1, k))
        s = jax.nn.sigmoid(g)
        silu = g * s
        h = (silu * u).astype(BF16)
        hidden[k, n] = h
        y = dot(h, matrix(2, k), ((1,), (1,))).astype(BF16).astype(F32)
        gated[k] = (gate * y).astype(BF16)
        c = c.astype(F32)
        slot_grads[k] = jnp.sum(c * y, axis=1, keepdims=True)
        dy = (gate * c).astype(BF16)
        c_rows[k, n] = dy.reshape(GROUP, CAP, 1024)
        dh = dot(dy, matrix(2, k))
        gg = (dh * u * s * (1.0 + g * (1.0 - s))).astype(BF16)
        ug = (dh * silu).astype(BF16)
        gate_g[k, n] = gg
        up_g[k, n] = ug
        row_g[k] = (
            dot(gg, matrix(0, k), ((1,), (1,))) + dot(ug, matrix(1, k), ((1,), (1,)))
        ).astype(BF16)

    def stage_copy(b, o):
        slot = lax.rem(o, 2)
        return pltpu.make_async_copy(stage.at[slot], out_parts.at[b], stage_sem.at[slot])

    def combine(n, first=False):
        owner_row = lax.broadcasted_iota(jnp.int32, (16, ROWS), 0) == own

        @pl.loop(0, 4)
        def _(o):
            b = block_of(ORDER[n], o)
            lines = pl.ds(pl.multiple_of(o * CAP, CAP), CAP)
            chosen = pick[n, o]

            def spread(rows):
                both = jnp.concatenate([rows[0, lines], rows[1, lines]], axis=0)
                return dot(chosen, both, ((0,), (0,))).astype(BF16)

            total = spread(row_g)
            for q in range(4):
                parts[b * 4 + q, 0:ROWS] = total[:, q * 256 : (q + 1) * 256]
            for k in range(2):
                hits = chosen[k * CAP : (k + 1) * CAP].astype(F32)
                vector = jnp.sum(hits * slot_grads[k, lines], axis=0, keepdims=True)
                high = vector.astype(BF16).astype(F32)
                for q, value in ((2 * k, high), (2 * k + 1, vector - high)):
                    parts[b * 4 + q, ROWS:LINES] = jnp.where(owner_row, value, 0.0).astype(BF16)
            total = spread(gated)
            if first:

                @pl.when(o >= 2)
                def _():
                    stage_copy(b, o).wait()

            else:
                stage_copy(b, o).wait()
            slot = lax.rem(o, 2)
            for q in range(4):
                stage[slot, q] = total[:, q * 256 : (q + 1) * 256]
            stage_copy(b, o).start()

    def add(target, *landed):
        value = parts[target].astype(F32)
        for at in landed:
            value = value + held[at].astype(F32)
        parts[target] = value.astype(BF16)

    def row_of(half, axis, k):
        return (half * 5 + (k % 4 if axis == 1 else 4)) * 6

    def block_at(half, axis, k, dest):
        return exp_block(dest, k, half, 1) if axis == 1 else exp_block(0, dest, half, 1)

    def send_far(half, axis, k):
        reduces[half, axis, k, 0].start()
        reduces[half, axis, k, 1].start()

    def pass_on(half, axis, k, s):
        reduces[half, axis, k, s].wait_recv()
        block = block_at(half, axis, k, 1 - 2 * s)
        add(block * 4 + 2 * half + s, row_of(half, axis, k) + s)
        reduces[half, axis, k, s + 2].start()

    def finish(half, axis, k):
        reduces[half, axis, k, 2].wait_recv()
        reduces[half, axis, k, 3].wait_recv()
        row = row_of(half, axis, k)
        for part in range(2):
            target = block_at(half, axis, k, 0) * 4 + 2 * half + part
            add(target, row + 2 + part, row + 4 + part)

    def term_copy(kind, k, tile):
        return pltpu.make_async_copy(
            term_stage.at[tile], terms.at[pl.ds(2 * tile, 2), 2 * kind + k], term_sem.at[tile]
        )

    def term(kind, k, first=False):
        left = c_rows if kind == 2 else x_rows
        right = (gate_g, up_g, hidden)[kind]

        @pl.loop(0, 4)
        def _(tile):
            at = pl.ds(pl.multiple_of(tile * 256, 256), 256)
            rows = left[k, :, :, :, at].reshape(16 * CAP, 256)
            value = dot(rows, right[k].reshape(16 * CAP, 512), ((0,), (0,)))
            if not first:
                term_copy(kind, k, tile).wait()
            term_stage[tile] = value.astype(BF16).reshape(2, 128, 512)
            term_copy(kind, k, tile).start()

    def forward(k):
        for s in (0, 1):
            for half in range(2):
                gathers[half, 2, k, s].wait_recv()
                gathers[half, 2, k, s + 2].start()

    for axis in (1, 2):
        for s in (0, 1):
            for half in range(2):
                gathers[half, axis, 0, s].start()
    for at in RING_START:
        ring[at].start()
    prepare(0)
    for s, k in ((0, -1), (1, 1)):
        for half in range(2):
            gathers[half, 1, 0, s].wait_recv()
            gathers[half, 1, 0, s + 2].start()
            gathers[half, 2, k, 0].start()
            gathers[half, 2, k, 1].start()
    prepare(1)
    forward(0)
    for half in range(2):
        gathers[half, 1, 0, 2].wait_recv()
        gathers[half, 1, 0, 3].wait_recv()
        gathers[half, 2, 2, 0].start()
        gathers[half, 2, 2, 1].start()
    prepare(2)
    ring_follow(ring, 1, 2, 3, 4)
    forward(-1)
    prepare(3)
    forward(1)
    gathers[1, 2, 0, 2].wait_recv()
    gathers[1, 2, 0, 3].wait_recv()
    ring_follow(ring, 5, 6)
    keep.wait()
    weight_load.wait()
    dispatch(0)
    expert(0, 0)
    forward(2)
    expert(0, 1)
    combine(0, first=True)
    for half in range(2):
        for k in (0, -1, 1, 2):
            if (half, k) != (1, 0):
                gathers[half, 2, k, 2].wait_recv()
                gathers[half, 2, k, 3].wait_recv()
    dispatch(1)
    dispatch(2)
    dispatch(3)
    for copy in gathers.values():
        copy.wait_send()
    for first, second in NEIGHBOURS:
        pl.semaphore_signal(
            ready, inc=1, device_id={"exp": exp_block(first, second, 0, 0)}, device_id_type=MESH
        )
    expert(1, 0)
    expert(1, 1)
    combine(1)
    pl.semaphore_wait(ready, 4)
    send_far(1, 1, 2)
    send_far(0, 1, 2)
    send_far(0, 1, 1)
    send_far(0, 1, -1)
    send_far(0, 1, 0)
    send_far(1, 1, 0)
    expert(2, 0)
    pass_on(1, 1, 2, 0)
    pass_on(1, 1, 2, 1)
    expert(2, 1)
    combine(2)
    send_far(1, 1, 1)
    for k in (2, 1, -1, 0):
        pass_on(0, 1, k, 0)
    expert(3, 0)
    pass_on(1, 1, 0, 0)
    pass_on(1, 1, 0, 1)
    expert(3, 1)
    combine(3)
    send_far(1, 1, -1)
    for k in (2, 1, -1, 0):
        pass_on(0, 1, k, 1)
    pass_on(1, 1, 1, 0)
    pass_on(1, 1, 1, 1)
    term(0, 0, first=True)
    finish(1, 1, 2)
    send_far(1, 2, 0)
    pass_on(1, 1, -1, 0)
    pass_on(1, 1, -1, 1)
    term(0, 1)
    finish(0, 1, 2)
    send_far(0, 2, 0)
    finish(1, 1, 1)
    finish(0, 1, 1)
    term(1, 0)
    finish(1, 1, -1)
    finish(0, 1, -1)
    for half in (1, 0):
        pass_on(half, 2, 0, 0)
        pass_on(half, 2, 0, 1)
    term(1, 1)
    finish(1, 1, 0)
    finish(0, 1, 0)
    term(2, 0)
    term(2, 1)
    finish(1, 2, 0)
    finish(0, 2, 0)
    for q in range(4):
        grad_total[q] = parts[own * 4 + q]
    for copy in reduces.values():
        copy.wait_send()
    for at in (0, 7, 8, 9, 10, 11, 12):
        ring[at].wait_recv()
    for copy in ring:
        copy.wait_send()
    w_keep.wait()
    for o in range(2):
        stage_copy(own, o).wait()
    for tile in range(4):
        term_copy(0, 0, tile).wait()


def moe_block(moe, misc, routes, cot, experts, head_w, collective_id):
    anywhere = pl.BlockSpec(memory_space=pl.ANY)
    dma = pltpu.SemaphoreType.DMA
    return pl.pallas_call(
        moe_kernel,
        out_shape=[
            jax.ShapeDtypeStruct((4, LINES, 256), BF16),
            jax.ShapeDtypeStruct((16, 4, ROWS, 256), BF16),
            jax.ShapeDtypeStruct((8, 6, 128, 512), BF16),
            jax.ShapeDtypeStruct((8, 1024, 256), BF16),
        ],
        in_specs=[vmem(), vmem(), vmem(), anywhere, anywhere, anywhere],
        out_specs=[vmem(), anywhere, anywhere, anywhere],
        scratch_shapes=[
            VMEM((64, LINES, 256), BF16),
            VMEM((64, LINES, 256), BF16),
            VMEM((8, 6, 128, 512), BF16),
            VMEM((4, ROWS, 1024), BF16),
            VMEM((2, 4, GROUP, CAP, 1024), BF16),
            VMEM((2, 4, GROUP, CAP, 1024), BF16),
            VMEM((2, 4, GROUP * CAP, 512), BF16),
            VMEM((2, 4, GROUP * CAP, 512), BF16),
            VMEM((2, 4, GROUP * CAP, 512), BF16),
            VMEM((4, GROUP, 2 * CAP, ROWS), BF16),
            VMEM((2, GROUP * CAP, 1024), BF16),
            VMEM((2, GROUP * CAP, 1024), BF16),
            VMEM((2, 4, ROWS, 256), BF16),
            VMEM((4, 2, 128, 512), BF16),
            VMEM((4, 2, GROUP * CAP, 1), F32),
            VMEM((2, GROUP * CAP, 1), F32),
            dma((40,)),
            dma((40,)),
            dma((40,)),
            dma((40,)),
            dma((4,)),
            dma((2,)),
            dma((4,)),
            dma((3,)),
            pltpu.SemaphoreType.REGULAR,
            dma((13,)),
            dma((13,)),
        ],
        compiler_params=pltpu.CompilerParams(
            collective_id=collective_id, has_side_effects=True, vmem_limit_bytes=63 << 20
        ),
    )(moe, misc, routes, cot, experts, head_w)


def add_rows(target, others):
    shape = target.shape
    chunk = 1 if len(shape) == 3 else min(shape[0], 65536 // shape[1])

    def add(at):
        value = target[at].astype(F32)
        for other in others:
            value = value + other[at].astype(F32)
        target[at] = value.astype(target.dtype)

    if chunk == shape[0]:
        add(slice(None))
        return

    @pl.loop(0, shape[0] // chunk)
    def _(i):
        add(i if len(shape) == 3 else pl.ds(pl.multiple_of(i * chunk, chunk), chunk))


class ExpReduce:
    def __init__(self, parts, landed, send, recv):
        self.parts, self.landed = parts, landed
        self.copies = part_reduce_copies(parts, landed, send, recv)

    def block_at(self, half, axis, k, dest):
        return exp_block(dest, k, half, 1) if axis == 1 else exp_block(0, dest, half, 1)

    def row_of(self, half, axis, k):
        return (half * 5 + (k % 4 if axis == 1 else 4)) * 6

    def send_far(self, half, axis, k):
        self.copies[half, axis, k, 0].start()
        self.copies[half, axis, k, 1].start()

    def pass_on(self, half, axis, k):
        for s in (0, 1):
            self.copies[half, axis, k, s].wait_recv()
            line = self.block_at(half, axis, k, 1 - 2 * s) * 4 + 2 * half + s
            add_rows(self.parts.at[line], [self.landed.at[self.row_of(half, axis, k) + s]])
            self.copies[half, axis, k, s + 2].start()

    def finish(self, half, axis, k):
        self.copies[half, axis, k, 2].wait_recv()
        self.copies[half, axis, k, 3].wait_recv()
        row = self.row_of(half, axis, k)
        for part in range(2):
            line = self.block_at(half, axis, k, 0) * 4 + 2 * half + part
            add_rows(
                self.parts.at[line],
                [self.landed.at[row + 2 + part], self.landed.at[row + 4 + part]],
            )

    def steps(self):
        def begin():
            for k in (2, 1, -1, 0):
                for half in range(2):
                    self.send_far(half, 1, k)

        def both(action, axis, k):
            def run():
                for half in range(2):
                    action(half, axis, k)

            return run

        def far():
            for half in range(2):
                self.finish(half, 1, 2)
                self.send_far(half, 2, 0)

        return [
            begin,
            both(self.pass_on, 1, 2),
            both(self.pass_on, 1, 1),
            both(self.pass_on, 1, -1),
            both(self.pass_on, 1, 0),
            far,
            both(self.finish, 1, 1),
            both(self.finish, 1, -1),
            both(self.pass_on, 2, 0),
            both(self.finish, 1, 0),
            both(self.finish, 2, 0),
        ]

    def sent(self):
        for copy in self.copies.values():
            copy.wait_send()


class CtxReduce:
    STEPS = (2, 1, -1, 0)

    def __init__(self, given, mine, near, landed, send, recv):
        self.mine, self.near, self.landed = mine, near, landed
        half = near.shape[1] // 2
        self.first, self.second = pl.ds(0, half), pl.ds(half, half)
        self.swaps = [
            to_ctx(
                given.at[ctx_block(step, True)], near.at[at], send.at[at], recv.at[at], (0, True)
            )
            for at, step in enumerate(self.STEPS)
        ]
        self.hops = [
            to_ctx(src, dst, send.at[4 + at], recv.at[4 + at], (step, False))
            for at, (src, dst, step) in enumerate(
                (
                    (mine[0].at[self.first], landed.at[0, self.first], 1),
                    (mine[0].at[self.second], landed.at[0, self.second], -1),
                    (mine[1], landed.at[1], 1),
                    (mine[2], landed.at[2], -1),
                )
            )
        ]

    def swap(self):
        for copy in self.swaps:
            copy.start()

    def take(self, at):
        self.swaps[at].wait_recv()
        add_rows(self.mine[at], [self.near.at[at]])

    def far(self):
        self.take(0)
        self.hops[0].start()
        self.hops[1].start()

    def sides(self):
        self.take(1)
        self.take(2)

    def pass_on(self):
        for at, part in ((0, self.first), (1, self.second)):
            self.hops[at].wait_recv()
            add_rows(self.mine[1 + at].at[part], [self.landed.at[0, part]])
            self.hops[2 + at].start()

    def finish(self):
        self.take(3)
        self.hops[2].wait_recv()
        self.hops[3].wait_recv()
        add_rows(self.mine[3], [self.landed.at[1], self.landed.at[2]])

    def sent(self):
        for copy in (*self.swaps, *self.hops):
            copy.wait_send()


class LineReduce:
    def __init__(self, parts, landed, send, recv):
        self.parts, self.landed = parts, landed
        self.copies = {}
        for half in range(2):
            for axis, k in ((1, 0), (1, 1), (1, -1), (1, 2), (2, 0)):
                for s, step in enumerate(STEPS):
                    block = self.block_at(half, axis, k, step)
                    target = exp_block(step, 0, half, 1) if axis == 1 else exp_block(0, step, half, 1)
                    row = self.row_of(half, axis, k, s)
                    self.copies[half, axis, k, s] = pltpu.make_async_remote_copy(
                        src_ref=parts.at[pl.ds(block * 4 + 2 * half, 2)],
                        dst_ref=landed.at[pl.ds(2 * row, 2)],
                        send_sem=send.at[row],
                        recv_sem=recv.at[row],
                        device_id={"exp": target},
                        device_id_type=MESH,
                    )

    def block_at(self, half, axis, k, dest):
        return exp_block(dest, k, half, 1) if axis == 1 else exp_block(0, dest, half, 1)

    def row_of(self, half, axis, k, s):
        return half * 15 + (3 * (k % 4) if axis == 1 else 12) + s

    def send(self, axis):
        for k in (2, 1, -1, 0) if axis == 1 else (0,):
            for s in range(3):
                for half in range(2):
                    self.copies[half, axis, k, s].start()

    def take(self, axis):
        for k in (2, 1, -1, 0) if axis == 1 else (0,):
            for half in range(2):
                rows = []
                for s in range(3):
                    self.copies[half, axis, k, s].wait_recv()
                    rows.append(2 * self.row_of(half, axis, k, s))
                line = self.block_at(half, axis, k, 0) * 4 + 2 * half
                for part in range(2):
                    add_rows(
                        self.parts.at[line + part], [self.landed.at[row + part] for row in rows]
                    )

    def sent(self):
        for copy in self.copies.values():
            copy.wait_send()


def split_dot(value, other, dims):
    high = value.astype(BF16)
    low = (value - high.astype(F32)).astype(BF16)
    return dot(high, other, dims) + dot(low, other, dims)


def norm_back(values, grads, gain):
    r = lax.rsqrt(jnp.mean(values * values, axis=1, keepdims=True) + EPSILON)
    n = values * r
    scaled = grads * gain
    back = r * (scaled - n * jnp.mean(scaled * n, axis=1, keepdims=True))
    return back, n


def finish_kernel(
    grad_total, resid, misc, router, routes, moe, cot, tokens, full_out, mixed_rows,
    q_t, q_s, k_s, k_t, v_s, lse, exact, attn_in, out_parts, terms, all_w,
    output, token_grad, head_sum, out_sum, term_sum,
    o_parts, o_landed, t_mine, t_near, t_landed, attn_grad, resid_grad, mg_out, mg_land,
    p_given, p_near, p_landed, out_s, out_t, delta, dq, d, d_land, w_full,
    head_acc, small, w_parts, w_landed, wide_small, f_given, f_land, attn_rows,
    o_send, o_recv, w_send, w_recv, ctx_send, ctx_recv, direct_send, direct_recv, local, rows_sem, d_send, d_recv,
):
    me = lax.axis_index("ctx")
    own = exp_block(0, 0, 0, 0)
    greet_signal(PEERS, LINES_OF)
    o_load = pltpu.make_async_copy(out_parts, o_parts, local.at[0])
    o_load.start()
    t_loads = [
        pltpu.make_async_copy(terms.at[ctx_block(step, False)], t_mine.at[at], local.at[1 + at])
        for at, step in enumerate(CtxReduce.STEPS)
    ]
    for load in t_loads:
        load.start()

    def rows_load(j):
        return pltpu.make_async_copy(
            attn_in.at[pl.ds(j * ROWS, ROWS)], attn_rows.at[j % 2], rows_sem.at[j % 2]
        )

    rows_load(0).start()
    w_load = pltpu.make_async_copy(all_w, w_full, local.at[5])
    w_load.start()
    out_reduce = ExpReduce(o_parts, o_landed, o_send, o_recv)
    o_steps = out_reduce.steps()
    term_reduce = CtxReduce(
        terms, [t_mine.at[at] for at in range(4)], t_near, t_landed, ctx_send.at[0], ctx_recv.at[0]
    )
    proj_reduce = CtxReduce(
        p_given, [p_given.at[ctx_block(step, False)] for step in CtxReduce.STEPS],
        p_near, p_landed, ctx_send.at[1], ctx_recv.at[1],
    )

    place = lax.broadcasted_iota(jnp.int32, (32, ROWS), 0)
    expert = 2 * lax.rem(place, 16) + lax.div(place, 16)
    listed = routes[own].astype(F32).astype(jnp.int32)
    listed = jnp.concatenate([listed[:8], listed[8:]], axis=1)
    chosen = expert < 0
    for j in range(8):
        chosen = chosen | (listed[j : j + 1] == expert)
    logits = jnp.zeros((32, ROWS), F32)
    for q in range(4):
        logits = logits + dot(router[:, q * 256 : (q + 1) * 256], moe[q], ((1,), (1,)))
    logits = jnp.where(chosen, logits, -1e30)
    gates = jnp.exp(logits - jnp.max(logits, axis=0, keepdims=True))
    gates = jnp.where(chosen, gates, 0.0)
    gates = gates / jnp.sum(gates, axis=0, keepdims=True)
    weight_grad = [grad_total[q, ROWS:LINES].astype(F32) for q in range(4)]
    weight_grad = jnp.concatenate(
        [weight_grad[0] + weight_grad[1], weight_grad[2] + weight_grad[3]], axis=0
    )
    logit_grad = gates * (weight_grad - jnp.sum(gates * weight_grad, axis=0, keepdims=True))
    logit_grad = jnp.where(chosen, logit_grad, 0.0)
    moe_in_grad = jnp.concatenate(
        [grad_total[q, 0:ROWS].astype(F32) for q in range(4)], axis=1
    )
    moe_in_grad = moe_in_grad + split_dot(logit_grad, router[...], ((0,), (0,)))
    greet_wait(PEERS, LINES_OF)
    term_reduce.swap()
    o_load.wait()
    o_steps[0]()
    back, n = norm_back(resid[...], moe_in_grad, misc[32:33])
    total = back + cot[...].astype(F32)
    resid_grad[...] = total
    attn_grad[...] = total.astype(BF16)
    mixed_grad = dot(attn_grad[...], full_out[...], ((1,), (1,))).astype(BF16)
    for c in range(8):
        mg_out[c] = mixed_grad[:, c * 128 : (c + 1) * 128]
    mg_copies = [
        to_ctx(
            mg_out.at[ctx_block(*peer)], mg_land.at[me],
            direct_send.at[0, at], direct_recv.at[0, at], peer,
        )
        for at, peer in enumerate(PEERS)
    ]
    for copy in mg_copies:
        copy.start()
    for load in t_loads:
        load.wait()
    term_reduce.far()
    mg_land[me] = mg_out[me]
    for c in range(8):
        p_given[c] = dot(mixed_rows[c], attn_grad[...], ((0,), (0,))).astype(BF16)
    proj_reduce.swap()
    for q in range(4):
        at = slice(q * 256, (q + 1) * 256)
        small[0:32, at] = split_dot(logit_grad, moe[q], ((1,), (0,)))
    small[32:40] = jnp.broadcast_to(jnp.sum(moe_in_grad * n, axis=0, keepdims=True), (8, 1024))
    o_steps[1]()
    proj_reduce.far()
    term_reduce.sides()
    proj_reduce.sides()
    o_steps[2]()
    for copy in mg_copies:
        copy.wait_recv()

    @pl.loop(0, 8)
    def _(i):
        g = mg_land[i].astype(F32)
        out_s[i] = one_below(g).astype(BF16)
        g = side_by_side(g.T)
        out_t[i] = g.astype(BF16)
        delta[i] = jnp.sum(g * exact[i], axis=0, keepdims=True)
        dq[i] = jnp.zeros_like(dq[i])

    key_row = lax.broadcasted_iota(jnp.int32, (ROWS, 2 * ROWS), 0)
    query_row = lax.rem(lax.broadcasted_iota(jnp.int32, (ROWS, 2 * ROWS), 1), ROWS)
    seen = key_row <= query_row

    def key_block(j):
        key, key_t, value = k_s[j], k_t[j], v_s[j]

        def add_block(i, carry, diagonal):
            dk, dv = carry
            probs = jnp.exp(dot(key, q_t[i]) - lse[i])
            if diagonal:
                probs = jnp.where(seen, probs, 0.0)
            grad = probs * (dot(value, out_t[i]) - delta[i])
            grad = grad.astype(BF16)
            dv = dv + dot(probs.astype(BF16), out_s[i])
            dk = dk + dot(grad, q_s[i])
            dq[i] += dot(key_t, grad)
            return dk, dv

        zero = jnp.zeros((ROWS, 64), F32)
        carry = add_block(j, (zero, zero), True)
        dk, dv = lax.fori_loop(j + 1, 8, lambda i, c: add_block(i, c, False), carry)
        g = dq[j] * 0.125
        g = jnp.concatenate([g[:, :ROWS], g[:, ROWS:]], axis=0).T
        d[j] = jnp.concatenate([g, dk, dv], axis=1).astype(BF16)

    def d_copy(j):
        return pltpu.make_async_remote_copy(
            src_ref=d.at[j],
            dst_ref=d_land.at[me],
            send_sem=d_send.at[j],
            recv_sem=d_recv.at[me],
            device_id={"ctx": jnp.int32(j)},
            device_id_type=MESH,
        )

    def d_begin(j):
        @pl.when(me != j)
        def _():
            d_copy(j).start()

        @pl.when(me == j)
        def _():
            d_land[j] = d[j]

    def head_term(j):
        rows_load(j).wait()
        if j < 7:
            rows_load(j + 1).start()
        value = dot(attn_rows[j % 2], d[j], ((0,), (0,)))
        value = value.reshape(8, 16, 8, 256)
        head_acc[...] = value if j == 0 else head_acc[...] + value

    between = (
        (o_steps[3],),
        (term_reduce.pass_on, o_steps[4]),
        (proj_reduce.pass_on, o_steps[5]),
        (o_steps[6],),
        (o_steps[7], o_steps[8]),
        (proj_reduce.finish,),
        (o_steps[9],),
        (),
    )
    for j in range(8):
        key_block(j)
        d_begin(j)
        if j < 7:
            head_term(j)
        for step in between[j]:
            step()
    head_term(7)
    wide = jnp.concatenate([small[...], jnp.zeros((88, 1024), F32)], axis=0)
    for c in range(8):
        wide_small[c] = wide[:, c * 128 : (c + 1) * 128].T
    mine = proj_reduce.mine[3]

    for x in range(16):
        head = head_acc[:, x].reshape(64, 256)
        rows = mine[pl.ds((x // 2) * 16, 16)].astype(F32)[(x % 2) * 8 : (x % 2) * 8 + 8]
        rows = jnp.concatenate([rows[:, q * 256 : (q + 1) * 256] for q in range(4)], axis=0)
        rest = wide_small[:, x * 8 : x * 8 + 8].reshape(64, 128)
        rest = jnp.concatenate([rest[:32], rest[32:]], axis=1)
        w_parts[4 * x] = head[:32].astype(BF16)
        w_parts[4 * x + 1] = head[32:].astype(BF16)
        w_parts[4 * x + 2] = rows.astype(BF16)
        w_parts[4 * x + 3] = rest.astype(BF16)
    w_reduce = LineReduce(w_parts, w_landed, w_send, w_recv)
    w_reduce.send(1)
    w_load.wait()
    w_reduce.take(1)
    w_reduce.send(2)
    for source in range(8):

        @pl.when(me != source)
        def _():
            pltpu.make_async_remote_copy(
                src_ref=d.at[source],
                dst_ref=d_land.at[source],
                send_sem=d_send.at[source],
                recv_sem=d_recv.at[source],
                device_id={"ctx": jnp.int32(source)},
                device_id_type=MESH,
            ).wait_recv()

    attn_in_grad = jnp.zeros((ROWS, 1024), F32)
    for c in range(8):
        attn_in_grad = attn_in_grad + dot(d_land[c], w_full[c], ((1,), (1,)))
    back, _ = norm_back(tokens[...].astype(F32), attn_in_grad, misc[33:34])
    token_grad[...] = (back + resid_grad[...]).astype(BF16)
    w_reduce.take(2)
    done = [w_parts[4 * own + q].astype(F32) for q in range(4)]
    for q in range(4):
        out_sum[:, q * 256 : (q + 1) * 256] = done[2][q * 8 : (q + 1) * 8]
    for c in range(8):
        source = done[c // 4][(c % 4) * 8 : (c % 4) * 8 + 8]
        f_send = jnp.concatenate(
            [
                source,
                done[3][(c % 4) * 8 : (c % 4) * 8 + 8, (c // 4) * 128 : (c // 4) * 128 + 128],
            ],
            axis=1,
        )
        f_given[c] = f_send
    f_copies = [
        to_ctx(
            f_given.at[ctx_block(*peer)], f_land.at[me],
            direct_send.at[1, at], direct_recv.at[1, at], peer,
        )
        for at, peer in enumerate(PEERS)
    ]
    for copy in f_copies:
        copy.start()
    f_land[me] = f_given[me]
    term_reduce.finish()
    term_sum[...] = t_mine[3]
    o_steps[10]()
    expert_out = jnp.concatenate([o_parts[4 * own + q].astype(F32) for q in range(4)], axis=1)
    output[...] = (resid[...] + expert_out).astype(BF16)
    for copy in f_copies:
        copy.wait_recv()
    for c in range(8):
        head_sum[c] = f_land[c]
    out_reduce.sent()
    w_reduce.sent()
    for reduce in (term_reduce, proj_reduce):
        reduce.sent()
    for copy in (*mg_copies, *f_copies):
        copy.wait_send()
    for j in range(8):

        @pl.when(me != j)
        def _():
            d_copy(j).wait_send()


def finish(args, collective_id):
    anywhere = pl.BlockSpec(memory_space=pl.ANY)
    dma = pltpu.SemaphoreType.DMA
    outs = [
        ((256, 1024), BF16),
        ((256, 1024), BF16),
        ((8, 8, 384), F32),
        ((8, 1024), F32),
        ((6, 128, 512), BF16),
    ]
    return pl.pallas_call(
        finish_kernel,
        out_shape=[jax.ShapeDtypeStruct(s, t) for s, t in outs],
        in_specs=[vmem()] * 17 + [anywhere] * 4,
        out_specs=[vmem()] * len(outs),
        scratch_shapes=[
            VMEM((64, 256, 256), BF16),
            VMEM((60, 256, 256), BF16),
            VMEM((4, 6, 128, 512), BF16),
            VMEM((4, 6, 128, 512), BF16),
            VMEM((3, 6, 128, 512), BF16),
            VMEM((256, 1024), BF16),
            VMEM((256, 1024), F32),
            VMEM((8, 256, 128), BF16),
            VMEM((8, 256, 128), BF16),
            VMEM((8, 128, 1024), BF16),
            VMEM((4, 128, 1024), BF16),
            VMEM((3, 128, 1024), BF16),
            VMEM((8, 512, 64), BF16),
            VMEM((8, 64, 512), BF16),
            VMEM((8, 1, 512), F32),
            VMEM((8, 64, 512), F32),
            VMEM((8, 256, 256), BF16),
            VMEM((8, 256, 256), BF16),
            VMEM((8, 1024, 256), BF16),
            VMEM((8, 16, 8, 256), F32),
            VMEM((40, 1024), F32),
            VMEM((64, 32, 256), BF16),
            VMEM((60, 32, 256), BF16),
            VMEM((8, 128, 128), F32),
            VMEM((8, 8, 384), F32),
            VMEM((8, 8, 384), F32),
            VMEM((2, 256, 1024), BF16),
            dma((40,)),
            dma((40,)),
            dma((40,)),
            dma((40,)),
            dma((2, 8)),
            dma((2, 8)),
            dma((2, 7)),
            dma((2, 7)),
            dma((6,)),
            dma((2,)),
            dma((8,)),
            dma((8,)),
        ],
        compiler_params=pltpu.CompilerParams(
            collective_id=collective_id, has_side_effects=True, vmem_limit_bytes=62 << 20
        ),
    )(*args)


def last_kernel(
    output, token_grad, head_in, out_in, term_in, query_in, key_in, value_in, narrow_in,
    output_end, token_grad_end, norms, query_sum, key_sum, value_sum, out_end, router_sum,
    gate_sum, up_sum, down_sum,
    head_sum, term_sum, w_query, w_key, w_value, norm_attn, sems,
):
    copies = [
        pltpu.make_async_copy(source, target, sems.at[at])
        for at, (source, target) in enumerate(
            (
                (head_in, head_sum), (query_in, w_query), (key_in, w_key), (value_in, w_value),
                (narrow_in, norm_attn), (term_in, term_sum), (output, output_end),
                (token_grad, token_grad_end), (out_in, out_end),
            )
        )
    ]
    for copy in copies:
        copy.start()
    for copy in copies[:5]:
        copy.wait()
    query = jnp.concatenate([head_sum[c, :, 0:128] for c in range(8)], axis=1)
    key = jnp.concatenate([head_sum[c, :, 128:192] for c in range(8)], axis=1)
    value = jnp.concatenate([head_sum[c, :, 192:256] for c in range(8)], axis=1)
    query_sum[...] = query
    key_sum[...] = key
    value_sum[...] = value
    small = head_sum[0, :, 256:384]
    for c in range(1, 8):
        small = small + head_sum[c, :, 256:384]
    router_sum[...] = small
    total = jnp.sum(query * w_query[...].astype(F32), axis=1, keepdims=True)
    total = total + jnp.sum(key * w_key[...].astype(F32), axis=1, keepdims=True)
    total = total + jnp.sum(value * w_value[...].astype(F32), axis=1, keepdims=True)
    total = total / norm_attn[:, 33:34]
    lane = lax.broadcasted_iota(jnp.int32, (8, 128), 1)
    both = jnp.where(lane == 0, total, small[:, 32:33])
    norms[...] = both.T[0:8, :]
    for copy in copies[5:]:
        copy.wait()
    for k in range(2):
        gate_sum[k] = term_sum[k].astype(F32)
        up_sum[k] = term_sum[2 + k].astype(F32)
        down_sum[k] = term_sum[4 + k].astype(F32).T


def last(*args):
    anywhere = pl.BlockSpec(memory_space=pl.ANY)
    outs = [
        ((256, 1024), BF16),
        ((256, 1024), BF16),
        ((8, 8), F32),
        ((8, 1024), F32),
        ((8, 512), F32),
        ((8, 512), F32),
        ((8, 1024), F32),
        ((8, 128), F32),
        ((2, 128, 512), F32),
        ((2, 128, 512), F32),
        ((2, 512, 128), F32),
    ]
    return pl.pallas_call(
        last_kernel,
        out_shape=[jax.ShapeDtypeStruct(s, t) for s, t in outs],
        in_specs=[anywhere] * len(args),
        out_specs=[anywhere if at in (0, 1, 6) else vmem() for at in range(len(outs))],
        scratch_shapes=[
            VMEM((8, 8, 384), F32),
            VMEM((6, 128, 512), BF16),
            VMEM((8, 1024), BF16),
            VMEM((8, 512), BF16),
            VMEM((8, 512), BF16),
            VMEM((8, 128), F32),
            pltpu.SemaphoreType.DMA((9,)),
        ],
        compiler_params=pltpu.CompilerParams(vmem_limit_bytes=30 << 20),
    )(*args)


def per_device(
    tokens,
    norm_attn,
    w_query,
    w_key,
    w_value,
    w_out,
    norm_moe,
    w_router,
    w_gate,
    w_up,
    w_down,
    routes,
    cotangent,
):
    narrow = jnp.concatenate([w_router, norm_moe[:, None], norm_attn[:, None]], axis=1)
    narrow = jnp.pad(narrow.astype(F32), ((0, 0), (0, 94)))
    (
        attn_in, q_t, q_s, k_s, k_t, v_s, lse, exact, mixed_rows,
        head_weights, misc_t, full_out, resid, moe_in, all_cot, all_routes, all_experts,
    ) = start(
        (
            tokens[0], cotangent[0], w_gate, w_up, w_down,
            w_query, w_key, w_value, w_out, narrow, routes[0],
        ),
        1,
    )
    grad_total, out_parts, expert_terms, all_weights = moe_block(
        moe_in, misc_t, all_routes, all_cot, all_experts, head_weights, 2
    )
    router = misc_t[:32].astype(BF16).reshape(16, 2, 1024).transpose(1, 0, 2).reshape(32, 1024)
    parts = finish(
        (
            grad_total, resid, misc_t, router, all_routes, moe_in, cotangent[0], tokens[0],
            full_out, mixed_rows, q_t, q_s, k_s, k_t, v_s, lse, exact, attn_in,
            out_parts.reshape(64, 256, 256), expert_terms, all_weights,
        ),
        3,
    )
    (
        output, token_grad, norms, query_sum, key_sum, value_sum, out_sum, router_sum,
        gate_sum, up_sum, down_sum,
    ) = last(*parts, w_query, w_key, w_value, narrow)
    router_sum = router_sum[:, :32].reshape(8, 2, 16).transpose(0, 2, 1).reshape(8, 32)
    return (
        output[None],
        token_grad[None],
        norms[0],
        query_sum,
        key_sum,
        value_sum,
        out_sum,
        norms[1],
        router_sum,
        gate_sum,
        up_sum,
        down_sum,
    )


def solution(mesh):
    in_specs = (
        P("exp", "ctx", None),
        P(("ctx", "exp")),
        P(("ctx", "exp"), None),
        P(("ctx", "exp"), None),
        P(("ctx", "exp"), None),
        P(("ctx", "exp"), None),
        P(("ctx", "exp")),
        P(("ctx", "exp"), None),
        P("exp", "ctx", None),
        P("exp", "ctx", None),
        P("exp", None, "ctx"),
        P("exp", "ctx", None),
        P("exp", "ctx", None),
    )
    out_specs = (
        P("exp", "ctx", None),
        P("exp", "ctx", None),
        P(("ctx", "exp")),
        P(("ctx", "exp"), None),
        P(("ctx", "exp"), None),
        P(("ctx", "exp"), None),
        P(("ctx", "exp"), None),
        P(("ctx", "exp")),
        P(("ctx", "exp"), None),
        P("exp", "ctx", None),
        P("exp", "ctx", None),
        P("exp", None, "ctx"),
    )
    return jax.shard_map(
        per_device, mesh=mesh, in_specs=in_specs, out_specs=out_specs, check_vma=False
    )
```

```python
import jax
import jax.numpy as jnp
from jax import lax
from jax.experimental import pallas as pl
from jax.experimental.pallas import tpu as pltpu
from jax.sharding import PartitionSpec as P

EPSILON = 1e-06
PRECISE = lax.Precision.HIGHEST
F32, BF16 = jnp.float32, jnp.bfloat16
VMEM = pltpu.VMEM
MESH = pl.DeviceIdType.MESH
SIDE = 4
ROWS = 256
CAP = 96
GROUP = 4


def exp_block(first, second, half, inner):
    index = lax.axis_index("exp")
    z, x = lax.div(index, SIDE), lax.rem(index, SIDE)
    by_x, by_z = (first, second) if half == inner else (second, first)
    return lax.rem(z + by_z + SIDE, SIDE) * SIDE + lax.rem(x + by_x + SIDE, SIDE)


def greet_exp():
    barrier = pltpu.get_barrier_semaphore()
    for half in range(2):
        for step in (1, -1):
            pl.semaphore_signal(
                barrier, inc=1, device_id={"exp": exp_block(step, 0, half, 0)}, device_id_type=MESH
            )
    pl.semaphore_wait(barrier, 4)


def gather_exp_copy(own, out, send, recv, rows, half, axis, k, s):
    part = rows // 4
    step = (1, -1, 1, -1)[s]
    off = (0, 0, -1, 1)[s]
    origin = exp_block(off, 0, half, 0) if axis == 1 else exp_block(k, off, half, 0)
    target = exp_block(step, 0, half, 0) if axis == 1 else exp_block(0, step, half, 0)
    lines = (
        pl.ds(half * 2 * part, 2 * part)
        if s < 2
        else pl.ds((half * 2 + s - 2) * part, part)
    )
    mine = s < 2 and (axis == 1 or k == 0)
    at = half * 20 + (s if axis == 1 else 4 + 4 * (k % 4) + s)
    return pltpu.make_async_remote_copy(
        src_ref=own.at[lines] if mine else out.at[origin, lines],
        dst_ref=out.at[origin, lines],
        send_sem=send.at[at],
        recv_sem=recv.at[at],
        device_id={"exp": target},
        device_id_type=MESH,
    )


def gather_exp_kernel(own, out, send, recv, local):
    rows = own.shape[0]
    greet_exp()
    copies = {
        (half, axis, k, s): gather_exp_copy(own, out, send, recv, rows, half, axis, k, s)
        for half in range(2)
        for axis, k in ((1, 0), (2, 0), (2, 1), (2, -1), (2, 2))
        for s in range(4)
    }
    keep = pltpu.make_async_copy(own, out.at[exp_block(0, 0, 0, 0)], local)
    keep.start()
    for axis in (1, 2):
        for s in (0, 1):
            for half in range(2):
                copies[half, axis, 0, s].start()
    for s, k in ((0, -1), (1, 1)):
        for half in range(2):
            copies[half, 1, 0, s].wait_recv()
            copies[half, 1, 0, s + 2].start()
            copies[half, 2, k, 0].start()
            copies[half, 2, k, 1].start()
    for s in (0, 1):
        for half in range(2):
            copies[half, 2, 0, s].wait_recv()
            copies[half, 2, 0, s + 2].start()
    for half in range(2):
        copies[half, 1, 0, 2].wait_recv()
        copies[half, 1, 0, 3].wait_recv()
        copies[half, 2, 2, 0].start()
        copies[half, 2, 2, 1].start()
    for k in (-1, 1, 2):
        for s in (0, 1):
            for half in range(2):
                copies[half, 2, k, s].wait_recv()
                copies[half, 2, k, s + 2].start()
    for k in (0, -1, 1, 2):
        for s in (2, 3):
            for half in range(2):
                copies[half, 2, k, s].wait_recv()
    for copy in copies.values():
        copy.wait_send()
    keep.wait()


def gather_exp(block, collective_id):
    rows, width = block.shape
    return pl.pallas_call(
        gather_exp_kernel,
        out_shape=jax.ShapeDtypeStruct((16, rows, width), block.dtype),
        in_specs=[pl.BlockSpec(memory_space=pl.ANY)],
        out_specs=pl.BlockSpec(memory_space=pl.ANY),
        scratch_shapes=[
            pltpu.SemaphoreType.DMA((40,)),
            pltpu.SemaphoreType.DMA((40,)),
            pltpu.SemaphoreType.DMA,
        ],
        compiler_params=pltpu.CompilerParams(collective_id=collective_id, has_side_effects=True),
    )(block)


def reduce_exp_copy(parts, landed, send, recv, half, axis, k, s):
    step = (1, -1, 1, -1)[s]
    dest = (2, 2, 1, -1)[s]
    block = exp_block(dest, k, half, 1) if axis == 1 else exp_block(0, dest, half, 1)
    target = exp_block(step, 0, half, 1) if axis == 1 else exp_block(0, step, half, 1)
    row = half * 5 + (k % 4 if axis == 1 else 4)
    source = (
        parts.at[block, pl.ds(2 * half + s, 1)] if s < 2 else parts.at[block, pl.ds(2 * half, 2)]
    )
    place = (pl.ds(0, 1), pl.ds(1, 1), pl.ds(2, 2), pl.ds(4, 2))[s]
    at = row * 4 + s
    return pltpu.make_async_remote_copy(
        src_ref=source,
        dst_ref=landed.at[row, place],
        send_sem=send.at[at],
        recv_sem=recv.at[at],
        device_id={"exp": target},
        device_id_type=MESH,
    )


def add_lines(total, others, step):
    lines = total.shape[0]

    @pl.loop(0, lines // step)
    def _(i):
        at = pl.ds(pl.multiple_of(i * step, step), step)
        value = total[at].astype(jnp.float32)
        for other in others:
            value = value + other[at].astype(jnp.float32)
        total[at] = value.astype(total.dtype)


def reduce_exp_kernel(given, out, parts, landed, send, recv, local, done):
    greet_exp()
    lines = given.shape[2]
    step = 16
    load = pltpu.make_async_copy(given, parts, local)
    load.start()
    load.wait()
    copies = {
        (half, axis, k, s): reduce_exp_copy(parts, landed, send, recv, half, axis, k, s)
        for half in range(2)
        for axis, k in ((1, 0), (1, 1), (1, -1), (1, 2), (2, 0))
        for s in range(4)
    }

    def row_of(half, axis, k):
        return half * 5 + (k % 4 if axis == 1 else 4)

    def block_of(half, axis, k, dest):
        return exp_block(dest, k, half, 1) if axis == 1 else exp_block(0, dest, half, 1)

    def pass_on(half, axis, k):
        for s, dest in ((0, 1), (1, -1)):
            copies[half, axis, k, s].wait_recv()
            add_lines(
                parts.at[block_of(half, axis, k, dest), 2 * half + s],
                [landed.at[row_of(half, axis, k), s]],
                step,
            )
            copies[half, axis, k, s + 2].start()

    def finish(half, axis, k):
        copies[half, axis, k, 2].wait_recv()
        copies[half, axis, k, 3].wait_recv()
        for part in range(2):
            add_lines(
                parts.at[block_of(half, axis, k, 0), 2 * half + part],
                [
                    landed.at[row_of(half, axis, k), 2 + part],
                    landed.at[row_of(half, axis, k), 4 + part],
                ],
                step,
            )

    order = (2, 1, -1, 0)
    for k in order:
        for half in range(2):
            for s in (0, 1):
                copies[half, 1, k, s].start()
    for k in order:
        for half in range(2):
            pass_on(half, 1, k)
    for k in order:
        for half in range(2):
            finish(half, 1, k)
            if k == 2:
                copies[half, 2, 0, 0].start()
                copies[half, 2, 0, 1].start()
    for half in range(2):
        pass_on(half, 2, 0)
    for half in range(2):
        finish(half, 2, 0)
    store = pltpu.make_async_copy(parts.at[exp_block(0, 0, 0, 0)], out, done)
    store.start()
    for copy in copies.values():
        copy.wait_send()
    store.wait()


def reduce_exp(parts, collective_id):
    _, quarters, lines, width = parts.shape
    return pl.pallas_call(
        reduce_exp_kernel,
        out_shape=jax.ShapeDtypeStruct((quarters, lines, width), parts.dtype),
        in_specs=[pl.BlockSpec(memory_space=pl.ANY)],
        out_specs=pl.BlockSpec(memory_space=pl.ANY),
        scratch_shapes=[
            pltpu.VMEM(parts.shape, parts.dtype),
            pltpu.VMEM((10, 6, lines, width), parts.dtype),
            pltpu.SemaphoreType.DMA((40,)),
            pltpu.SemaphoreType.DMA((40,)),
            pltpu.SemaphoreType.DMA,
            pltpu.SemaphoreType.DMA,
        ],
        compiler_params=pltpu.CompilerParams(
            collective_id=collective_id, has_side_effects=True, vmem_limit_bytes=40 << 20
        ),
    )(parts)


def ctx_block(step, other):
    index = lax.axis_index("ctx")
    y, core = lax.div(index, 2), lax.rem(index, 2)
    if other:
        core = 1 - core
    return lax.rem(y + step + SIDE, SIDE) * 2 + core


def greet_ctx():
    barrier = pltpu.get_barrier_semaphore()
    for step, other in ((1, False), (-1, False), (0, True)):
        pl.semaphore_signal(
            barrier, inc=1, device_id={"ctx": ctx_block(step, other)}, device_id_type=MESH
        )
    pl.semaphore_wait(barrier, 3)


def gather_ctx_copies(own, out, send, recv):
    half = own.shape[0] // 2
    every, first, second = pl.ds(0, 2 * half), pl.ds(0, half), pl.ds(half, half)
    plan = (
        (0, every, 0, True),
        (0, first, 1, False),
        (0, second, -1, False),
        (0, second, 1, False),
        (0, first, -1, False),
        (-1, first, 1, False),
        (1, second, -1, False),
        (-1, first, 0, True),
        (-1, second, 0, True),
        (1, second, 0, True),
        (1, first, 0, True),
        (2, first, 0, True),
        (2, second, 0, True),
    )
    copies = []
    for at, (origin, lines, step, other) in enumerate(plan):
        slot = out.at[ctx_block(origin, False), lines]
        copies.append(
            pltpu.make_async_remote_copy(
                src_ref=own.at[lines] if origin == 0 else slot,
                dst_ref=slot,
                send_sem=send.at[at],
                recv_sem=recv.at[at],
                device_id={"ctx": ctx_block(step, other)},
                device_id_type=MESH,
            )
        )
    return copies


RING_START = (1, 2, 3, 4, 0)
RING_FOLLOW = {1: (5, 7), 2: (6, 9), 3: (8,), 4: (10,), 5: (11,), 6: (12,)}


def ring_follow(copies, *arrivals):
    for arrival in arrivals:
        copies[arrival].wait_recv()
        for at in RING_FOLLOW[arrival]:
            copies[at].start()


def dot(a, b, dims=((1,), (0,))):
    return lax.dot_general(a, b, (dims, ((), ())), preferred_element_type=F32)


def vmem(shape=None, index=None):
    return pl.BlockSpec(memory_space=VMEM)


def whole(*shape):
    return pl.BlockSpec(shape, lambda *_: (0,) * len(shape), pipeline_mode=pl.Buffered(1))


def side_by_side(a):
    return jnp.concatenate([a[:64], a[64:]], axis=1)


def one_below(a):
    return jnp.concatenate([a[:, :64], a[:, 64:]], axis=0)


def attend_kernel(
    tokens, gain, weights, attn_in, q_t, q_s, k_s, k_t, v_s, v_t, lse, exact, mixed
):
    scale = gain[...]

    @pl.loop(0, 8)
    def _(i):
        at = pl.ds(pl.multiple_of(i * ROWS, ROWS), ROWS)
        x = tokens[at].astype(F32)
        x = x * lax.rsqrt(jnp.mean(x * x, axis=1, keepdims=True) + EPSILON) * scale
        x = x.astype(BF16)
        attn_in[at] = x
        qkv = dot(x, weights[...]).astype(BF16).astype(F32)
        q = qkv[:, :128] * 0.125
        k, v = qkv[:, 128:192], qkv[:, 192:]
        q_s[i] = one_below(q).astype(BF16)
        q_t[i] = side_by_side(q.T).astype(BF16)
        k_s[i] = k.astype(BF16)
        v_s[i] = v.astype(BF16)
        kv_t = qkv[:, 128:].T
        k_t[i] = kv_t[:64].astype(BF16)
        v_t[i] = kv_t[64:].astype(BF16)

    key_row = lax.broadcasted_iota(jnp.int32, (ROWS, 2 * ROWS), 0)
    query_row = lax.rem(lax.broadcasted_iota(jnp.int32, (ROWS, 2 * ROWS), 1), ROWS)
    seen = key_row <= query_row

    @pl.loop(0, 8)
    def _(i):
        query = q_t[i]

        def add_block(j, carry, diagonal):
            top, total, acc = carry
            scores = dot(k_s[j], query)
            if diagonal:
                scores = jnp.where(seen, scores, -1e30)
            new_top = jnp.maximum(top, jnp.max(scores, axis=0, keepdims=True))
            fade = jnp.exp(top - new_top)
            weights = jnp.exp(scores - new_top)
            total = total * fade + jnp.sum(weights, axis=0, keepdims=True)
            acc = acc * fade + dot(v_t[j], weights.astype(BF16))
            return new_top, total, acc

        carry = (
            jnp.full((1, 2 * ROWS), -1e30, F32),
            jnp.zeros((1, 2 * ROWS), F32),
            jnp.zeros((64, 2 * ROWS), F32),
        )
        carry = lax.fori_loop(0, i, lambda j, c: add_block(j, c, False), carry)
        top, total, acc = add_block(i, carry, True)
        lse[i] = top + jnp.log(total)
        value = acc / total
        exact[i] = value
        both = jnp.concatenate([value[:, :ROWS], value[:, ROWS:]], axis=0)
        at = pl.ds(pl.multiple_of(i * ROWS, ROWS), ROWS)
        mixed[at] = both.T.astype(BF16)


def attend(tokens, gain, weights):
    shapes = [
        ((2048, 1024), BF16),
        ((8, 64, 512), BF16),
        ((8, 512, 64), BF16),
        ((8, 256, 64), BF16),
        ((8, 64, 256), BF16),
        ((8, 256, 64), BF16),
        ((8, 64, 256), BF16),
        ((8, 1, 512), F32),
        ((8, 64, 512), F32),
        ((2048, 128), BF16),
    ]
    return pl.pallas_call(
        attend_kernel,
        out_shape=[jax.ShapeDtypeStruct(s, t) for s, t in shapes],
        in_specs=[vmem()] * 3,
        out_specs=[vmem()] * len(shapes),
        compiler_params=pltpu.CompilerParams(vmem_limit_bytes=50 << 20),
    )(tokens, gain, weights)


def attend_back_kernel(
    mixed_grad, q_t, q_s, k_s, k_t, v_s, lse, exact, d, out_s, out_t, delta, dq
):
    @pl.loop(0, 8)
    def _(i):
        at = pl.ds(pl.multiple_of(i * ROWS, ROWS), ROWS)
        g = mixed_grad[at].astype(F32)
        out_s[i] = one_below(g).astype(BF16)
        g = side_by_side(g.T)
        out_t[i] = g.astype(BF16)
        delta[i] = jnp.sum(g * exact[i], axis=0, keepdims=True)
        dq[i] = jnp.zeros_like(dq[i])

    key_row = lax.broadcasted_iota(jnp.int32, (ROWS, 2 * ROWS), 0)
    query_row = lax.rem(lax.broadcasted_iota(jnp.int32, (ROWS, 2 * ROWS), 1), ROWS)
    seen = key_row <= query_row

    @pl.loop(0, 8)
    def _(j):
        key, key_t, value = k_s[j], k_t[j], v_s[j]

        def add_block(i, carry, diagonal):
            dk, dv = carry
            probs = jnp.exp(dot(key, q_t[i]) - lse[i])
            if diagonal:
                probs = jnp.where(seen, probs, 0.0)
            grad = probs * (dot(value, out_t[i]) - delta[i])
            grad = grad.astype(BF16)
            dv = dv + dot(probs.astype(BF16), out_s[i])
            dk = dk + dot(grad, q_s[i])
            dq[i] += dot(key_t, grad)
            return dk, dv

        zero = jnp.zeros((ROWS, 64), F32)
        carry = add_block(j, (zero, zero), True)
        dk, dv = lax.fori_loop(j + 1, 8, lambda i, c: add_block(i, c, False), carry)
        at = pl.ds(pl.multiple_of(j * ROWS, ROWS), ROWS)
        d[at, 128:256] = jnp.concatenate([dk, dv], axis=1).astype(BF16)

    @pl.loop(0, 8)
    def _(i):
        at = pl.ds(pl.multiple_of(i * ROWS, ROWS), ROWS)
        g = dq[i] * 0.125
        g = jnp.concatenate([g[:, :ROWS], g[:, ROWS:]], axis=0)
        d[at, 0:128] = g.T.astype(BF16)


def attend_back(mixed_grad, q_t, q_s, k_s, k_t, v_s, lse, exact):
    return pl.pallas_call(
        attend_back_kernel,
        out_shape=jax.ShapeDtypeStruct((2048, 256), BF16),
        in_specs=[vmem()] * 8,
        out_specs=vmem(),
        scratch_shapes=[
            VMEM((8, 512, 64), BF16),
            VMEM((8, 64, 512), BF16),
            VMEM((8, 1, 512), F32),
            VMEM((8, 64, 512), F32),
        ],
        compiler_params=pltpu.CompilerParams(vmem_limit_bytes=50 << 20),
    )(mixed_grad, q_t, q_s, k_s, k_t, v_s, lse, exact)


def experts_kernel(
    owner, moe, cot, routes, misc, weights,
    out_parts, grad_parts, rows, slot_grads, hidden, gate_grads, up_grads,
):
    own = owner[0]
    router = misc[0:32].astype(BF16)
    listed = [routes[b].astype(jnp.int32) for b in range(GROUP)]
    listed = [jnp.concatenate([r[:8], r[8:]], axis=1) for r in listed]

    def matrix(kind, k):
        return weights[:, 2 * kind + k].reshape(1024, 512)

    expert = lax.broadcasted_iota(jnp.int32, (32, ROWS), 0)
    named = [[None, None] for _ in range(GROUP)]
    gates = [[None, None] for _ in range(GROUP)]
    for b in range(GROUP):
        logits = dot(router, moe[b], ((1,), (1,)))
        chosen = expert < 0
        for j in range(8):
            chosen = chosen | (listed[b][j : j + 1] == expert)
        logits = jnp.where(chosen, logits, -1e30)
        weight = jnp.where(chosen, jnp.exp(logits - jnp.max(logits, axis=0, keepdims=True)), 0.0)
        weight = weight / jnp.sum(weight, axis=0, keepdims=True)
        for k in range(2):
            mine = expert == 2 * own + k
            gates[b][k] = jnp.sum(jnp.where(mine, weight, 0.0), axis=0, keepdims=True)
            named[b][k] = jnp.sum(
                jnp.where(mine & chosen, 1.0, 0.0), axis=0, keepdims=True
            )
    before = lax.broadcasted_iota(jnp.int32, (ROWS, ROWS), 0) < lax.broadcasted_iota(
        jnp.int32, (ROWS, ROWS), 1
    )
    flat = jnp.concatenate([named[b][k] for b in range(GROUP) for k in range(2)], axis=0)
    place = dot(flat.astype(BF16), before.astype(BF16))
    slot = lax.broadcasted_iota(jnp.int32, (CAP, ROWS), 0).astype(F32)
    spread = [[None, None] for _ in range(GROUP)]
    slot_gates = [[None, None] for _ in range(GROUP)]
    for b in range(GROUP):
        for k in range(2):
            at = 2 * b + k
            hit = (slot == place[at : at + 1]) & (flat[at : at + 1] > 0.5)
            spread[b][k] = jnp.where(hit, 1.0, 0.0).astype(BF16)
            slot_gates[b][k] = jnp.sum(
                jnp.where(hit, gates[b][k], 0.0), axis=1, keepdims=True
            )
    pick = [jnp.concatenate(spread[b], axis=0) for b in range(GROUP)]
    cots = [None] * GROUP
    for b in range(GROUP):
        both = dot(pick[b], moe[b]).astype(BF16)
        rows[0, b] = both[:CAP]
        rows[1, b] = both[CAP:]
        cots[b] = dot(pick[b], cot[b])
        for k in range(2):
            slot_grads[k, b] = (slot_gates[b][k] * cots[b][k * CAP : (k + 1) * CAP]).astype(BF16)
    gated = [None, None]
    row_grads = [None, None]
    weight_grads = [None, None]
    for k in range(2):
        x = rows[k].reshape(GROUP * CAP, 1024)
        dy = slot_grads[k].reshape(GROUP * CAP, 1024)
        g = dot(x, matrix(0, k))
        u = dot(x, matrix(1, k))
        s = jax.nn.sigmoid(g)
        silu = g * s
        h = (silu * u).astype(BF16)
        hidden[k] = h.reshape(GROUP, CAP, 512)
        y = dot(h, matrix(2, k), ((1,), (1,))).astype(BF16).astype(F32)
        gate = jnp.concatenate([slot_gates[b][k] for b in range(GROUP)], axis=0)
        gated[k] = (gate * y).astype(BF16)
        upstream = jnp.concatenate(
            [cots[b][k * CAP : (k + 1) * CAP] for b in range(GROUP)], axis=0
        )
        weight_grads[k] = jnp.sum(upstream * y, axis=1, keepdims=True)
        dh = dot(dy, matrix(2, k))
        gg = (dh * u * s * (1.0 + g * (1.0 - s))).astype(BF16)
        ug = (dh * silu).astype(BF16)
        gate_grads[k] = gg.reshape(GROUP, CAP, 512)
        up_grads[k] = ug.reshape(GROUP, CAP, 512)
        row_grads[k] = (
            dot(gg, matrix(0, k), ((1,), (1,))) + dot(ug, matrix(1, k), ((1,), (1,)))
        ).astype(BF16)
    owner_row = lax.broadcasted_iota(jnp.int32, (16, ROWS), 0) == own
    for b in range(GROUP):
        at = slice(b * CAP, (b + 1) * CAP)
        for source, target in ((gated, out_parts), (row_grads, grad_parts)):
            both = jnp.concatenate([source[0][at], source[1][at]], axis=0)
            total = dot(pick[b], both, ((0,), (0,))).astype(BF16)
            for q in range(4):
                target[b, q, 0:ROWS] = total[:, q * 256 : (q + 1) * 256]
        for k in range(2):
            vector = jnp.sum(
                spread[b][k].astype(F32) * weight_grads[k][at], axis=0, keepdims=True
            )
            high = vector.astype(BF16)
            low = (vector - high.astype(F32)).astype(BF16)
            grad_parts[b, 2 * k, ROWS : ROWS + 16] = jnp.where(
                owner_row, high.astype(F32), 0.0
            ).astype(BF16)
            grad_parts[b, 2 * k + 1, ROWS : ROWS + 16] = jnp.where(
                owner_row, low.astype(F32), 0.0
            ).astype(BF16)


def experts(owner, moe, cot, routes, misc, weights):
    steps = 16 // GROUP

    def block(*shape, dim=0):
        def index(g, owner):
            return tuple(g if i == dim else 0 for i in range(len(shape)))

        return pl.BlockSpec(shape, index)

    outs = [
        ((16, 4, 256, 256), BF16),
        ((16, 4, 272, 256), BF16),
        ((2, 16, CAP, 1024), BF16),
        ((2, 16, CAP, 1024), BF16),
        ((2, 16, CAP, 512), BF16),
        ((2, 16, CAP, 512), BF16),
        ((2, 16, CAP, 512), BF16),
    ]
    return pl.pallas_call(
        experts_kernel,
        grid_spec=pltpu.PrefetchScalarGridSpec(
            num_scalar_prefetch=1,
            grid=(steps,),
            in_specs=[
                block(GROUP, 256, 1024),
                block(GROUP, 256, 1024),
                block(GROUP, 16, 128),
                whole(40, 1024),
                whole(8, 6, 128, 512),
            ],
            out_specs=[
                block(GROUP, 4, 256, 256),
                block(GROUP, 4, 272, 256),
                block(2, GROUP, CAP, 1024, dim=1),
                block(2, GROUP, CAP, 1024, dim=1),
                block(2, GROUP, CAP, 512, dim=1),
                block(2, GROUP, CAP, 512, dim=1),
                block(2, GROUP, CAP, 512, dim=1),
            ],
        ),
        out_shape=[jax.ShapeDtypeStruct(s, t) for s, t in outs],
        compiler_params=pltpu.CompilerParams(vmem_limit_bytes=58 << 20),
    )(owner, moe, cot, routes, misc, weights)

PEERS = ((2, False), (2, True), (1, False), (1, True), (-1, False), (-1, True), (0, True))


def greet_signal(ctx_peers, exp_steps):
    barrier = pltpu.get_barrier_semaphore()
    for step, other in ctx_peers:
        pl.semaphore_signal(
            barrier, inc=1, device_id={"ctx": ctx_block(step, other)}, device_id_type=MESH
        )
    for first, second in exp_steps:
        pl.semaphore_signal(
            barrier, inc=1, device_id={"exp": exp_block(first, second, 0, 0)}, device_id_type=MESH
        )


def greet_wait(ctx_peers, exp_steps):
    pl.semaphore_wait(pltpu.get_barrier_semaphore(), len(ctx_peers) + len(exp_steps))


NEIGHBOURS = ((1, 0), (-1, 0), (0, 1), (0, -1))
LINES_OF = NEIGHBOURS + ((2, 0), (0, 2))
STEPS = (1, -1, 2)


def to_ctx(src, dst, send, recv, peer):
    return pltpu.make_async_remote_copy(
        src_ref=src,
        dst_ref=dst,
        send_sem=send,
        recv_sem=recv,
        device_id={"ctx": ctx_block(*peer)},
        device_id_type=MESH,
    )


def gather_exp_stages(own, out, send, recv):
    rows = own.shape[0]
    copies = {
        (half, axis, k, s): gather_exp_copy(own, out, send, recv, rows, half, axis, k, s)
        for half in range(2)
        for axis, k in ((1, 0), (2, 0), (2, 1), (2, -1), (2, 2))
        for s in range(4)
    }

    def begin():
        for axis in (1, 2):
            for s in (0, 1):
                for half in range(2):
                    copies[half, axis, 0, s].start()

    def first(s, k):
        for half in range(2):
            copies[half, 1, 0, s].wait_recv()
            copies[half, 1, 0, s + 2].start()
            copies[half, 2, k, 0].start()
            copies[half, 2, k, 1].start()

    def middle():
        for half in range(2):
            copies[half, 1, 0, 2].wait_recv()
            copies[half, 1, 0, 3].wait_recv()
            copies[half, 2, 2, 0].start()
            copies[half, 2, 2, 1].start()

    def forward(k):
        for s in (0, 1):
            for half in range(2):
                copies[half, 2, k, s].wait_recv()
                copies[half, 2, k, s + 2].start()

    def last():
        for k in (0, -1, 1, 2):
            for s in (2, 3):
                for half in range(2):
                    copies[half, 2, k, s].wait_recv()

    def sent():
        for copy in copies.values():
            copy.wait_send()

    steps = [
        begin,
        lambda: first(0, -1),
        lambda: first(1, 1),
        lambda: forward(0),
        middle,
        lambda: forward(-1),
        lambda: forward(1),
        lambda: forward(2),
        last,
    ]
    return steps, sent


def relay_exp_steps(own, out, send, recv):
    part = own.shape[0] // 2
    copies = {}
    for half in range(2):
        lines = pl.ds(half * part, part)
        for axis, k in ((1, 0), (2, 0), (2, 1), (2, -1), (2, 2)):
            origin = exp_block(k, 0, half, 0)
            for s, step in enumerate(STEPS):
                target = exp_block(step, 0, half, 0) if axis == 1 else exp_block(0, step, half, 0)
                at = half * 15 + (s if axis == 1 else 3 + 3 * (k % 4) + s)
                copies[half, axis, k, s] = pltpu.make_async_remote_copy(
                    src_ref=own.at[lines] if k == 0 else out.at[origin, lines],
                    dst_ref=out.at[origin, lines],
                    send_sem=send.at[at],
                    recv_sem=recv.at[at],
                    device_id={"exp": target},
                    device_id_type=MESH,
                )

    def begin():
        for axis in (1, 2):
            for s in range(3):
                for half in range(2):
                    copies[half, axis, 0, s].start()

    def relay():
        for s, k in ((0, -1), (1, 1), (2, 2)):
            for half in range(2):
                copies[half, 1, 0, s].wait_recv()
                for t in range(3):
                    copies[half, 2, k, t].start()

    def last():
        for half in range(2):
            for k in (0, -1, 1, 2):
                for s in range(3):
                    copies[half, 2, k, s].wait_recv()

    def sent():
        for copy in copies.values():
            copy.wait_send()

    return begin, relay, last, sent


def start_kernel(
    tokens, cot, w_gate, w_up, w_down, w_query, w_key, w_value, w_out, narrow, routes,
    attn_in, q_t, q_s, k_s, k_t, v_s, lse, exact, mixed_rows,
    head_w, misc_t, full_out, resid, moe_in, all_cot, all_routes, all_experts,
    land, own_experts, down_in, w_block, w_all, o_rows, o_all, w_wide, o_wide, misc, v_t, mixed, mixed_land, pieces, out_piece,
    exp_send, exp_recv, ctx_send, ctx_recv, ring_send, ring_recv, local,
):
    me = lax.axis_index("ctx")
    own = exp_block(0, 0, 0, 0)
    greet_signal(PEERS, LINES_OF)
    loads = [
        pltpu.make_async_copy(w_gate, own_experts.at[pl.ds(0, 2)], local.at[0]),
        pltpu.make_async_copy(w_up, own_experts.at[pl.ds(2, 2)], local.at[1]),
        pltpu.make_async_copy(w_down, down_in, local.at[2]),
        pltpu.make_async_copy(tokens, land.at[me], local.at[3]),
        pltpu.make_async_copy(cot, all_cot.at[own], local.at[4]),
    ]
    for load in loads:
        load.start()
    query = w_query[...].astype(F32)
    key = w_key[...].astype(F32)
    value = w_value[...].astype(F32)
    rest = jnp.concatenate([narrow[...], jnp.zeros((8, 128), F32)], axis=0).astype(BF16)
    for c in range(8):
        pair = [key[:, c * 64 : (c + 1) * 64], value[:, c * 64 : (c + 1) * 64]]
        columns = [query[:, c * 128 : (c + 1) * 128], jnp.concatenate(pair, axis=1)]
        pieces[c, 0:16] = jnp.concatenate(columns, axis=0).astype(BF16)
        pieces[c, 16:32] = rest
    wide = w_out[...].astype(F32)
    for t in range(4):
        columns = [wide[:, 256 * t : 256 * t + 128], wide[:, 256 * t + 128 : 256 * t + 256]]
        out_piece[t * 16 : (t + 1) * 16] = jnp.concatenate(columns, axis=0).astype(BF16)
    listed = jnp.concatenate([routes[...].astype(F32), jnp.zeros((ROWS, 120), F32)], axis=1).T[:8]
    listed = jnp.concatenate([listed[:, :128], listed[:, 128:]], axis=0)
    w_block[256:288] = jnp.concatenate([listed, jnp.zeros((16, 128), F32)], axis=0).astype(BF16)
    greet_wait(PEERS, LINES_OF)
    piece_copies = [
        to_ctx(
            pieces.at[ctx_block(*peer)], w_block.at[pl.ds(me * 32, 32)],
            ctx_send.at[0, at], ctx_recv.at[0, at], peer,
        )
        for at, peer in enumerate(PEERS)
    ]
    for copy in piece_copies:
        copy.start()
    ring = gather_ctx_copies(tokens, land, ring_send.at[0], ring_recv.at[0])
    for at in RING_START:
        ring[at].start()
    w_block[pl.ds(pl.multiple_of(me * 32, 32), 32)] = pieces[me]
    w_begin, w_relay, w_last, w_sent = relay_exp_steps(
        w_block, w_all, exp_send.at[0], exp_recv.at[0]
    )
    o_begin, o_relay, o_last, o_sent = relay_exp_steps(
        out_piece, o_rows, exp_send.at[1], exp_recv.at[1]
    )
    c_steps, c_sent = gather_exp_stages(cot, all_cot, exp_send.at[2], exp_recv.at[2])
    c_steps[0]()
    o_begin()
    o_rows[own] = out_piece[...]
    for copy in piece_copies:
        copy.wait_recv()
    w_begin()
    w_keep = pltpu.make_async_copy(w_block, w_all.at[own], local.at[5])
    w_keep.start()
    o_relay()
    w_relay()
    ring_follow(ring, 1, 2)
    for at in (0, 1, 2):
        loads[at].wait()
    for k in range(2):
        own_experts[4 + k] = down_in[k].astype(F32).T.astype(BF16)
    w_ring = gather_ctx_copies(own_experts, all_experts, ring_send.at[1], ring_recv.at[1])
    w_ring[1].start()
    w_ring[2].start()
    w_ring_keep = pltpu.make_async_copy(own_experts, all_experts.at[me], local.at[7])
    w_ring_keep.start()
    w_last()
    w_keep.wait()

    @pl.loop(0, 128)
    def _(i):
        x, c = lax.div(i, 8), lax.rem(i, 8)
        at = pl.ds(pl.multiple_of(c * 128 + x * 8, 8), 8)
        line = pl.multiple_of(c * 32, 32)
        first = w_all[x, pl.ds(line, 16)].astype(F32)
        second = w_all[x, pl.ds(line + 16, 16)].astype(F32)
        w_wide[at, 0:128] = first[:8]
        w_wide[at, 128:256] = first[8:]
        misc[at] = second[:8]

    all_routes[...] = w_all[:, 256:272]
    head_w[...] = w_wide[...].astype(BF16)

    @pl.loop(0, 8)
    def _(c):
        at = pl.ds(pl.multiple_of(c * 128, 128), 128)
        misc_t[:, at] = misc[at].T[:40]

    def project(i):
        at = pl.ds(pl.multiple_of(i * ROWS, ROWS), ROWS)
        x = land[i].astype(F32)
        x = x * lax.rsqrt(jnp.mean(x * x, axis=1, keepdims=True) + EPSILON) * misc_t[33:34]
        x = x.astype(BF16)
        attn_in[at] = x
        qkv = dot(x, head_w[...]).astype(BF16).astype(F32)
        q = qkv[:, :128] * 0.125
        k, v = qkv[:, 128:192], qkv[:, 192:]
        q_s[i] = one_below(q).astype(BF16)
        q_t[i] = side_by_side(q.T).astype(BF16)
        k_s[i] = k.astype(BF16)
        v_s[i] = v.astype(BF16)
        kv_t = qkv[:, 128:].T
        k_t[i] = kv_t[:64].astype(BF16)
        v_t[i] = kv_t[64:].astype(BF16)

    loads[3].wait()
    ring_follow(ring, 3, 4)
    for at in (3, 4, 0):
        w_ring[at].start()
    o_last()
    o_ring = gather_ctx_copies(o_rows, o_all, ring_send.at[2], ring_recv.at[2])
    for at in RING_START:
        o_ring[at].start()
    o_keep = pltpu.make_async_copy(o_rows, o_all.at[me], local.at[6])
    o_keep.start()
    project(ctx_block(0, False))
    c_steps[1]()
    ring[0].wait_recv()
    project(ctx_block(0, True))
    ring_follow(ring, 5, 6)
    c_steps[2]()
    project(ctx_block(-1, False))
    project(ctx_block(1, False))
    c_steps[3]()
    for at in (7, 8):
        ring[at].wait_recv()
    project(ctx_block(-1, True))
    for at in (9, 10):
        ring[at].wait_recv()
    project(ctx_block(1, True))
    ring_follow(w_ring, 1, 2)
    project(ctx_block(2, False))
    for at in (11, 12):
        ring[at].wait_recv()
    project(ctx_block(2, True))
    c_steps[4]()

    key_row = lax.broadcasted_iota(jnp.int32, (ROWS, 2 * ROWS), 0)
    query_row = lax.rem(lax.broadcasted_iota(jnp.int32, (ROWS, 2 * ROWS), 1), ROWS)
    seen = key_row <= query_row

    def tile(i):
        query = q_t[i]

        def add_block(j, carry, diagonal):
            top, total, acc = carry
            scores = dot(k_s[j], query)
            if diagonal:
                scores = jnp.where(seen, scores, -1e30)
            new_top = jnp.maximum(top, jnp.max(scores, axis=0, keepdims=True))
            fade = jnp.exp(top - new_top)
            weights = jnp.exp(scores - new_top)
            total = total * fade + jnp.sum(weights, axis=0, keepdims=True)
            acc = acc * fade + dot(v_t[j], weights.astype(BF16))
            return new_top, total, acc

        carry = (
            jnp.full((1, 2 * ROWS), -1e30, F32),
            jnp.zeros((1, 2 * ROWS), F32),
            jnp.zeros((64, 2 * ROWS), F32),
        )
        carry = lax.fori_loop(0, i, lambda j, c: add_block(j, c, False), carry)
        top, total, acc = add_block(i, carry, True)
        lse[i] = top + jnp.log(total)
        value = acc / total
        exact[i] = value
        both = jnp.concatenate([value[:, :ROWS], value[:, ROWS:]], axis=0)
        mixed[i] = both.T.astype(BF16)

    def unpack_out():
        o_keep.wait()
        for at in (0, 7, 8, 9, 10, 11, 12):
            o_ring[at].wait_recv()

        @pl.loop(0, 128)
        def _(i):
            x, c = lax.div(i, 8), lax.rem(i, 8)
            at = pl.ds(pl.multiple_of(c * 128 + x * 8, 8), 8)
            for t in range(4):
                both = o_all[c, x, t * 16 : t * 16 + 16].astype(F32)
                o_wide[at, 256 * t : 256 * t + 128] = both[:8]
                o_wide[at, 256 * t + 128 : 256 * t + 256] = both[8:]

        full_out[...] = o_wide[...].astype(BF16)

    between = (
        (lambda: ring_follow(w_ring, 3, 4), lambda: ring_follow(o_ring, 1, 2)),
        (c_steps[5], lambda: ring_follow(o_ring, 3, 4)),
        (c_steps[6], lambda: ring_follow(w_ring, 5, 6)),
        (c_steps[7], lambda: ring_follow(o_ring, 5, 6)),
        (),
        (unpack_out,),
        (),
    )
    mixed_copies = []
    for at, peer in enumerate(PEERS):
        i = ctx_block(*peer)
        tile(i)
        copy = to_ctx(
            mixed.at[i], mixed_land.at[me], ctx_send.at[2, at], ctx_recv.at[2, at], peer
        )
        copy.start()
        mixed_copies.append(copy)
        for step in between[at]:
            step()
    tile(me)
    mixed_land[me] = mixed[me]
    total = tokens[...].astype(F32)
    for copy in mixed_copies:
        copy.wait_recv()
    for c in range(4):
        pair = jnp.concatenate([mixed_land[2 * c], mixed_land[2 * c + 1]], axis=1)
        total = total + dot(pair, full_out[c * 256 : (c + 1) * 256])
    mixed_rows[...] = mixed_land[...]
    resid[...] = total
    scaled = total * lax.rsqrt(jnp.mean(total * total, axis=1, keepdims=True) + EPSILON)
    scaled = (scaled * misc_t[32:33]).astype(BF16)
    for q in range(4):
        moe_in[q] = scaled[:, q * 256 : (q + 1) * 256]
    c_steps[8]()
    for at in (0, 7, 8, 9, 10, 11, 12):
        w_ring[at].wait_recv()
    w_ring_keep.wait()
    loads[4].wait()
    w_sent()
    o_sent()
    c_sent()
    for copy in (*piece_copies, *ring, *w_ring, *o_ring, *mixed_copies):
        copy.wait_send()


def start(args, collective_id):
    anywhere = pl.BlockSpec(memory_space=pl.ANY)
    outs = [
        ((2048, 1024), BF16, vmem()),
        ((8, 64, 512), BF16, vmem()),
        ((8, 512, 64), BF16, vmem()),
        ((8, 256, 64), BF16, vmem()),
        ((8, 64, 256), BF16, vmem()),
        ((8, 256, 64), BF16, vmem()),
        ((8, 1, 512), F32, vmem()),
        ((8, 64, 512), F32, vmem()),
        ((8, 256, 128), BF16, vmem()),
        ((1024, 256), BF16, vmem()),
        ((40, 1024), F32, vmem()),
        ((1024, 1024), BF16, vmem()),
        ((256, 1024), F32, vmem()),
        ((4, 256, 256), BF16, vmem()),
        ((16, 256, 1024), BF16, anywhere),
        ((16, 16, 128), BF16, vmem()),
        ((8, 6, 128, 512), BF16, anywhere),
    ]
    dma = pltpu.SemaphoreType.DMA
    return pl.pallas_call(
        start_kernel,
        out_shape=[jax.ShapeDtypeStruct(s, t) for s, t, _ in outs],
        in_specs=[vmem()] + [anywhere] * 4 + [vmem()] * 6,
        out_specs=[spec for _, _, spec in outs],
        scratch_shapes=[
            VMEM((8, 256, 1024), BF16),
            VMEM((6, 128, 512), BF16),
            VMEM((2, 512, 128), BF16),
            VMEM((288, 128), BF16),
            VMEM((16, 288, 128), BF16),
            VMEM((16, 64, 128), BF16),
            VMEM((8, 16, 64, 128), BF16),
            VMEM((1024, 256), F32),
            VMEM((1024, 1024), F32),
            VMEM((1024, 128), F32),
            VMEM((8, 64, 256), BF16),
            VMEM((8, 256, 128), BF16),
            VMEM((8, 256, 128), BF16),
            VMEM((8, 32, 128), BF16),
            VMEM((64, 128), BF16),
            dma((3, 40)),
            dma((3, 40)),
            dma((3, 7)),
            dma((3, 7)),
            dma((3, 13)),
            dma((3, 13)),
            dma((8,)),
        ],
        compiler_params=pltpu.CompilerParams(
            collective_id=collective_id, has_side_effects=True, vmem_limit_bytes=56 << 20
        ),
    )(*args)

ORDER = (0, 2, 1, -1)
LINES = ROWS + 16


def part_gather_copies(own, held, send, recv):
    copies = {}
    for half in range(2):
        for axis, k in ((1, 0), (2, 0), (2, 1), (2, -1), (2, 2)):
            for s in range(4):
                step = (1, -1, 1, -1)[s]
                off = (0, 0, -1, 1)[s]
                origin = exp_block(off, 0, half, 0) if axis == 1 else exp_block(k, off, half, 0)
                target = exp_block(step, 0, half, 0) if axis == 1 else exp_block(0, step, half, 0)
                first, count = (2 * half, 2) if s < 2 else (2 * half + s - 2, 1)
                place = held.at[pl.ds(origin * 4 + first, count), pl.ds(0, ROWS)]
                mine = s < 2 and (axis == 1 or k == 0)
                at = half * 20 + (s if axis == 1 else 4 + 4 * (k % 4) + s)
                copies[half, axis, k, s] = pltpu.make_async_remote_copy(
                    src_ref=own.at[pl.ds(first, count)] if mine else place,
                    dst_ref=place,
                    send_sem=send.at[at],
                    recv_sem=recv.at[at],
                    device_id={"exp": target},
                    device_id_type=MESH,
                )
    return copies


def part_reduce_copies(parts, held, send, recv):
    copies = {}
    for half in range(2):
        for axis, k in ((1, 0), (1, 1), (1, -1), (1, 2), (2, 0)):
            row = half * 5 + (k % 4 if axis == 1 else 4)
            for s in range(4):
                step = (1, -1, 1, -1)[s]
                dest = (2, 2, 1, -1)[s]
                block = exp_block(dest, k, half, 1) if axis == 1 else exp_block(0, dest, half, 1)
                target = exp_block(step, 0, half, 1) if axis == 1 else exp_block(0, step, half, 1)
                first, count = (2 * half + s, 1) if s < 2 else (2 * half, 2)
                at = row * 4 + s
                copies[half, axis, k, s] = pltpu.make_async_remote_copy(
                    src_ref=parts.at[pl.ds(block * 4 + first, count)],
                    dst_ref=held.at[pl.ds(row * 6 + (0, 1, 2, 4)[s], count)],
                    send_sem=send.at[at],
                    recv_sem=recv.at[at],
                    device_id={"exp": target},
                    device_id_type=MESH,
                )
    return copies


def moe_kernel(
    moe, misc, routes, cot, experts, head_w,
    grad_total, out_parts, terms, all_w,
    held, parts, weights, cots, x_rows, c_rows, hidden, gate_g, up_g, pick,
    gated, row_g, stage, term_stage, slot_gates, slot_grads,
    gather_send, gather_recv, reduce_send, reduce_recv, cot_sem, stage_sem, term_sem, local, ready, ring_send, ring_recv,
):
    own = exp_block(0, 0, 0, 0)
    beside = ((1, False), (-1, False), (0, True))
    greet_signal(beside, NEIGHBOURS)

    def block_of(group, o):
        return exp_block(o, group, 0, 0)

    def cot_load(n, o):
        return pltpu.make_async_copy(cot.at[block_of(ORDER[n], o)], cots.at[o], cot_sem.at[o])

    weight_load = pltpu.make_async_copy(experts, weights, local.at[0])
    weight_load.start()
    for o in range(4):
        cot_load(0, o).start()
    keep = pltpu.make_async_copy(
        moe, held.at[pl.ds(own * 4, 4), pl.ds(0, ROWS)], local.at[1]
    )
    keep.start()
    w_keep = pltpu.make_async_copy(head_w, all_w.at[lax.axis_index("ctx")], local.at[2])
    w_keep.start()
    greet_wait(beside, NEIGHBOURS)
    ring = gather_ctx_copies(head_w, all_w, ring_send, ring_recv)
    gathers = part_gather_copies(moe, held, gather_send, gather_recv)
    reduces = part_reduce_copies(parts, held, reduce_send, reduce_recv)
    router = misc[0:32].astype(BF16)

    def listed_at(b):
        listed = routes[b].astype(F32).astype(jnp.int32)
        return jnp.concatenate([listed[:8], listed[8:]], axis=1)

    def prepare(n):
        before = lax.broadcasted_iota(jnp.int32, (ROWS, ROWS), 0) < lax.broadcasted_iota(
            jnp.int32, (ROWS, ROWS), 1
        )
        before = jnp.where(before, 1.0, 0.0).astype(BF16)
        slot = lax.broadcasted_iota(jnp.int32, (CAP, ROWS), 0).astype(F32)

        @pl.loop(0, 4)
        def _(o):
            listed = listed_at(block_of(ORDER[n], o))
            named = [
                jnp.sum(jnp.where(listed == 2 * own + k, 1.0, 0.0), axis=0, keepdims=True)
                for k in range(2)
            ]
            flat = jnp.concatenate(named + [jnp.zeros((6, ROWS), F32)], axis=0)
            place = dot(flat.astype(BF16), before)
            spread = []
            for k in range(2):
                hit = (slot == place[k : k + 1]) & (named[k] > 0.5)
                spread.append(jnp.where(hit, 1.0, 0.0).astype(BF16))
            both = jnp.concatenate(spread, axis=0)
            pick[n, o] = both
            cot_load(n, o).wait()
            for q in range(4):
                at = slice(q * 256, (q + 1) * 256)
                grads = dot(both, cots[o, :, at]).astype(BF16)
                for k in range(2):
                    c_rows[k, n, o, :, at] = grads[k * CAP : (k + 1) * CAP]
            if n < 3:
                cot_load(n + 1, o).start()

    def dispatch(n):
        expert = lax.broadcasted_iota(jnp.int32, (32, ROWS), 0)

        @pl.loop(0, 4)
        def _(o):
            b = block_of(ORDER[n], o)
            both = pick[n, o]
            logits = jnp.zeros((32, ROWS), F32)
            for q in range(4):
                rows = held[b * 4 + q, 0:ROWS]
                logits = logits + dot(router[:, q * 256 : (q + 1) * 256], rows, ((1,), (1,)))
                rows = dot(both, rows).astype(BF16)
                for k in range(2):
                    x_rows[k, n, o, :, q * 256 : (q + 1) * 256] = rows[k * CAP : (k + 1) * CAP]
            listed = listed_at(b)
            chosen = expert < 0
            for j in range(8):
                chosen = chosen | (listed[j : j + 1] == expert)
            logits = jnp.where(chosen, logits, -1e30)
            weight = jnp.exp(logits - jnp.max(logits, axis=0, keepdims=True))
            weight = jnp.where(chosen, weight, 0.0)
            weight = weight / jnp.sum(weight, axis=0, keepdims=True)
            lines = pl.ds(pl.multiple_of(o * CAP, CAP), CAP)
            for k in range(2):
                mine = jnp.where(expert == 2 * own + k, weight, 0.0)
                gate = jnp.sum(mine, axis=0, keepdims=True)
                hits = both[k * CAP : (k + 1) * CAP].astype(F32)
                slot_gates[n, k, lines] = jnp.sum(hits * gate, axis=1, keepdims=True)

    def matrix(kind, k):
        return weights[:, 2 * kind + k].reshape(1024, 512)

    def expert(n, k):
        x = x_rows[k, n].reshape(GROUP * CAP, 1024)
        c = c_rows[k, n].reshape(GROUP * CAP, 1024)
        gate = slot_gates[n, k]
        g = dot(x, matrix(0, k))
        u = dot(x, matrix(1, k))
        s = jax.nn.sigmoid(g)
        silu = g * s
        h = (silu * u).astype(BF16)
        hidden[k, n] = h
        y = dot(h, matrix(2, k), ((1,), (1,))).astype(BF16).astype(F32)
        gated[k] = (gate * y).astype(BF16)
        c = c.astype(F32)
        slot_grads[k] = jnp.sum(c * y, axis=1, keepdims=True)
        dy = (gate * c).astype(BF16)
        c_rows[k, n] = dy.reshape(GROUP, CAP, 1024)
        dh = dot(dy, matrix(2, k))
        gg = (dh * u * s * (1.0 + g * (1.0 - s))).astype(BF16)
        ug = (dh * silu).astype(BF16)
        gate_g[k, n] = gg
        up_g[k, n] = ug
        row_g[k] = (
            dot(gg, matrix(0, k), ((1,), (1,))) + dot(ug, matrix(1, k), ((1,), (1,)))
        ).astype(BF16)

    def stage_copy(b, o):
        slot = lax.rem(o, 2)
        return pltpu.make_async_copy(stage.at[slot], out_parts.at[b], stage_sem.at[slot])

    def combine(n, first=False):
        owner_row = lax.broadcasted_iota(jnp.int32, (16, ROWS), 0) == own

        @pl.loop(0, 4)
        def _(o):
            b = block_of(ORDER[n], o)
            lines = pl.ds(pl.multiple_of(o * CAP, CAP), CAP)
            chosen = pick[n, o]

            def spread(rows):
                both = jnp.concatenate([rows[0, lines], rows[1, lines]], axis=0)
                return dot(chosen, both, ((0,), (0,))).astype(BF16)

            total = spread(row_g)
            for q in range(4):
                parts[b * 4 + q, 0:ROWS] = total[:, q * 256 : (q + 1) * 256]
            for k in range(2):
                hits = chosen[k * CAP : (k + 1) * CAP].astype(F32)
                vector = jnp.sum(hits * slot_grads[k, lines], axis=0, keepdims=True)
                high = vector.astype(BF16).astype(F32)
                for q, value in ((2 * k, high), (2 * k + 1, vector - high)):
                    parts[b * 4 + q, ROWS:LINES] = jnp.where(owner_row, value, 0.0).astype(BF16)
            total = spread(gated)
            if first:

                @pl.when(o >= 2)
                def _():
                    stage_copy(b, o).wait()

            else:
                stage_copy(b, o).wait()
            slot = lax.rem(o, 2)
            for q in range(4):
                stage[slot, q] = total[:, q * 256 : (q + 1) * 256]
            stage_copy(b, o).start()

    def add(target, *landed):
        value = parts[target].astype(F32)
        for at in landed:
            value = value + held[at].astype(F32)
        parts[target] = value.astype(BF16)

    def row_of(half, axis, k):
        return (half * 5 + (k % 4 if axis == 1 else 4)) * 6

    def block_at(half, axis, k, dest):
        return exp_block(dest, k, half, 1) if axis == 1 else exp_block(0, dest, half, 1)

    def send_far(half, axis, k):
        reduces[half, axis, k, 0].start()
        reduces[half, axis, k, 1].start()

    def pass_on(half, axis, k, s):
        reduces[half, axis, k, s].wait_recv()
        block = block_at(half, axis, k, 1 - 2 * s)
        add(block * 4 + 2 * half + s, row_of(half, axis, k) + s)
        reduces[half, axis, k, s + 2].start()

    def finish(half, axis, k):
        reduces[half, axis, k, 2].wait_recv()
        reduces[half, axis, k, 3].wait_recv()
        row = row_of(half, axis, k)
        for part in range(2):
            target = block_at(half, axis, k, 0) * 4 + 2 * half + part
            add(target, row + 2 + part, row + 4 + part)

    def term_copy(kind, k, tile):
        return pltpu.make_async_copy(
            term_stage.at[tile], terms.at[pl.ds(2 * tile, 2), 2 * kind + k], term_sem.at[tile]
        )

    def term(kind, k, first=False):
        left = c_rows if kind == 2 else x_rows
        right = (gate_g, up_g, hidden)[kind]

        @pl.loop(0, 4)
        def _(tile):
            at = pl.ds(pl.multiple_of(tile * 256, 256), 256)
            rows = left[k, :, :, :, at].reshape(16 * CAP, 256)
            value = dot(rows, right[k].reshape(16 * CAP, 512), ((0,), (0,)))
            if not first:
                term_copy(kind, k, tile).wait()
            term_stage[tile] = value.astype(BF16).reshape(2, 128, 512)
            term_copy(kind, k, tile).start()

    def forward(k):
        for s in (0, 1):
            for half in range(2):
                gathers[half, 2, k, s].wait_recv()
                gathers[half, 2, k, s + 2].start()

    for axis in (1, 2):
        for s in (0, 1):
            for half in range(2):
                gathers[half, axis, 0, s].start()
    for at in RING_START:
        ring[at].start()
    prepare(0)
    for s, k in ((0, -1), (1, 1)):
        for half in range(2):
            gathers[half, 1, 0, s].wait_recv()
            gathers[half, 1, 0, s + 2].start()
            gathers[half, 2, k, 0].start()
            gathers[half, 2, k, 1].start()
    prepare(1)
    forward(0)
    for half in range(2):
        gathers[half, 1, 0, 2].wait_recv()
        gathers[half, 1, 0, 3].wait_recv()
        gathers[half, 2, 2, 0].start()
        gathers[half, 2, 2, 1].start()
    prepare(2)
    ring_follow(ring, 1, 2, 3, 4)
    forward(-1)
    prepare(3)
    forward(1)
    gathers[1, 2, 0, 2].wait_recv()
    gathers[1, 2, 0, 3].wait_recv()
    ring_follow(ring, 5, 6)
    keep.wait()
    weight_load.wait()
    dispatch(0)
    expert(0, 0)
    forward(2)
    expert(0, 1)
    combine(0, first=True)
    for half in range(2):
        for k in (0, -1, 1, 2):
            if (half, k) != (1, 0):
                gathers[half, 2, k, 2].wait_recv()
                gathers[half, 2, k, 3].wait_recv()
    dispatch(1)
    dispatch(2)
    dispatch(3)
    for copy in gathers.values():
        copy.wait_send()
    for first, second in NEIGHBOURS:
        pl.semaphore_signal(
            ready, inc=1, device_id={"exp": exp_block(first, second, 0, 0)}, device_id_type=MESH
        )
    expert(1, 0)
    expert(1, 1)
    combine(1)
    pl.semaphore_wait(ready, 4)
    send_far(1, 1, 2)
    send_far(0, 1, 2)
    send_far(0, 1, 1)
    send_far(0, 1, -1)
    send_far(0, 1, 0)
    send_far(1, 1, 0)
    expert(2, 0)
    pass_on(1, 1, 2, 0)
    pass_on(1, 1, 2, 1)
    expert(2, 1)
    combine(2)
    send_far(1, 1, 1)
    for k in (2, 1, -1, 0):
        pass_on(0, 1, k, 0)
    expert(3, 0)
    pass_on(1, 1, 0, 0)
    pass_on(1, 1, 0, 1)
    expert(3, 1)
    combine(3)
    send_far(1, 1, -1)
    for k in (2, 1, -1, 0):
        pass_on(0, 1, k, 1)
    pass_on(1, 1, 1, 0)
    pass_on(1, 1, 1, 1)
    term(0, 0, first=True)
    finish(1, 1, 2)
    send_far(1, 2, 0)
    pass_on(1, 1, -1, 0)
    pass_on(1, 1, -1, 1)
    term(0, 1)
    finish(0, 1, 2)
    send_far(0, 2, 0)
    finish(1, 1, 1)
    finish(0, 1, 1)
    term(1, 0)
    finish(1, 1, -1)
    finish(0, 1, -1)
    for half in (1, 0):
        pass_on(half, 2, 0, 0)
        pass_on(half, 2, 0, 1)
    term(1, 1)
    finish(1, 1, 0)
    finish(0, 1, 0)
    term(2, 0)
    term(2, 1)
    finish(1, 2, 0)
    finish(0, 2, 0)
    for q in range(4):
        grad_total[q] = parts[own * 4 + q]
    for copy in reduces.values():
        copy.wait_send()
    for at in (0, 7, 8, 9, 10, 11, 12):
        ring[at].wait_recv()
    for copy in ring:
        copy.wait_send()
    w_keep.wait()
    for o in range(2):
        stage_copy(own, o).wait()
    for tile in range(4):
        term_copy(0, 0, tile).wait()


def moe_block(moe, misc, routes, cot, experts, head_w, collective_id):
    anywhere = pl.BlockSpec(memory_space=pl.ANY)
    dma = pltpu.SemaphoreType.DMA
    return pl.pallas_call(
        moe_kernel,
        out_shape=[
            jax.ShapeDtypeStruct((4, LINES, 256), BF16),
            jax.ShapeDtypeStruct((16, 4, ROWS, 256), BF16),
            jax.ShapeDtypeStruct((8, 6, 128, 512), BF16),
            jax.ShapeDtypeStruct((8, 1024, 256), BF16),
        ],
        in_specs=[vmem(), vmem(), vmem(), anywhere, anywhere, anywhere],
        out_specs=[vmem(), anywhere, anywhere, anywhere],
        scratch_shapes=[
            VMEM((64, LINES, 256), BF16),
            VMEM((64, LINES, 256), BF16),
            VMEM((8, 6, 128, 512), BF16),
            VMEM((4, ROWS, 1024), BF16),
            VMEM((2, 4, GROUP, CAP, 1024), BF16),
            VMEM((2, 4, GROUP, CAP, 1024), BF16),
            VMEM((2, 4, GROUP * CAP, 512), BF16),
            VMEM((2, 4, GROUP * CAP, 512), BF16),
            VMEM((2, 4, GROUP * CAP, 512), BF16),
            VMEM((4, GROUP, 2 * CAP, ROWS), BF16),
            VMEM((2, GROUP * CAP, 1024), BF16),
            VMEM((2, GROUP * CAP, 1024), BF16),
            VMEM((2, 4, ROWS, 256), BF16),
            VMEM((4, 2, 128, 512), BF16),
            VMEM((4, 2, GROUP * CAP, 1), F32),
            VMEM((2, GROUP * CAP, 1), F32),
            dma((40,)),
            dma((40,)),
            dma((40,)),
            dma((40,)),
            dma((4,)),
            dma((2,)),
            dma((4,)),
            dma((3,)),
            pltpu.SemaphoreType.REGULAR,
            dma((13,)),
            dma((13,)),
        ],
        compiler_params=pltpu.CompilerParams(
            collective_id=collective_id, has_side_effects=True, vmem_limit_bytes=63 << 20
        ),
    )(moe, misc, routes, cot, experts, head_w)


def add_rows(target, others):
    shape = target.shape
    chunk = 1 if len(shape) == 3 else min(shape[0], 65536 // shape[1])

    def add(at):
        value = target[at].astype(F32)
        for other in others:
            value = value + other[at].astype(F32)
        target[at] = value.astype(target.dtype)

    if chunk == shape[0]:
        add(slice(None))
        return

    @pl.loop(0, shape[0] // chunk)
    def _(i):
        add(i if len(shape) == 3 else pl.ds(pl.multiple_of(i * chunk, chunk), chunk))


class ExpReduce:
    def __init__(self, parts, landed, send, recv):
        self.parts, self.landed = parts, landed
        self.copies = part_reduce_copies(parts, landed, send, recv)

    def block_at(self, half, axis, k, dest):
        return exp_block(dest, k, half, 1) if axis == 1 else exp_block(0, dest, half, 1)

    def row_of(self, half, axis, k):
        return (half * 5 + (k % 4 if axis == 1 else 4)) * 6

    def send_far(self, half, axis, k):
        self.copies[half, axis, k, 0].start()
        self.copies[half, axis, k, 1].start()

    def pass_on(self, half, axis, k):
        for s in (0, 1):
            self.copies[half, axis, k, s].wait_recv()
            line = self.block_at(half, axis, k, 1 - 2 * s) * 4 + 2 * half + s
            add_rows(self.parts.at[line], [self.landed.at[self.row_of(half, axis, k) + s]])
            self.copies[half, axis, k, s + 2].start()

    def finish(self, half, axis, k):
        self.copies[half, axis, k, 2].wait_recv()
        self.copies[half, axis, k, 3].wait_recv()
        row = self.row_of(half, axis, k)
        for part in range(2):
            line = self.block_at(half, axis, k, 0) * 4 + 2 * half + part
            add_rows(
                self.parts.at[line],
                [self.landed.at[row + 2 + part], self.landed.at[row + 4 + part]],
            )

    def steps(self):
        def begin():
            for k in (2, 1, -1, 0):
                for half in range(2):
                    self.send_far(half, 1, k)

        def both(action, axis, k):
            def run():
                for half in range(2):
                    action(half, axis, k)

            return run

        def far():
            for half in range(2):
                self.finish(half, 1, 2)
                self.send_far(half, 2, 0)

        return [
            begin,
            both(self.pass_on, 1, 2),
            both(self.pass_on, 1, 1),
            both(self.pass_on, 1, -1),
            both(self.pass_on, 1, 0),
            far,
            both(self.finish, 1, 1),
            both(self.finish, 1, -1),
            both(self.pass_on, 2, 0),
            both(self.finish, 1, 0),
            both(self.finish, 2, 0),
        ]

    def sent(self):
        for copy in self.copies.values():
            copy.wait_send()


class CtxReduce:
    STEPS = (2, 1, -1, 0)

    def __init__(self, given, mine, near, landed, send, recv):
        self.mine, self.near, self.landed = mine, near, landed
        half = near.shape[1] // 2
        self.first, self.second = pl.ds(0, half), pl.ds(half, half)
        self.swaps = [
            to_ctx(
                given.at[ctx_block(step, True)], near.at[at], send.at[at], recv.at[at], (0, True)
            )
            for at, step in enumerate(self.STEPS)
        ]
        self.hops = [
            to_ctx(src, dst, send.at[4 + at], recv.at[4 + at], (step, False))
            for at, (src, dst, step) in enumerate(
                (
                    (mine[0].at[self.first], landed.at[0, self.first], 1),
                    (mine[0].at[self.second], landed.at[0, self.second], -1),
                    (mine[1], landed.at[1], 1),
                    (mine[2], landed.at[2], -1),
                )
            )
        ]

    def swap(self):
        for copy in self.swaps:
            copy.start()

    def take(self, at):
        self.swaps[at].wait_recv()
        add_rows(self.mine[at], [self.near.at[at]])

    def far(self):
        self.take(0)
        self.hops[0].start()
        self.hops[1].start()

    def sides(self):
        self.take(1)
        self.take(2)

    def pass_on(self):
        for at, part in ((0, self.first), (1, self.second)):
            self.hops[at].wait_recv()
            add_rows(self.mine[1 + at].at[part], [self.landed.at[0, part]])
            self.hops[2 + at].start()

    def finish(self):
        self.take(3)
        self.hops[2].wait_recv()
        self.hops[3].wait_recv()
        add_rows(self.mine[3], [self.landed.at[1], self.landed.at[2]])

    def sent(self):
        for copy in (*self.swaps, *self.hops):
            copy.wait_send()


class LineReduce:
    def __init__(self, parts, landed, send, recv):
        self.parts, self.landed = parts, landed
        self.copies = {}
        for half in range(2):
            for axis, k in ((1, 0), (1, 1), (1, -1), (1, 2), (2, 0)):
                for s, step in enumerate(STEPS):
                    block = self.block_at(half, axis, k, step)
                    target = exp_block(step, 0, half, 1) if axis == 1 else exp_block(0, step, half, 1)
                    row = self.row_of(half, axis, k, s)
                    self.copies[half, axis, k, s] = pltpu.make_async_remote_copy(
                        src_ref=parts.at[pl.ds(block * 4 + 2 * half, 2)],
                        dst_ref=landed.at[pl.ds(2 * row, 2)],
                        send_sem=send.at[row],
                        recv_sem=recv.at[row],
                        device_id={"exp": target},
                        device_id_type=MESH,
                    )

    def block_at(self, half, axis, k, dest):
        return exp_block(dest, k, half, 1) if axis == 1 else exp_block(0, dest, half, 1)

    def row_of(self, half, axis, k, s):
        return half * 15 + (3 * (k % 4) if axis == 1 else 12) + s

    def send(self, axis):
        for k in (2, 1, -1, 0) if axis == 1 else (0,):
            for s in range(3):
                for half in range(2):
                    self.copies[half, axis, k, s].start()

    def take(self, axis):
        for k in (2, 1, -1, 0) if axis == 1 else (0,):
            for half in range(2):
                rows = []
                for s in range(3):
                    self.copies[half, axis, k, s].wait_recv()
                    rows.append(2 * self.row_of(half, axis, k, s))
                line = self.block_at(half, axis, k, 0) * 4 + 2 * half
                for part in range(2):
                    add_rows(
                        self.parts.at[line + part], [self.landed.at[row + part] for row in rows]
                    )

    def sent(self):
        for copy in self.copies.values():
            copy.wait_send()


def split_dot(value, other, dims):
    high = value.astype(BF16)
    low = (value - high.astype(F32)).astype(BF16)
    return dot(high, other, dims) + dot(low, other, dims)


def norm_back(values, grads, gain):
    r = lax.rsqrt(jnp.mean(values * values, axis=1, keepdims=True) + EPSILON)
    n = values * r
    scaled = grads * gain
    back = r * (scaled - n * jnp.mean(scaled * n, axis=1, keepdims=True))
    return back, n


def finish_kernel(
    grad_total, resid, misc, routes, moe, cot, tokens, full_out, mixed_rows,
    q_t, q_s, k_s, k_t, v_s, lse, exact, attn_in, out_parts, terms, all_w,
    output, token_grad, head_sum, out_sum, term_sum,
    o_parts, o_landed, t_mine, t_near, t_landed, attn_grad, resid_grad, mg_out, mg_land,
    p_given, p_near, p_landed, out_s, out_t, delta, dq, d, d_land, w_full,
    head_acc, small, w_parts, w_landed, wide_small, f_given, f_land, attn_rows,
    o_send, o_recv, w_send, w_recv, ctx_send, ctx_recv, direct_send, direct_recv, local, rows_sem, d_send, d_recv,
):
    me = lax.axis_index("ctx")
    own = exp_block(0, 0, 0, 0)
    greet_signal(PEERS, LINES_OF)
    o_load = pltpu.make_async_copy(out_parts, o_parts, local.at[0])
    o_load.start()
    t_loads = [
        pltpu.make_async_copy(terms.at[ctx_block(step, False)], t_mine.at[at], local.at[1 + at])
        for at, step in enumerate(CtxReduce.STEPS)
    ]
    for load in t_loads:
        load.start()

    def rows_load(j):
        return pltpu.make_async_copy(
            attn_in.at[pl.ds(j * ROWS, ROWS)], attn_rows.at[j % 2], rows_sem.at[j % 2]
        )

    rows_load(0).start()
    w_load = pltpu.make_async_copy(all_w, w_full, local.at[5])
    w_load.start()
    out_reduce = ExpReduce(o_parts, o_landed, o_send, o_recv)
    o_steps = out_reduce.steps()
    term_reduce = CtxReduce(
        terms, [t_mine.at[at] for at in range(4)], t_near, t_landed, ctx_send.at[0], ctx_recv.at[0]
    )
    proj_reduce = CtxReduce(
        p_given, [p_given.at[ctx_block(step, False)] for step in CtxReduce.STEPS],
        p_near, p_landed, ctx_send.at[1], ctx_recv.at[1],
    )

    place = lax.broadcasted_iota(jnp.int32, (32, ROWS), 0)
    expert = 2 * lax.rem(place, 16) + lax.div(place, 16)
    order = lax.broadcasted_iota(jnp.int32, (32, 32), 0)
    order = 2 * lax.rem(order, 16) + lax.div(order, 16)
    order = order == lax.broadcasted_iota(jnp.int32, (32, 32), 1)
    router = dot(jnp.where(order, 1.0, 0.0).astype(BF16), misc[0:32].astype(BF16)).astype(BF16)
    listed = routes[own].astype(F32).astype(jnp.int32)
    listed = jnp.concatenate([listed[:8], listed[8:]], axis=1)
    chosen = expert < 0
    for j in range(8):
        chosen = chosen | (listed[j : j + 1] == expert)
    logits = jnp.zeros((32, ROWS), F32)
    for q in range(4):
        logits = logits + dot(router[:, q * 256 : (q + 1) * 256], moe[q], ((1,), (1,)))
    logits = jnp.where(chosen, logits, -1e30)
    gates = jnp.exp(logits - jnp.max(logits, axis=0, keepdims=True))
    gates = jnp.where(chosen, gates, 0.0)
    gates = gates / jnp.sum(gates, axis=0, keepdims=True)
    weight_grad = [grad_total[q, ROWS:LINES].astype(F32) for q in range(4)]
    weight_grad = jnp.concatenate(
        [weight_grad[0] + weight_grad[1], weight_grad[2] + weight_grad[3]], axis=0
    )
    logit_grad = gates * (weight_grad - jnp.sum(gates * weight_grad, axis=0, keepdims=True))
    logit_grad = jnp.where(chosen, logit_grad, 0.0)
    moe_in_grad = jnp.concatenate(
        [grad_total[q, 0:ROWS].astype(F32) for q in range(4)], axis=1
    )
    moe_in_grad = moe_in_grad + split_dot(logit_grad, router, ((0,), (0,)))
    greet_wait(PEERS, LINES_OF)
    term_reduce.swap()
    o_load.wait()
    o_steps[0]()
    back, n = norm_back(resid[...], moe_in_grad, misc[32:33])
    total = back + cot[...].astype(F32)
    resid_grad[...] = total
    attn_grad[...] = total.astype(BF16)
    mixed_grad = dot(attn_grad[...], full_out[...], ((1,), (1,))).astype(BF16)
    for c in range(8):
        mg_out[c] = mixed_grad[:, c * 128 : (c + 1) * 128]
    mg_copies = [
        to_ctx(
            mg_out.at[ctx_block(*peer)], mg_land.at[me],
            direct_send.at[0, at], direct_recv.at[0, at], peer,
        )
        for at, peer in enumerate(PEERS)
    ]
    for copy in mg_copies:
        copy.start()
    for load in t_loads:
        load.wait()
    term_reduce.far()
    mg_land[me] = mg_out[me]
    for c in range(8):
        p_given[c] = dot(mixed_rows[c], attn_grad[...], ((0,), (0,))).astype(BF16)
    proj_reduce.swap()
    for q in range(4):
        at = slice(q * 256, (q + 1) * 256)
        small[0:32, at] = split_dot(logit_grad, moe[q], ((1,), (0,)))
    small[32:40] = jnp.broadcast_to(jnp.sum(moe_in_grad * n, axis=0, keepdims=True), (8, 1024))
    o_steps[1]()
    proj_reduce.far()
    term_reduce.sides()
    proj_reduce.sides()
    o_steps[2]()
    for copy in mg_copies:
        copy.wait_recv()

    @pl.loop(0, 8)
    def _(i):
        g = mg_land[i].astype(F32)
        out_s[i] = one_below(g).astype(BF16)
        g = side_by_side(g.T)
        out_t[i] = g.astype(BF16)
        delta[i] = jnp.sum(g * exact[i], axis=0, keepdims=True)
        dq[i] = jnp.zeros_like(dq[i])

    key_row = lax.broadcasted_iota(jnp.int32, (ROWS, 2 * ROWS), 0)
    query_row = lax.rem(lax.broadcasted_iota(jnp.int32, (ROWS, 2 * ROWS), 1), ROWS)
    seen = key_row <= query_row

    def key_block(j):
        key, key_t, value = k_s[j], k_t[j], v_s[j]

        def add_block(i, carry, diagonal):
            dk, dv = carry
            probs = jnp.exp(dot(key, q_t[i]) - lse[i])
            if diagonal:
                probs = jnp.where(seen, probs, 0.0)
            grad = probs * (dot(value, out_t[i]) - delta[i])
            grad = grad.astype(BF16)
            dv = dv + dot(probs.astype(BF16), out_s[i])
            dk = dk + dot(grad, q_s[i])
            dq[i] += dot(key_t, grad)
            return dk, dv

        zero = jnp.zeros((ROWS, 64), F32)
        carry = add_block(j, (zero, zero), True)
        dk, dv = lax.fori_loop(j + 1, 8, lambda i, c: add_block(i, c, False), carry)
        g = dq[j] * 0.125
        g = jnp.concatenate([g[:, :ROWS], g[:, ROWS:]], axis=0).T
        d[j] = jnp.concatenate([g, dk, dv], axis=1).astype(BF16)

    def d_copy(j):
        return pltpu.make_async_remote_copy(
            src_ref=d.at[j],
            dst_ref=d_land.at[me],
            send_sem=d_send.at[j],
            recv_sem=d_recv.at[me],
            device_id={"ctx": jnp.int32(j)},
            device_id_type=MESH,
        )

    def d_begin(j):
        @pl.when(me != j)
        def _():
            d_copy(j).start()

        @pl.when(me == j)
        def _():
            d_land[j] = d[j]

    def head_term(j):
        rows_load(j).wait()
        if j < 7:
            rows_load(j + 1).start()
        value = dot(attn_rows[j % 2], d[j], ((0,), (0,)))
        value = value.reshape(8, 16, 8, 256)
        head_acc[...] = value if j == 0 else head_acc[...] + value

    between = (
        (o_steps[3],),
        (term_reduce.pass_on, o_steps[4]),
        (proj_reduce.pass_on, o_steps[5]),
        (o_steps[6],),
        (o_steps[7], o_steps[8]),
        (proj_reduce.finish,),
        (o_steps[9],),
        (),
    )
    for j in range(8):
        key_block(j)
        d_begin(j)
        if j < 7:
            head_term(j)
        for step in between[j]:
            step()
    head_term(7)
    wide = jnp.concatenate([small[...], jnp.zeros((88, 1024), F32)], axis=0)
    for c in range(8):
        wide_small[c] = wide[:, c * 128 : (c + 1) * 128].T
    mine = proj_reduce.mine[3]

    for x in range(16):
        head = head_acc[:, x].reshape(64, 256)
        rows = mine[pl.ds((x // 2) * 16, 16)].astype(F32)[(x % 2) * 8 : (x % 2) * 8 + 8]
        rows = jnp.concatenate([rows[:, q * 256 : (q + 1) * 256] for q in range(4)], axis=0)
        rest = wide_small[:, x * 8 : x * 8 + 8].reshape(64, 128)
        rest = jnp.concatenate([rest[:32], rest[32:]], axis=1)
        w_parts[4 * x] = head[:32].astype(BF16)
        w_parts[4 * x + 1] = head[32:].astype(BF16)
        w_parts[4 * x + 2] = rows.astype(BF16)
        w_parts[4 * x + 3] = rest.astype(BF16)
    w_reduce = LineReduce(w_parts, w_landed, w_send, w_recv)
    w_reduce.send(1)
    w_load.wait()
    w_reduce.take(1)
    w_reduce.send(2)
    for source in range(8):

        @pl.when(me != source)
        def _():
            pltpu.make_async_remote_copy(
                src_ref=d.at[source],
                dst_ref=d_land.at[source],
                send_sem=d_send.at[source],
                recv_sem=d_recv.at[source],
                device_id={"ctx": jnp.int32(source)},
                device_id_type=MESH,
            ).wait_recv()

    attn_in_grad = jnp.zeros((ROWS, 1024), F32)
    for c in range(8):
        attn_in_grad = attn_in_grad + dot(d_land[c], w_full[c], ((1,), (1,)))
    back, _ = norm_back(tokens[...].astype(F32), attn_in_grad, misc[33:34])
    token_grad[...] = (back + resid_grad[...]).astype(BF16)
    w_reduce.take(2)
    done = [w_parts[4 * own + q].astype(F32) for q in range(4)]
    for q in range(4):
        out_sum[:, q * 256 : (q + 1) * 256] = done[2][q * 8 : (q + 1) * 8]
    for c in range(8):
        source = done[c // 4][(c % 4) * 8 : (c % 4) * 8 + 8]
        f_send = jnp.concatenate(
            [
                source,
                done[3][(c % 4) * 8 : (c % 4) * 8 + 8, (c // 4) * 128 : (c // 4) * 128 + 128],
            ],
            axis=1,
        )
        f_given[c] = f_send
    f_copies = [
        to_ctx(
            f_given.at[ctx_block(*peer)], f_land.at[me],
            direct_send.at[1, at], direct_recv.at[1, at], peer,
        )
        for at, peer in enumerate(PEERS)
    ]
    for copy in f_copies:
        copy.start()
    f_land[me] = f_given[me]
    term_reduce.finish()
    term_sum[...] = t_mine[3]
    o_steps[10]()
    expert_out = jnp.concatenate([o_parts[4 * own + q].astype(F32) for q in range(4)], axis=1)
    output[...] = (resid[...] + expert_out).astype(BF16)
    for copy in f_copies:
        copy.wait_recv()
    for c in range(8):
        head_sum[c] = f_land[c]
    out_reduce.sent()
    w_reduce.sent()
    for reduce in (term_reduce, proj_reduce):
        reduce.sent()
    for copy in (*mg_copies, *f_copies):
        copy.wait_send()
    for j in range(8):

        @pl.when(me != j)
        def _():
            d_copy(j).wait_send()


def finish(args, collective_id):
    anywhere = pl.BlockSpec(memory_space=pl.ANY)
    dma = pltpu.SemaphoreType.DMA
    outs = [
        ((256, 1024), BF16),
        ((256, 1024), BF16),
        ((8, 8, 384), F32),
        ((8, 1024), F32),
        ((6, 128, 512), BF16),
    ]
    return pl.pallas_call(
        finish_kernel,
        out_shape=[jax.ShapeDtypeStruct(s, t) for s, t in outs],
        in_specs=[vmem()] * 16 + [anywhere] * 4,
        out_specs=[vmem()] * len(outs),
        scratch_shapes=[
            VMEM((64, 256, 256), BF16),
            VMEM((60, 256, 256), BF16),
            VMEM((4, 6, 128, 512), BF16),
            VMEM((4, 6, 128, 512), BF16),
            VMEM((3, 6, 128, 512), BF16),
            VMEM((256, 1024), BF16),
            VMEM((256, 1024), F32),
            VMEM((8, 256, 128), BF16),
            VMEM((8, 256, 128), BF16),
            VMEM((8, 128, 1024), BF16),
            VMEM((4, 128, 1024), BF16),
            VMEM((3, 128, 1024), BF16),
            VMEM((8, 512, 64), BF16),
            VMEM((8, 64, 512), BF16),
            VMEM((8, 1, 512), F32),
            VMEM((8, 64, 512), F32),
            VMEM((8, 256, 256), BF16),
            VMEM((8, 256, 256), BF16),
            VMEM((8, 1024, 256), BF16),
            VMEM((8, 16, 8, 256), F32),
            VMEM((40, 1024), F32),
            VMEM((64, 32, 256), BF16),
            VMEM((60, 32, 256), BF16),
            VMEM((8, 128, 128), F32),
            VMEM((8, 8, 384), F32),
            VMEM((8, 8, 384), F32),
            VMEM((2, 256, 1024), BF16),
            dma((40,)),
            dma((40,)),
            dma((40,)),
            dma((40,)),
            dma((2, 8)),
            dma((2, 8)),
            dma((2, 7)),
            dma((2, 7)),
            dma((6,)),
            dma((2,)),
            dma((8,)),
            dma((8,)),
        ],
        compiler_params=pltpu.CompilerParams(
            collective_id=collective_id, has_side_effects=True, vmem_limit_bytes=62 << 20
        ),
    )(*args)


def last_kernel(
    output, token_grad, head_in, out_in, term_in, query_in, key_in, value_in, narrow_in,
    output_end, token_grad_end, norms, query_sum, key_sum, value_sum, out_end, router_sum,
    gate_sum, up_sum, down_sum,
    head_sum, term_sum, w_query, w_key, w_value, norm_attn, sems,
):
    copies = [
        pltpu.make_async_copy(source, target, sems.at[at])
        for at, (source, target) in enumerate(
            (
                (head_in, head_sum), (query_in, w_query), (key_in, w_key), (value_in, w_value),
                (narrow_in, norm_attn), (term_in, term_sum), (output, output_end),
                (token_grad, token_grad_end), (out_in, out_end),
            )
        )
    ]
    for copy in copies:
        copy.start()
    for copy in copies[:5]:
        copy.wait()
    query = jnp.concatenate([head_sum[c, :, 0:128] for c in range(8)], axis=1)
    key = jnp.concatenate([head_sum[c, :, 128:192] for c in range(8)], axis=1)
    value = jnp.concatenate([head_sum[c, :, 192:256] for c in range(8)], axis=1)
    query_sum[...] = query
    key_sum[...] = key
    value_sum[...] = value
    small = head_sum[0, :, 256:384]
    for c in range(1, 8):
        small = small + head_sum[c, :, 256:384]
    router_sum[...] = small
    total = jnp.sum(query * w_query[...].astype(F32), axis=1, keepdims=True)
    total = total + jnp.sum(key * w_key[...].astype(F32), axis=1, keepdims=True)
    total = total + jnp.sum(value * w_value[...].astype(F32), axis=1, keepdims=True)
    total = total / norm_attn[:, 33:34]
    lane = lax.broadcasted_iota(jnp.int32, (8, 128), 1)
    both = jnp.where(lane == 0, total, small[:, 32:33])
    norms[...] = both.T[0:8, :]
    for copy in copies[5:]:
        copy.wait()
    for k in range(2):
        gate_sum[k] = term_sum[k].astype(F32)
        up_sum[k] = term_sum[2 + k].astype(F32)
        down_sum[k] = term_sum[4 + k].astype(F32).T


def last(*args):
    anywhere = pl.BlockSpec(memory_space=pl.ANY)
    outs = [
        ((256, 1024), BF16),
        ((256, 1024), BF16),
        ((8, 8), F32),
        ((8, 1024), F32),
        ((8, 512), F32),
        ((8, 512), F32),
        ((8, 1024), F32),
        ((8, 128), F32),
        ((2, 128, 512), F32),
        ((2, 128, 512), F32),
        ((2, 512, 128), F32),
    ]
    return pl.pallas_call(
        last_kernel,
        out_shape=[jax.ShapeDtypeStruct(s, t) for s, t in outs],
        in_specs=[anywhere] * len(args),
        out_specs=[anywhere if at in (0, 1, 6) else vmem() for at in range(len(outs))],
        scratch_shapes=[
            VMEM((8, 8, 384), F32),
            VMEM((6, 128, 512), BF16),
            VMEM((8, 1024), BF16),
            VMEM((8, 512), BF16),
            VMEM((8, 512), BF16),
            VMEM((8, 128), F32),
            pltpu.SemaphoreType.DMA((9,)),
        ],
        compiler_params=pltpu.CompilerParams(vmem_limit_bytes=62 << 20),
    )(*args)


def per_device(
    tokens,
    norm_attn,
    w_query,
    w_key,
    w_value,
    w_out,
    norm_moe,
    w_router,
    w_gate,
    w_up,
    w_down,
    routes,
    cotangent,
):
    narrow = jnp.concatenate([w_router, norm_moe[:, None], norm_attn[:, None]], axis=1)
    narrow = jnp.pad(narrow.astype(F32), ((0, 0), (0, 94)))
    (
        attn_in, q_t, q_s, k_s, k_t, v_s, lse, exact, mixed_rows,
        head_weights, misc_t, full_out, resid, moe_in, all_cot, all_routes, all_experts,
    ) = start(
        (
            tokens[0], cotangent[0], w_gate, w_up, w_down,
            w_query, w_key, w_value, w_out, narrow, routes[0],
        ),
        1,
    )
    grad_total, out_parts, expert_terms, all_weights = moe_block(
        moe_in, misc_t, all_routes, all_cot, all_experts, head_weights, 2
    )
    parts = finish(
        (
            grad_total, resid, misc_t, all_routes, moe_in, cotangent[0], tokens[0],
            full_out, mixed_rows, q_t, q_s, k_s, k_t, v_s, lse, exact, attn_in,
            out_parts.reshape(64, 256, 256), expert_terms, all_weights,
        ),
        3,
    )
    (
        output, token_grad, norms, query_sum, key_sum, value_sum, out_sum, router_sum,
        gate_sum, up_sum, down_sum,
    ) = last(*parts, w_query, w_key, w_value, narrow)
    router_sum = router_sum[:, :32].reshape(8, 2, 16).transpose(0, 2, 1).reshape(8, 32)
    return (
        output[None],
        token_grad[None],
        norms[0],
        query_sum,
        key_sum,
        value_sum,
        out_sum,
        norms[1],
        router_sum,
        gate_sum,
        up_sum,
        down_sum,
    )


def solution(mesh):
    in_specs = (
        P("exp", "ctx", None),
        P(("ctx", "exp")),
        P(("ctx", "exp"), None),
        P(("ctx", "exp"), None),
        P(("ctx", "exp"), None),
        P(("ctx", "exp"), None),
        P(("ctx", "exp")),
        P(("ctx", "exp"), None),
        P("exp", "ctx", None),
        P("exp", "ctx", None),
        P("exp", None, "ctx"),
        P("exp", "ctx", None),
        P("exp", "ctx", None),
    )
    out_specs = (
        P("exp", "ctx", None),
        P("exp", "ctx", None),
        P(("ctx", "exp")),
        P(("ctx", "exp"), None),
        P(("ctx", "exp"), None),
        P(("ctx", "exp"), None),
        P(("ctx", "exp"), None),
        P(("ctx", "exp")),
        P(("ctx", "exp"), None),
        P("exp", "ctx", None),
        P("exp", "ctx", None),
        P("exp", None, "ctx"),
    )
    return jax.shard_map(
        per_device, mesh=mesh, in_specs=in_specs, out_specs=out_specs, check_vma=False
    )
```
